32 devices in a mesh: rows: 4 (over x, core), tract: 8 (over z, y).
Axes of the slice: x: 2, y: 2, z: 4, core: 2. Of those that a mesh axis runs over, the one named last changes fastest.
Arguments:
- byte_values: int32 [64, 2048], P('rows', 'tract'), may hold values from 0 to 255
- segment_ids: int32 [64, 2048], P('rows', 'tract'), may hold values from 0 to 15, as said below
- valid: int32 [64, 2048], P('rows', 'tract'), may hold values from 0 to 1, as said below
- table: float32 [256, 768], P('rows'), may hold values from -6 to 6
- conv_weight: float32 [3072, 768], P('rows'), may hold values from -0.109375 to 0.109375
- conv_bias: float32 [768], P('rows'), may hold values from -3 to 3
- score_weight: float32 [768], P('rows'), may hold values from -0.4375 to 0.4375
- cotangent: bfloat16 [64, 1024, 768], P('rows', 'tract'), may hold values from -6 to 6
Outputs:
- output: bfloat16 [64, 1024, 768], P('rows', 'tract')
- table_grad: float32 [256, 768], P('rows')
- conv_weight_grad: float32 [3072, 768], P('rows')
- conv_bias_grad: float32 [768], P('rows')
- score_weight_grad: float32 [768], P('rows')
The draws below stay inside these ranges and needn't reach their ends.
Inputs may be any that keep to these rules, and one draw needn't show every extreme that they name: `segment_ids`: segment numbers start at 0 in each row and never fall along it; in each group of 16 consecutive rows one row is a single segment. `valid`: in each row the ones come first and cover at least half of it; in each group of 16 consecutive rows the row that is a single segment is all ones.
All inputs are finite; a program needn't handle non-finite values.
Results may differ from the reference program's by a relative error of at most 0.008.
Values may be sent and summed in bfloat16 or wider, within the bound.
No kernel may reach another device: no remote copies, remote signals or barrier semaphores. Data moves between devices by JAX's collectives and lax.ppermute only.
A program may use at most 384 MiB of HBM per device.

```python
import math
import jax
import jax.numpy as jnp
import numpy as np
from jax import lax

D = 768
BYTE_VALUES = 256
R_DEV = 16
STRETCH_LEN = 256
ROWS = 64
LENGTH = 2048


def chosen_rows(key):
    chosen = jax.random.randint(jax.random.fold_in(key, 101), (ROWS // R_DEV,), 0, R_DEV)
    return jnp.repeat(chosen, R_DEV, total_repeat_length=ROWS)


def whole_rows(key):
    return jnp.arange(ROWS) % R_DEV == chosen_rows(key)


def draw_segment_ids(key, part):
    chosen_all = chosen_rows(key)
    whole_row = whole_rows(key)
    forced_row = (jnp.arange(ROWS) % R_DEV == (chosen_all + 1) % R_DEV) & jnp.logical_not(whole_row)
    key = jax.random.fold_in(key, 3)
    positions = jnp.arange(LENGTH)[None, :]
    starts = jax.random.randint(key, (ROWS, LENGTH), 0, STRETCH_LEN) == 0
    half_span = STRETCH_LEN // 2
    forced = forced_row[:, None] & (positions % half_span == 0)
    boundary = (starts | forced) & jnp.logical_not(whole_row)[:, None] & (positions > 0)
    top_id = 2 * (LENGTH // STRETCH_LEN) - 1
    return jnp.minimum(jnp.cumsum(boundary.astype(jnp.int32), axis=1), top_id).astype(jnp.int32)


def draw_valid(key, part):
    whole_row = whole_rows(key)
    key = jax.random.fold_in(key, 5)
    row_lengths = jax.random.randint(key, (ROWS,), LENGTH // 2, LENGTH + 1)
    row_lengths = jnp.where(whole_row, LENGTH, row_lengths)
    return (jnp.arange(LENGTH)[None, :] < row_lengths[:, None]).astype(jnp.int32)


def plant(values, stream_key, smallest, top_value):
    shape = values.shape
    spot = [jax.random.randint(jax.random.fold_in(stream_key, axis), (), 0, shape[axis]) for axis in range(len(shape))]
    values = values.at[tuple(spot)].set(smallest)
    longest = shape.index(max(shape))
    spot[longest] = (spot[longest] + 1) % shape[longest]
    return values.at[tuple(spot)].set(top_value)


def block_scale(key, dims, pieces, least, largest):
    def one(axis_at, blocks):
        draws = jax.random.uniform(jax.random.fold_in(jax.random.fold_in(key, 6), axis_at), (blocks,), jnp.float32, least / len(pieces), largest / len(pieces))
        return jnp.repeat(jnp.exp(draws), dims[axis_at] // blocks).reshape((-1,) + (1,) * (len(dims) - axis_at - 1))

    level = one(*pieces[0])
    for cut in pieces[1:]:
        level = level * one(*cut)
    return level


def cumulative_ranks(count, lean):
    portions = [(1 << 20) // math.isqrt(grade ** lean) + 1 for grade in range(1, count + 1)]
    spread = 1 + sum(portions) // (1 << 30)
    return np.cumsum(np.array([max(1, weight // spread) for weight in portions]))


def ranked_ids(key, dims, number_of, lean):
    grid = cumulative_ranks(number_of, lean)
    pick = jax.random.randint(jax.random.fold_in(key, 1), dims, 0, int(grid[number_of - 1]))
    rank = jnp.searchsorted(jnp.asarray(grid, jnp.int32), pick, side="right")
    return jax.random.permutation(jax.random.fold_in(key, 2), number_of)[rank].astype(jnp.int32)


def centred(rng, dims, spread, most, split=(), kind=jnp.bfloat16):
    drawn = jax.random.normal(rng, dims, jnp.float32) * spread
    if len(split) > 0:
        drawn = block_scale(rng, dims, split, -0.22, 0.18) * drawn
    return jnp.clip(drawn, min=-most, max=most).astype(kind)


def setup_inputs(seed: int = 0) -> dict:
    key_of = jax.random.split(jax.random.key(seed), 9)
    byte_values = plant(ranked_ids(key_of[0], (ROWS, LENGTH), BYTE_VALUES, 2), jax.random.fold_in(key_of[0], 3), 0, BYTE_VALUES - 1).astype(jnp.int32)
    segment_ids = draw_segment_ids(jax.random.fold_in(key_of[8], 71), 0)
    valid = draw_valid(jax.random.fold_in(key_of[8], 71), 0)
    table = centred(key_of[3], (BYTE_VALUES, D), 1.0, 6.0, ((0, 4),), jnp.float32)
    conv_weight = centred(key_of[4], (4 * D, D), (4 * D) ** -0.5, 0.109375, ((0, 4),), jnp.float32)
    conv_bias = centred(key_of[5], (D,), 0.5, 3.0, ((0, 4),), jnp.float32)
    score_weight = centred(key_of[6], (D,), (D // 4) ** -0.5, 0.4375, ((0, 4),), jnp.float32)
    cotangent = centred(key_of[7], (ROWS, LENGTH // 2, D), 1.0, 6.0, ((0, 4), (1, 8)))
    return {"byte_values": byte_values, "segment_ids": segment_ids, "valid": valid, "table": table, "conv_weight": conv_weight, "conv_bias": conv_bias, "score_weight": score_weight, "cotangent": cotangent}


PRECISE = lax.Precision.HIGHEST

@jax.custom_vjp
def low(v):
    return lax.optimization_barrier(v.astype(jnp.bfloat16)).astype(jnp.float32)

@jax.custom_vjp
def low_back(v):
    return v

def low_keep(v):
    return (low(v), None)

def low_pass(kept, grad):
    return (grad,)

def back_keep(v):
    return (v, None)

def back_low(kept, grad):
    return (low(grad),)
low.defvjp(low_keep, low_pass)
low_back.defvjp(back_keep, back_low)

def row_forward(table, conv_weight, conv_bias, score_weight, row_bytes, row_segments, row_valid):
    length = row_bytes.shape[0]
    model_width = table.shape[1]
    valid_float = row_valid.astype(jnp.float32)
    one_hot = (row_bytes[:, None] == jnp.arange(table.shape[0], dtype=jnp.int32)[None, :]).astype(jnp.float32)
    one_hot = one_hot * valid_float[:, None]
    embedded = jnp.dot(one_hot, table, precision=PRECISE)
    embed_pad = jnp.concatenate([jnp.zeros((3, model_width), jnp.float32), embedded], 0)
    seg_pad = jnp.concatenate([jnp.full((3,), -1, jnp.int32), row_segments.astype(jnp.int32)], 0)
    valid_pad = jnp.concatenate([jnp.zeros((3,), jnp.float32), valid_float], 0)
    same_list = [(seg_pad[3 - offset:3 - offset + length] == row_segments).astype(jnp.float32) for offset in range(4)]
    windows = jnp.concatenate([embed_pad[3 - offset:3 - offset + length] * same_list[offset][:, None] for offset in range(4)], 1)
    conv_out = low_back(conv_bias + jnp.dot(windows, conv_weight, precision=PRECISE))
    conv_pad = jnp.concatenate([jnp.zeros((3, model_width), jnp.float32), conv_out], 0)
    running = jnp.zeros((length, model_width), jnp.float32)
    counts = jnp.zeros((length,), jnp.float32)
    pooled = []
    for offset in range(4):
        keep_now = same_list[offset] * valid_pad[3 - offset:3 - offset + length]
        running = running + keep_now[:, None] * conv_pad[3 - offset:3 - offset + length]
        counts = counts + keep_now
        pooled.append(running / jnp.maximum(counts, 1.0)[:, None])
    stacked = jnp.stack(pooled, 0)
    scores = jnp.einsum('bld,d->bl', stacked, score_weight, precision=PRECISE)
    block_probs = jax.nn.softmax(scores, axis=0)
    mixed_rows = lax.optimization_barrier(jnp.sum(block_probs[:, :, None] * stacked, 0))
    return lax.optimization_barrier(jnp.mean(mixed_rows.reshape(length // 2, 2, model_width), 1))

def reference(byte_values, segment_ids, valid, table, conv_weight, conv_bias, score_weight, cotangent):

    def forward(table_f, weight_f, bias_f, score_f):
        table_low, weight_low, bias_low, score_low = (low(table_f), low(weight_f), low(bias_f), low(score_f))

        def row_step(row_args):
            return row_forward(table_low, weight_low, bias_low, score_low, row_args[0], row_args[1], row_args[2])
        return lax.map(jax.checkpoint(row_step), (byte_values, segment_ids, valid))
    mixed_all, pullback = jax.vjp(forward, table.astype(jnp.float32), conv_weight.astype(jnp.float32), conv_bias.astype(jnp.float32), score_weight.astype(jnp.float32))
    gradients = pullback(cotangent.astype(jnp.float32))
    return (mixed_all.astype(jnp.bfloat16), gradients[0], gradients[1], gradients[2], gradients[3])
```

```python
import functools

import jax
import jax.numpy as jnp
from jax import lax
from jax.experimental import pallas as pl
from jax.experimental.pallas import tpu as pltpu
from jax.sharding import PartitionSpec as P

F32 = jnp.float32
BF16 = jnp.bfloat16
OFFSETS = 4
REACH = 5
SPAN = 8
EXTRA = 16
VMEM_LIMIT = 56 * 1024 * 1024
NT = (((1,), (1,)), ((), ()))
TN = (((0,), (0,)), ((), ()))
NN = (((1,), (0,)), ((), ()))


def dot(a, b, dims=NN, precision=None):
    return lax.dot_general(a, b, dims, precision=precision, preferred_element_type=F32)


def exact(a, b, dims=NN):
    return dot(a, b, dims, lax.Precision.HIGHEST)


def call(kernel, outs, *operands, scratch=(), scalars=1, flops=0, name=None):
    smem = pl.BlockSpec(memory_space=pltpu.SMEM)
    vmem = pl.BlockSpec(memory_space=pltpu.VMEM)
    moved = sum(a.size * a.dtype.itemsize for a in operands)
    result = pl.pallas_call(
        kernel,
        out_shape=[jax.ShapeDtypeStruct(s, t) for s, t in outs],
        in_specs=[smem] * scalars + [vmem] * (len(operands) - scalars),
        out_specs=[vmem] * len(outs),
        scratch_shapes=list(scratch),
        compiler_params=pltpu.CompilerParams(vmem_limit_bytes=VMEM_LIMIT),
        cost_estimate=pl.CostEstimate(flops=flops, bytes_accessed=moved, transcendentals=0),
        name=name,
    )(*operands)
    return result


def swap(value, axis, bit):
    count = lax.axis_size(axis)
    return lax.ppermute(value, axis, [(i, i ^ bit) for i in range(count)])


def gather_slots(value, axis, bits):
    slots = {0: value}
    for bit in bits:
        for m in list(slots):
            slots[m | bit] = swap(slots[m], axis, bit)
    return slots


def payload_kernel(where, table, score, bias, out):
    rows, width = table.shape
    shard = score.shape[1]
    out[:rows] = table[...].astype(BF16)
    source = lax.broadcasted_iota(jnp.int32, (shard, width), 0) + where[0] * shard
    column = lax.broadcasted_iota(jnp.int32, (shard, width), 1)
    place = (source == column).astype(BF16)
    both = jnp.concatenate(
        [jnp.broadcast_to(score[...], (8, shard)), jnp.broadcast_to(bias[...], (8, shard))], 0
    ).astype(BF16)
    out[rows:] = dot(both, place).astype(BF16)


def table_kernel(order, where, *refs):
    count = len(order)
    slots, (weight,) = refs[:count], refs[count : count + 1]
    product, scores, weight_low, table_low, vectors = refs[count + 1 :]
    rows = slots[0].shape[0] - EXTRA
    total = jnp.zeros((EXTRA, slots[0].shape[1]), F32)
    for slot, m in zip(slots, order):
        at = pl.multiple_of((where[0] ^ m) * rows, rows)
        table_low[pl.ds(at, rows), :] = slot[:rows]
        total = total + slot[rows:].astype(F32)
    vectors[...] = total.astype(BF16)
    weight_low[...] = weight[...].astype(BF16)
    full = dot(table_low[...], weight_low[...])
    product[...] = full.astype(BF16)
    scores[...] = exact(total[:8], full, NT)


def planes_kernel(where, ids, before, out):
    length = ids.shape[1]
    half = length // 2
    for m in range(SPAN):
        target = 2 * lax.broadcasted_iota(jnp.int32, (length, half), 1) + 1 - m
        source = lax.broadcasted_iota(jnp.int32, (length, half), 0)
        got = dot(ids[...], (source == target).astype(BF16))
        if m > 1:
            tail = before.shape[1]
            target = 2 * lax.broadcasted_iota(jnp.int32, (tail, half), 1) + 1 - m + tail
            source = lax.broadcasted_iota(jnp.int32, (tail, half), 0)
            got = got + dot(before[...], (source == target).astype(BF16))
        out[:, m * half : (m + 1) * half] = got


class Window:
    def __init__(self, planes, rows):
        half = planes.shape[1] // SPAN

        def part(which, m):
            return planes[which * rows : (which + 1) * rows, m * half : (m + 1) * half]

        self.bytes = [part(0, m) for m in range(SPAN)]
        self.segments = [part(1, m) for m in range(SPAN)]
        self.valid = [part(2, m) for m in range(SPAN)]
        self.mask = {
            (k, j): (self.segments[j + k] == self.segments[j]).astype(F32) * self.valid[j + k]
            for k in range(OFFSETS)
            for j in range(REACH)
        }
        self.keep, self.divide = [], []
        for side in range(2):
            keep = [self.mask[k, side] for k in range(OFFSETS)]
            counts, total = [], 0.0
            for k in range(OFFSETS):
                total = total + keep[k]
                counts.append(1.0 / jnp.maximum(total, 1.0))
            self.keep.append(keep)
            self.divide.append(counts)

    def pooled(self, side, values):
        means, total = [], 0.0
        for k in range(OFFSETS):
            total = total + self.keep[side][k] * values[side + k]
            means.append(total * self.divide[side][k])
        return means

    def spread(self, sides):
        result = [0.0] * REACH
        for side in range(2):
            carried = 0.0
            for k in reversed(range(OFFSETS)):
                carried = carried + sides[side][k] * self.divide[side][k]
                result[side + k] = result[side + k] + self.keep[side][k] * carried
        return result


def lookup(row, codes):
    index = codes.astype(jnp.int32)
    lanes = 128
    low = jnp.bitwise_and(index, lanes - 1)
    parts = [
        jnp.take_along_axis(
            jnp.broadcast_to(row[:, at : at + lanes], codes.shape), low, axis=1
        )
        for at in range(0, row.shape[1], lanes)
    ]
    return jnp.where(index >= lanes, parts[1], parts[0])


def packed_row(ref, plane, row):
    return jnp.broadcast_to(ref[plane, pl.ds(row, 1), :], (16, ref.shape[2])).astype(BF16)


def spread_rows(codes_ref, weights_ref, k, row, values):
    lanes = codes_ref.shape[2]
    blocks = values // 16
    name = (
        lax.broadcasted_iota(jnp.int32, (blocks, 16, lanes), 0) * 16
        + lax.broadcasted_iota(jnp.int32, (blocks, 16, lanes), 1)
    ).astype(F32).astype(BF16)
    total = jnp.zeros((blocks, 16, lanes), BF16)
    for j in range(REACH):
        code = packed_row(codes_ref, k + j, row)
        weight = packed_row(weights_ref, k * REACH + j, row)
        total = jnp.where(name == code[None], total + weight[None], total)
    return total.reshape(values, lanes)


def accumulate(codes_ref, weights_ref, total_ref, ks, cot, values, extra=None):
    rows, half = codes_ref.shape[1:]
    for chunk in range(rows // 2):
        pieces = [
            jnp.concatenate(
                [
                    spread_rows(codes_ref, weights_ref, k, 2 * chunk, values),
                    spread_rows(codes_ref, weights_ref, k, 2 * chunk + 1, values),
                ],
                1,
            )
            for k in ks
        ]
        if extra is not None:
            pieces.append(extra(chunk))
        left = jnp.concatenate(pieces, 0)
        part = dot(left, cot[2 * chunk * half : 2 * (chunk + 1) * half, :])
        if chunk == 0:
            total_ref[...] = part
        else:
            total_ref[...] += part


def split(value):
    high = value.astype(BF16)
    return high, (value - high.astype(F32)).astype(BF16)


def far_kernel(order, slots, values, group, *refs):
    scores = refs[: len(order)]
    planes, vectors, cot = refs[len(order) : len(order) + 3]
    out, codes, weights, probs, masks, averages = refs[len(order) + 3 : len(order) + 9]
    table, total = refs[len(order) + 9 :]
    rows = codes.shape[1]
    for score, m in zip(scores, order):
        table[group[0] ^ m] = score[...]
    window = Window(planes[...], rows)
    shared = jnp.sum(vectors[:8].astype(F32) * vectors[8:].astype(F32), 1, keepdims=True)[:1]
    conv_scores = [shared] * REACH
    for k in range(OFFSETS):
        row = table[k, :1, :]
        for m in range(k, k + REACH):
            found = lookup(row, window.bytes[m])
            conv_scores[m - k] = conv_scores[m - k] + window.mask[k, m - k] * found
    for m in range(SPAN):
        codes[m] = window.bytes[m]
    shares = []
    for side in range(2):
        block = window.pooled(side, conv_scores)
        top = functools.reduce(jnp.maximum, block)
        exps = [jnp.exp(b - top) for b in block]
        inverse = 1.0 / functools.reduce(jnp.add, exps)
        shares.append([e * inverse for e in exps])
        for k in range(OFFSETS):
            probs[side * OFFSETS + k] = shares[side][k]
    mixing = [0.5 * e for e in window.spread(shares)]
    averages[...] = functools.reduce(jnp.add, mixing)
    for k in range(OFFSETS):
        for j in range(REACH):
            masks[k * REACH + j] = window.mask[k, j]
            weights[k * REACH + j] = window.mask[k, j] * mixing[j]
    accumulate(codes, weights, total, [group[0] ^ m for m in slots], cot, values)
    for at in range(len(slots)):
        out[at] = total[at * values : (at + 1) * values].astype(BF16)


def near_kernel(slots, values, group, codes, weights, averages, cot, out, bias_out, total):
    half = codes.shape[2]

    def extra(chunk):
        line = jnp.concatenate(
            [averages[2 * chunk : 2 * chunk + 1, :], averages[2 * chunk + 1 : 2 * chunk + 2, :]], 1
        )
        line = jnp.broadcast_to(line, (EXTRA, 2 * half))
        high, low = split(line)
        at = lax.broadcasted_iota(jnp.int32, line.shape, 0)
        return jnp.where(at == 0, high.astype(F32), jnp.where(at == 1, low.astype(F32), 0.0)).astype(BF16)

    accumulate(codes, weights, total, [group[0] ^ m for m in slots], cot, values, extra)
    for at in range(len(slots)):
        out[at] = total[at * values : (at + 1) * values].astype(BF16)
    end = total[len(slots) * values :]
    bias_out[...] = jnp.broadcast_to(end[:1] + end[1:2], (8, end.shape[1]))


def score_kernel(order, values, group, *refs):
    products = refs[: len(order)]
    planes, vectors, probs, masks, codes, bias_part, cot = refs[len(order) : len(order) + 7]
    out, inner_ref, grads_ref, rows_ref = refs[len(order) + 7 :]
    rows, half = codes.shape[1:]
    biases = vectors[8:]
    blocks = values // 8
    name = (
        lax.broadcasted_iota(jnp.int32, (blocks, 8, half), 0) * 8
        + lax.broadcasted_iota(jnp.int32, (blocks, 8, half), 1)
    ).astype(F32)
    for chunk in range(rows // 2):
        here = cot[2 * chunk * half : 2 * (chunk + 1) * half, :]
        base = dot(biases, here, NT)
        found = {}
        for slot, m in zip(products, order):
            k = group[0] ^ m
            each = dot(slot[...], here, NT)
            for side in range(2):
                row = 2 * chunk + side
                mine = each[:, side * half : (side + 1) * half].reshape(blocks, 8, half)
                for j in range(REACH):
                    code = jnp.broadcast_to(codes[k + j, row : row + 1, :], (8, half))
                    picked = jnp.sum(jnp.where(name == code[None], mine, 0.0), 0)
                    mask = masks[k * REACH + j, row : row + 1, :]
                    found[j, side] = found.get((j, side), 0.0) + picked * mask
        for side in range(2):
            row = 2 * chunk + side
            for j in range(REACH):
                inner_ref[j, row : row + 1, :] = (
                    jnp.sum(found[j, side], 0, keepdims=True)
                    + base[:1, side * half : (side + 1) * half]
                )
    window = Window(planes[...], rows)
    inner_rows = [0.5 * inner_ref[j] for j in range(REACH)]
    sides = []
    for side in range(2):
        inner = window.pooled(side, inner_rows)
        share = [probs[side * OFFSETS + k] for k in range(OFFSETS)]
        mean = functools.reduce(jnp.add, [s * i for s, i in zip(share, inner)])
        sides.append([s * (i - mean) for s, i in zip(share, inner)])
    grads = window.spread(sides)
    overall = jnp.sum(jnp.sum(functools.reduce(jnp.add, grads), 1, keepdims=True), 0, keepdims=True)
    for k in range(OFFSETS):
        for j in range(REACH):
            grads_ref[k * REACH + j] = grads[j] * window.mask[k, j]
    ones = jnp.ones((8, half), F32)
    out[...] = jnp.zeros(out.shape, F32)
    for k in range(OFFSETS):
        total = jnp.zeros((blocks, 8, half), F32)
        for row in range(rows):
            for j in range(REACH):
                code = jnp.broadcast_to(codes[k + j, row : row + 1, :], (8, half))
                grad = jnp.broadcast_to(grads_ref[k * REACH + j, row : row + 1, :], (8, half))
                total = jnp.where(name == code[None], total + grad[None], total)
        line = exact(ones, total.reshape(values, half), NT)
        rows_ref[k] = line
        out[k : k + 1, :values] = line[:1]
    at = lax.broadcasted_iota(jnp.int32, (EXTRA, values), 0)
    score_grad = jnp.zeros((1, biases.shape[1]), F32)
    for slot, m in zip(products, order):
        line = jnp.broadcast_to(rows_ref[group[0] ^ m][:1], (EXTRA, values))
        high, low = split(line)
        both = jnp.where(at == 0, high.astype(F32), jnp.where(at == 1, low.astype(F32), 0.0))
        got = dot(both.astype(BF16), slot[...])
        score_grad = score_grad + got[:1] + got[1:2]
    score_grad = score_grad + overall * biases[:1].astype(F32)
    width = biases.shape[1]
    out[4:5, :width] = score_grad
    out[5:6, :width] = bias_part[:1] + overall * vectors[:1].astype(F32)


def output_kernel(order, values, group, *refs):
    products = refs[: len(order)]
    codes, weights, averages, vectors, out = refs[len(order) :]
    rows, half = codes.shape[1:]
    biases = vectors[8:].astype(F32)
    at = lax.broadcasted_iota(jnp.int32, (8, 2 * half), 0)
    first = lax.broadcasted_iota(jnp.int32, biases.shape, 0)
    biases = jnp.where(first < 2, biases, 0.0)
    for chunk in range(rows // 2):
        line = jnp.concatenate(
            [averages[2 * chunk : 2 * chunk + 1, :], averages[2 * chunk + 1 : 2 * chunk + 2, :]], 1
        )
        line = jnp.broadcast_to(line, (8, 2 * half))
        high, low = split(line)
        both = jnp.where(at == 0, high.astype(F32), jnp.where(at == 1, low.astype(F32), 0.0))
        total = dot(both, biases, TN)
        for slot, m in zip(products, order):
            k = group[0] ^ m
            left = jnp.concatenate(
                [
                    spread_rows(codes, weights, k, 2 * chunk, values),
                    spread_rows(codes, weights, k, 2 * chunk + 1, values),
                ],
                1,
            )
            total = total + dot(left, slot[...], TN)
        out[2 * chunk * half : 2 * (chunk + 1) * half, :] = total.astype(BF16)


def merge_kernel(bits, where, group, near, near_other, far_other, *refs):
    sums = refs[:-3]
    vectors, out, line = refs[-3:]
    values = near.shape[0]
    width = vectors.shape[1]
    line[...] = functools.reduce(jnp.add, [s[...] for s in sums])
    high, low = split(jnp.broadcast_to(line[pl.ds(group[0], 1), :values], (EXTRA, values)))
    at = lax.broadcasted_iota(jnp.int32, (EXTRA, values), 0)
    both = jnp.where(at == 0, high.astype(F32), jnp.where(at == 1, low.astype(F32), 0.0))
    scores = jnp.concatenate([vectors[:8], vectors[:8]], 0)
    total = dot(both.astype(BF16), scores, TN)
    total = total + near[...].astype(F32) + near_other[...].astype(F32) + far_other[...].astype(F32)
    total = total.astype(BF16)
    out[values:] = pack(jnp.concatenate([line[4:6, :width]] * 4, 0))
    size = values >> bits
    for actual in range(1 << bits):
        at = pl.multiple_of(reversed_bits(where[0] ^ actual, bits) * size, size)
        out[pl.ds(at, size), :] = total[actual * size : (actual + 1) * size]


def reversed_bits(number, bits):
    return sum((((number >> b) & 1) << (bits - 1 - b)) for b in range(bits))


def pack(rows):
    high, low = split(rows)
    return jnp.concatenate([high.astype(F32), low.astype(F32)], 0).astype(BF16)


def unpack(block):
    return block[:8].astype(F32) + block[8:].astype(F32)


def halve_kernel(where, mine, other, out):
    del where
    keep = out.shape[0] - EXTRA
    out[:keep] = (mine[:keep].astype(F32) + other[:keep].astype(F32)).astype(BF16)
    out[keep:] = pack(unpack(mine[mine.shape[0] - EXTRA :]) + unpack(other[keep:]))


def share_kernel(bits, where, group, block, weight_low, out, table_part):
    size = out.shape[0] >> bits
    for m in range(1 << bits):
        at = pl.multiple_of((where[0] ^ m) * size, size)
        place = reversed_bits(m, bits) * size
        out[pl.ds(at, size), :] = block[place : place + size]
    product = dot(out[...], weight_low[...], NT).astype(BF16)
    size = table_part.shape[0] // OFFSETS
    for actual in range(OFFSETS):
        at = pl.multiple_of((group[0] ^ actual) * size, size)
        table_part[pl.ds(at, size), :] = product[actual * size : (actual + 1) * size]


def weight_kernel(where, table_low, block, out):
    del where
    out[...] = dot(table_low[...], block[...], TN)


def bits_of(count):
    return [1 << at for at in reversed(range(count.bit_length() - 1))]


def body(byte_values, segment_ids, valid, table, conv_weight, conv_bias, score_weight, cotangent):
    rows_count, tract_count = lax.axis_size("rows"), lax.axis_size("tract")
    rows_at, tract_at = lax.axis_index("rows"), lax.axis_index("tract")
    values, width = table.shape[0] * rows_count, table.shape[1]
    rows, length = byte_values.shape
    half = length // 2
    copies = rows_count // OFFSETS
    me = rows_at[None].astype(jnp.int32)
    group = (rows_at // copies)[None].astype(jnp.int32)
    order = [0, 2, 1, 3]

    payload = call(
        payload_kernel, [((table.shape[0] + EXTRA, width), BF16)], me, table, score_weight[None], conv_bias[None],
        name="payload",
    )[0]
    slots = gather_slots(payload, "rows", bits_of(rows_count))
    ids = jnp.concatenate([byte_values, segment_ids, valid], 0)
    steps = [(i, i + 1) for i in range(tract_count - 1)]
    before = lax.ppermute(ids[:, half:], "tract", steps)
    planes = call(
        planes_kernel, [((3 * rows, SPAN * half), F32)], me, ids.astype(BF16), before.astype(BF16), name="planes"
    )[0]
    weight = conv_weight
    if copies > 1:
        near_by = [[g * copies + c for c in range(copies)] for g in range(OFFSETS)]
        weight = lax.all_gather(conv_weight.astype(BF16), "rows", axis=0, tiled=True, axis_index_groups=near_by)
    product, score_part, weight_low, table_low, vectors = call(
        functools.partial(table_kernel, list(slots)),
        [((values, width), BF16), ((8, values), F32), ((width, width), BF16), ((values, width), BF16), ((EXTRA, width), BF16)],
        me, *slots.values(), weight, name="products",
    )
    group_bits = [2 * copies, copies]
    score_slots = gather_slots(score_part, "rows", group_bits)
    score_slots = [score_slots[m * copies] for m in order]
    product_slots = gather_slots(product, "rows", group_bits)
    product_slots = [product_slots[m * copies] for m in order]

    cot = cotangent.reshape(rows * half, width)
    pair = [2, 3]
    far, codes, weights, probs, masks, averages = call(
        functools.partial(far_kernel, order, pair, values),
        [((2, values, width), BF16), ((SPAN, rows, half), F32), ((OFFSETS * REACH, rows, half), F32),
         ((2 * OFFSETS, rows, half), F32), ((OFFSETS * REACH, rows, half), F32), ((rows, half), F32)],
        group, *score_slots, planes, vectors, cot,
        scratch=[pltpu.VMEM((OFFSETS, 8, values), F32), pltpu.VMEM((2 * values, width), F32)],
        flops=2 * 2 * values * width * rows * half, name="far",
    )
    far_here = far[0] + swap(far[1], "rows", copies)
    far_other = swap(far_here, "rows", 2 * copies)
    near, bias_part = call(
        functools.partial(near_kernel, [0, 1], values),
        [((2, values, width), BF16), ((8, width), F32)],
        group, codes, weights, averages, cot,
        scratch=[pltpu.VMEM((2 * values + EXTRA, width), F32)],
        flops=2 * 2 * values * width * rows * half, name="near",
    )
    near_other = swap(near[1], "rows", copies)
    sums = call(
        functools.partial(score_kernel, order, values), [((8, 1024), F32)],
        group, *product_slots, planes, vectors, probs, masks, codes, bias_part, cot,
        scratch=[pltpu.VMEM((REACH, rows, half), F32), pltpu.VMEM((OFFSETS * REACH, rows, half), F32),
                 pltpu.VMEM((OFFSETS, 8, values), F32)],
        flops=4 * 2 * values * width * rows * half, name="scores",
    )[0]
    all_sums = list(gather_slots(sums, "rows", group_bits).values())

    exchanges = [("tract", 1 << at) for at in range(tract_count.bit_length() - 1)]
    exchanges += [("rows", 1 << at) for at in range(copies.bit_length() - 1)]
    halved = [e for at, e in enumerate(exchanges) if values >> (at + 1) >= 16]
    piece = jnp.zeros((1,), jnp.int32)
    for at, (axis, bit) in enumerate(halved):
        mine = tract_at if axis == "tract" else rows_at
        piece = piece + ((mine & bit) != 0).astype(jnp.int32) * (1 << at)
    block = call(
        functools.partial(merge_kernel, len(halved)), [((values + EXTRA, width), BF16)],
        piece, group, near[0], near_other, far_other, *all_sums, vectors,
        scratch=[pltpu.VMEM((8, 1024), F32)], scalars=2, name="merge",
    )[0]
    for axis, bit in halved:
        keep = (block.shape[0] - EXTRA) // 2
        other = swap(block[keep:], axis, bit)
        block = call(halve_kernel, [((keep + EXTRA, width), BF16)], me, block, other, name="halve")[0]
    for axis, bit in exchanges[len(halved) :]:
        other = swap(block, axis, bit)
        block = call(halve_kernel, [(block.shape, BF16)], me, block, other, name="whole")[0]
    ends = block[-EXTRA:].astype(F32)
    ends = ends[:2] + ends[8:10]
    block = block[:-EXTRA]
    for axis, bit in reversed(halved):
        block = jnp.concatenate([block, swap(block, axis, bit)], 0)

    full, table_part = call(
        functools.partial(share_kernel, len(halved)),
        [((values, width), BF16), ((values, width), BF16)], piece, group, block, weight_low,
        scalars=2, name="share",
    )
    for bit in group_bits:
        keep = table_part.shape[0] // 2
        other = swap(table_part[keep:].astype(BF16), "rows", bit)
        table_part = table_part[:keep].astype(F32) + other.astype(F32)
    out = call(
        functools.partial(output_kernel, order, values), [((rows * half, width), BF16)],
        group, *product_slots, codes, weights, averages, vectors,
        flops=4 * 2 * values * width * rows * half, name="output",
    )[0]
    if copies > 1:
        inside = rows_at % copies
        columns = lax.dynamic_slice_in_dim(table_low, inside * (width // copies), width // copies, 1)
        table_part = lax.dynamic_slice_in_dim(table_part, inside * table.shape[0], table.shape[0], 0)
    else:
        columns = table_low
    weight_grad = call(
        weight_kernel, [((conv_weight.shape[0], width), F32)], me, columns, full, name="weights",
    )[0]
    shard = conv_bias.shape[0]
    ends = lax.dynamic_slice_in_dim(ends, rows_at * shard, shard, 1)
    return out.reshape(cotangent.shape), table_part, weight_grad, ends[1], ends[0]


def solution(mesh):
    return jax.shard_map(
        body,
        mesh=mesh,
        in_specs=(
            P("rows", "tract"), P("rows", "tract"), P("rows", "tract"), P("rows", None),
            P("rows", None), P("rows"), P("rows"), P("rows", "tract", None),
        ),
        out_specs=(P("rows", "tract", None), P("rows", None), P("rows", None), P("rows"), P("rows")),
        check_vma=False,
    )
```

```python
import functools

import jax
import jax.numpy as jnp
from jax import lax
from jax.experimental import pallas as pl
from jax.experimental.pallas import tpu as pltpu
from jax.sharding import PartitionSpec as P

F32 = jnp.float32
BF16 = jnp.bfloat16
OFFSETS = 4
REACH = 5
SPAN = 8
EXTRA = 16
HALVINGS = 2
EDGE = 3
VMEM_LIMIT = 16 * 1024 * 1024
LONG = 10**11
NT = (((1,), (1,)), ((), ()))
TN = (((0,), (0,)), ((), ()))
NN = (((1,), (0,)), ((), ()))


def dot(a, b, dims=NN, precision=None):
    return lax.dot_general(a, b, dims, precision=precision, preferred_element_type=F32)


def exact(a, b, dims=NN):
    return dot(a, b, dims, lax.Precision.HIGHEST)


def call(kernel, outs, *operands, scratch=(), cost=0, name=None, after=(), final=False):
    vmem = pl.BlockSpec(memory_space=pltpu.VMEM)
    hbm = pl.BlockSpec(memory_space=pltpu.HBM)
    stored = [isinstance(operand, tuple) for operand in operands]
    held = [
        pltpu.with_memory_space_constraint(operand[0] if far else operand, pltpu.HBM if far else pltpu.VMEM)
        for operand, far in zip(operands, stored)
    ]
    count = len(operands)

    def run(*refs):
        kernel(*refs[:count], *refs[count + len(after) :])

    return pl.pallas_call(
        run if after else kernel,
        out_shape=[jax.ShapeDtypeStruct(*o) if final else pltpu.VMEM(*o) for o in outs],
        in_specs=[hbm if far else vmem for far in stored] + [pl.BlockSpec(memory_space=pl.ANY)] * len(after),
        out_specs=[vmem] * len(outs),
        scratch_shapes=list(scratch),
        compiler_params=pltpu.CompilerParams(vmem_limit_bytes=VMEM_LIMIT),
        cost_estimate=pl.CostEstimate(flops=cost, bytes_accessed=0, transcendentals=0),
        name=name,
    )(*held, *after)


def swap(value, axis, bit):
    count = lax.axis_size(axis)
    return lax.ppermute(value, axis, [(i, i ^ bit) for i in range(count)])


def gather_slots(value, axis, bits):
    slots = {0: value}
    for bit in bits:
        for m in list(slots):
            slots[m | bit] = swap(slots[m], axis, bit)
    return slots


def row_index():
    return lax.axis_index("rows")


def group_index():
    return lax.axis_index("rows") // (lax.axis_size("rows") // OFFSETS)


def piece_index():
    return lax.axis_index("tract") % (1 << HALVINGS)


def load_kernel(rows, *refs):
    weight, table, score, bias = refs[:4]
    ids = refs[4:7]
    weight_low, table_low, score_here, bias_here, together, tail = refs[7:13]
    weight_here, table_here, ids_here, sems = refs[13:]
    parts = weight_here.shape[0]
    size = weight_here.shape[1]
    copies = [pltpu.make_async_copy(source, ids_here.at[at], sems.at[at]) for at, source in enumerate(ids)]
    copies.append(pltpu.make_async_copy(table, table_here, sems.at[3]))
    copies.append(pltpu.make_async_copy(score, score_here, sems.at[4]))
    copies.append(pltpu.make_async_copy(bias, bias_here, sems.at[5]))
    copies += [
        pltpu.make_async_copy(weight.at[pl.ds(at * size, size), :], weight_here.at[at], sems.at[6 + at]) for at in range(parts)
    ]
    for copy in copies:
        copy.start()
    length = ids_here.shape[2]
    for at in range(3):
        copies[at].wait()
        together[at * rows : (at + 1) * rows, :] = ids_here[at].astype(F32)
        tail[at * rows : (at + 1) * rows, :] = ids_here[at, :, length - tail.shape[1] :]
    copies[3].wait()
    table_low[...] = table_here[...].astype(BF16)
    copies[4].wait()
    copies[5].wait()
    for at in range(parts):
        copies[6 + at].wait()
        weight_low[at * size : (at + 1) * size, :] = weight_here[at].astype(BF16)


def kept_kernel(*refs):
    half = len(refs) // 2
    for value, out in zip(refs[:half], refs[half:]):
        out[...] = value[...]


def placed(parts, width):
    total = None
    for part, at in parts:
        shard = part.shape[1]
        source = lax.broadcasted_iota(jnp.int32, (shard, width), 0) + at * shard
        column = lax.broadcasted_iota(jnp.int32, (shard, width), 1)
        row = jnp.broadcast_to(part[...], (8, shard)).astype(BF16)
        got = dot(row, (source == column).astype(BF16))
        total = got if total is None else total + got
    return total


def scorer_kernel(order, near_order, *refs):
    scores = refs[: len(order)]
    biases = refs[len(order) : len(order) + len(near_order)]
    weight_low, scorer, out = refs[len(order) + len(near_order) :]
    width = out.shape[1]
    full = placed([(part, row_index() ^ m) for part, m in zip(scores, order)], width)
    bias = placed([(part, row_index() ^ m) for part, m in zip(biases, near_order)], width)
    full = jnp.concatenate([full, full], 0).astype(BF16)
    scorer[...] = full
    at = lax.broadcasted_iota(jnp.int32, bias.shape, 0)
    out[...] = jnp.where(at == 0, dot(full, weight_low[...], NT)[:8], bias)


def table_kernel(order, *refs):
    slots = refs[: len(order)]
    weight_low, product, table_low, table_turned = refs[len(order) :]
    rows = slots[0].shape[0]
    for slot, m in zip(slots, order):
        at = pl.multiple_of((row_index() ^ m) * rows, rows)
        table_low[pl.ds(at, rows), :] = slot[...].astype(BF16)
    product[...] = dot(table_low[...], weight_low[...]).astype(BF16)
    table_turned[...] = table_low[...].T


def planes_kernel(ids, before, out, hot):
    length = ids.shape[1]
    rows = ids.shape[0] // 3
    half = length // 2
    tail = before.shape[1]
    ids = ids[...].astype(BF16)
    earlier = before[...].astype(F32).astype(BF16)
    for m in range(SPAN):
        target = 2 * lax.broadcasted_iota(jnp.int32, (length, half), 1) + 1 - m
        source = lax.broadcasted_iota(jnp.int32, (length, half), 0)
        got = dot(ids, (source == target).astype(BF16))
        if m > 1:
            target = 2 * lax.broadcasted_iota(jnp.int32, (tail, half), 1) + 1 - m + tail
            source = lax.broadcasted_iota(jnp.int32, (tail, half), 0)
            got = got + dot(earlier, (source == target).astype(BF16))
        out[:, m * half : (m + 1) * half] = got
    values = hot.shape[0]
    name = names(values, half)
    for side in range(2):
        for row in range(rows):
            code = out[row : row + 1, side * half : (side + 1) * half]
            hot[:, (side * rows + row) * half : (side * rows + row + 1) * half] = one_hot(name, code)
    edge = gathered_edges([out[:rows, (SPAN - 2 + side) * half : (SPAN - 1 + side) * half] for side in range(2)])
    hot[:, 2 * rows * half :] = one_hot(name, edge)


def names(values, lanes):
    shape = (values // 16, 16, lanes)
    return (lax.broadcasted_iota(jnp.int32, shape, 0) * 16 + lax.broadcasted_iota(jnp.int32, shape, 1)).astype(F32).astype(BF16)


def one_hot(name, code):
    code = jnp.broadcast_to(code, name.shape[1:]).astype(BF16)
    return jnp.where(name == code[None], jnp.ones(name.shape, BF16), jnp.zeros(name.shape, BF16)).reshape(-1, name.shape[2])


def gathered_edges(planes):
    rows, lanes = planes[0].shape
    lane = lax.broadcasted_iota(jnp.int32, (rows, lanes), 1)
    row = lax.broadcasted_iota(jnp.int32, (rows, lanes), 0)
    total = jnp.zeros((rows, lanes), F32)
    for side, plane in enumerate(planes):
        for at in range(EDGE):
            place = (side * rows + row) * EDGE + at
            total = total + jnp.where(lane == place, plane[:, at : at + 1], 0.0)
    return jnp.sum(total, 0, keepdims=True)


class Window:
    def __init__(self, mask):
        self.mask = mask
        self.keep, self.divide = [], []
        for side in range(2):
            keep = [self.mask[k, side] for k in range(OFFSETS)]
            counts, total = [], 0.0
            for k in range(OFFSETS):
                total = total + keep[k]
                counts.append(1.0 / jnp.maximum(total, 1.0))
            self.keep.append(keep)
            self.divide.append(counts)

    def pooled(self, side, values):
        means, total = [], 0.0
        for k in range(OFFSETS):
            total = total + self.keep[side][k] * values[side + k]
            means.append(total * self.divide[side][k])
        return means

    def spread(self, sides):
        result = [0.0] * REACH
        for side in range(2):
            carried = 0.0
            for k in reversed(range(OFFSETS)):
                carried = carried + sides[side][k] * self.divide[side][k]
                result[side + k] = result[side + k] + self.keep[side][k] * carried
        return result


def window_of(planes, rows):
    half = planes.shape[1] // SPAN

    def part(which, m):
        return planes[which * rows : (which + 1) * rows, m * half : (m + 1) * half]

    segments = [part(1, m) for m in range(SPAN)]
    valid = [part(2, m) for m in range(SPAN)]
    mask = {
        (k, j): (segments[j + k] == segments[j]).astype(F32) * valid[j + k]
        for k in range(OFFSETS)
        for j in range(REACH)
    }
    return [part(0, m) for m in range(SPAN)], Window(mask)


CODES = 0
WEIGHTS = CODES + SPAN
MASKS = WEIGHTS + OFFSETS * REACH
PROBS = MASKS + OFFSETS * REACH
AVERAGE = PROBS + 2 * OFFSETS
PLANES = AVERAGE + 1


def lookup(row, codes):
    index = codes.astype(jnp.int32)
    lanes = 128
    low = jnp.bitwise_and(index, lanes - 1)
    parts = [
        jnp.take_along_axis(
            jnp.broadcast_to(row[:, at : at + lanes], codes.shape), low, axis=1
        )
        for at in range(0, row.shape[1], lanes)
    ]
    return jnp.where(index >= lanes, parts[1], parts[0])


def packed_row(ref, plane, row):
    return jnp.broadcast_to(ref[plane, pl.ds(row, 1), :], (16, ref.shape[2])).astype(BF16)


def spread_rows(plan, k, row, values):
    lanes = plan.shape[2]
    blocks = values // 16
    name = names(values, lanes)
    total = jnp.zeros((blocks, 16, lanes), BF16)
    for j in range(REACH):
        code = packed_row(plan, CODES + k + j, row)
        weight = packed_row(plan, WEIGHTS + k * REACH + j, row)
        total = jnp.where(name == code[None], total + weight[None], total)
    return total.reshape(values, lanes)


def accumulate(plan, total_ref, ks, cot, values, extra=None):
    rows, half = plan.shape[1:]
    for chunk in range(rows // 2):
        pieces = [
            jnp.concatenate(
                [
                    spread_rows(plan, k, 2 * chunk, values),
                    spread_rows(plan, k, 2 * chunk + 1, values),
                ],
                1,
            )
            for k in ks
        ]
        if extra is not None:
            pieces.append(extra(chunk))
        left = jnp.concatenate(pieces, 0)
        part = dot(left, cot[2 * chunk * half : 2 * (chunk + 1) * half, :])
        if chunk == 0:
            total_ref[...] = part
        else:
            total_ref[...] += part


def split(value):
    high = value.astype(BF16)
    return high, (value - high.astype(F32)).astype(BF16)


def thirds(value):
    high = value.astype(BF16)
    rest = value - high.astype(F32)
    middle = rest.astype(BF16)
    return high, middle, (rest - middle.astype(F32)).astype(BF16)


def far_kernel(order, slots, values, *refs):
    scorers = refs[: len(order)]
    table_low, planes, scorer, cot = refs[len(order) : len(order) + 4]
    own, sent, sent_too, plan, vectors, table, total = refs[len(order) + 4 :]
    rows = plan.shape[1]
    every = jnp.concatenate([s[...] for s in scorers], 0)
    parts = thirds(every)
    found = dot(jnp.concatenate(parts, 0), table_low[...], NT)
    count = every.shape[0]
    found = found[:count] + found[count : 2 * count] + found[2 * count :]
    for at, m in enumerate(order):
        table[group_index() ^ m] = found[at * 8 : (at + 1) * 8]
    codes, window = window_of(planes[...], rows)
    bias = functools.reduce(jnp.add, [s[1:2] for s in scorers])
    both = [scorer[:8].astype(F32), jnp.broadcast_to(bias, (8, bias.shape[1]))]
    vectors[...] = jnp.concatenate(both, 0).astype(BF16)
    shared = jnp.sum(both[0] * both[1], 1, keepdims=True)[:1]
    conv_scores = [shared] * REACH
    for k in range(OFFSETS):
        row = table[k, :1, :]
        for m in range(k, k + REACH):
            conv_scores[m - k] = conv_scores[m - k] + window.mask[k, m - k] * lookup(row, codes[m])
    for m in range(SPAN):
        plan[CODES + m] = codes[m]
    shares = []
    for side in range(2):
        block = window.pooled(side, conv_scores)
        top = functools.reduce(jnp.maximum, block)
        exps = [jnp.exp(b - top) for b in block]
        inverse = 1.0 / functools.reduce(jnp.add, exps)
        shares.append([e * inverse for e in exps])
        for k in range(OFFSETS):
            plan[PROBS + side * OFFSETS + k] = shares[side][k]
    mixing = [0.5 * e for e in window.spread(shares)]
    plan[AVERAGE] = functools.reduce(jnp.add, mixing)
    for k in range(OFFSETS):
        for j in range(REACH):
            plan[MASKS + k * REACH + j] = window.mask[k, j]
            plan[WEIGHTS + k * REACH + j] = window.mask[k, j] * mixing[j]
    accumulate(plan, total, [group_index() ^ m for m in slots], cot, values)
    own[...] = total[:values]
    sent[...] = total[values : values + values // 2].astype(BF16)
    sent_too[...] = total[values + values // 2 : 2 * values].astype(BF16)


def average_line(plan, chunk):
    return jnp.concatenate([plan[AVERAGE, row : row + 1, :] for row in (2 * chunk, 2 * chunk + 1)], 1)


def near_kernel(slots, values, plan, cot, own, sent, bias_out, total):
    half = plan.shape[2]

    def extra(chunk):
        line = jnp.broadcast_to(average_line(plan, chunk), (EXTRA, 2 * half))
        high, low = split(line)
        at = lax.broadcasted_iota(jnp.int32, line.shape, 0)
        return jnp.where(at == 0, high.astype(F32), jnp.where(at == 1, low.astype(F32), 0.0)).astype(BF16)

    accumulate(plan, total, [group_index() ^ m for m in slots], cot, values, extra)
    own[...] = total[:values]
    sent[...] = total[values : 2 * values].astype(BF16)
    end = total[len(slots) * values :]
    bias_out[...] = jnp.broadcast_to(end[:1] + end[1:2], (8, end.shape[1]))


def inner_kernel(order, values, *refs):
    products = refs[: len(order)]
    plan, vectors, cot = refs[len(order) : len(order) + 3]
    before, out = (refs[-2] if len(refs) > len(order) + 4 else None), refs[-1]
    rows, half = plan.shape[1:]
    blocks = values // 16
    name = names(values, half)
    for chunk in range(rows // 2):
        here = cot[2 * chunk * half : 2 * (chunk + 1) * half, :]
        base = dot(vectors[8:], here, NT) if before is None else None
        found = {}
        for slot, m in zip(products, order):
            k = group_index() ^ m
            each = dot(slot[...], here, NT).astype(BF16)
            for side in range(2):
                row = 2 * chunk + side
                mine = each[:, side * half : (side + 1) * half].reshape(blocks, 16, half)
                for j in range(REACH):
                    code = packed_row(plan, CODES + k + j, row)
                    picked = jnp.zeros((16, half), BF16)
                    for at in range(blocks):
                        picked = jnp.where(name[at] == code, mine[at], picked)
                    mask = plan[MASKS + k * REACH + j, row : row + 1, :]
                    found[j, side] = found.get((j, side), 0.0) + picked.astype(F32) * mask
        for side in range(2):
            row = 2 * chunk + side
            for j in range(REACH):
                if before is None:
                    start = base[:1, side * half : (side + 1) * half]
                else:
                    start = before[j, row : row + 1, :]
                out[j, row : row + 1, :] = jnp.sum(found[j, side], 0, keepdims=True) + start


def score_kernel(order, values, *refs):
    products = refs[: len(order)]
    inner_ref, plan, vectors, hot = refs[len(order) : len(order) + 4]
    out, flat, rows_ref = refs[len(order) + 4 :]
    rows, half = plan.shape[1:]
    biases = vectors[8:]
    window = Window({(k, j): plan[MASKS + k * REACH + j] for k in range(OFFSETS) for j in range(REACH)})
    inner_rows = [0.5 * inner_ref[j] for j in range(REACH)]
    sides = []
    for side in range(2):
        inner = window.pooled(side, inner_rows)
        share = [plan[PROBS + side * OFFSETS + k] for k in range(OFFSETS)]
        mean = functools.reduce(jnp.add, [s * i for s, i in zip(share, inner)])
        sides.append([s * (i - mean) for s, i in zip(share, inner)])
    grads = window.spread(sides)
    overall = jnp.sum(jnp.sum(functools.reduce(jnp.add, grads), 1, keepdims=True), 0, keepdims=True)
    lane = lax.broadcasted_iota(jnp.int32, (rows, half), 1)
    flat[...] = jnp.zeros(flat.shape, F32)
    for k in range(OFFSETS):
        edges = []
        for side in range(2):
            inside = jnp.zeros((rows, half), F32)
            edge = jnp.zeros((rows, half), F32)
            for m in range(side, SPAN, 2):
                if not 0 <= m - k < REACH:
                    continue
                value = grads[m - k] * window.mask[k, m - k]
                steps = m // 2
                if steps:
                    inside = inside + jnp.where(lane < half - steps, pltpu.roll(value, half - steps, 1), 0.0)
                    moved = pltpu.roll(value, EDGE - steps, 1) if steps < EDGE else value
                    edge = edge + jnp.where((lane >= EDGE - steps) & (lane < EDGE), moved, 0.0)
                else:
                    inside = inside + value
            for row in range(rows):
                at = (side * rows + row) * half
                flat[k : k + 1, at : at + half] = inside[row : row + 1, :]
            edges.append(edge)
        flat[k : k + 1, 2 * rows * half :] = gathered_edges(edges)
    high, low = split(flat[...])
    both = jnp.concatenate([high.astype(F32), low.astype(F32)], 0).astype(BF16)
    lines = dot(both, hot[...], NT)
    lines = lines[:8] + lines[8:]
    for k in range(OFFSETS):
        rows_ref[k] = jnp.broadcast_to(lines[k : k + 1], (8, values))
    width = biases.shape[1]
    score_grad = jnp.zeros((1, width), F32)
    for slot, m in zip(products, order):
        got = dot(pack(rows_ref[group_index() ^ m]), slot[...])
        score_grad = score_grad + got[:1] + got[8:9]
    out[...] = jnp.zeros(out.shape, F32)
    out[:1] = score_grad + overall * biases[:1].astype(F32)
    out[1:2] = overall * vectors[:1].astype(F32)
    for k in range(OFFSETS):
        out[2 + k : 3 + k, :values] = lines[k : k + 1]


def output_kernel(order, values, chunks_here, *refs):
    products = refs[: len(order)]
    plan, vectors = refs[len(order) : len(order) + 2]
    out, token, staged, sems = refs[-4:]
    token[...] = jnp.zeros(token.shape, F32)
    half = plan.shape[2]
    step = 2 * half
    biases = vectors[8:].astype(F32)
    at = lax.broadcasted_iota(jnp.int32, (8, step), 0)
    first = lax.broadcasted_iota(jnp.int32, biases.shape, 0)
    biases = jnp.where(first < 2, biases, 0.0)
    copies = []
    for place, chunk in enumerate(chunks_here):
        high, low = split(jnp.broadcast_to(average_line(plan, chunk), (8, step)))
        both = jnp.where(at == 0, high.astype(F32), jnp.where(at == 1, low.astype(F32), 0.0))
        total = dot(both, biases, TN)
        for slot, m in zip(products, order):
            k = group_index() ^ m
            left = jnp.concatenate([spread_rows(plan, k, row, values) for row in (2 * chunk, 2 * chunk + 1)], 1)
            total = total + dot(left, slot[...], TN)
        staged[place * step : (place + 1) * step, :] = total.astype(BF16)
        copies.append(
            pltpu.make_async_copy(
                staged.at[pl.ds(place * step, step), :], out.at[pl.ds(chunk * step, step), :], sems.at[place]
            )
        )
        copies[-1].start()
    for copy in copies:
        copy.wait()


def output_part(before, part, parts, order, values, products, plan, vectors, after):
    rows, half = plan.shape[1:]
    width = vectors.shape[1]
    each = rows // 2 // parts
    operands = [pltpu.with_memory_space_constraint(x, pltpu.VMEM) for x in (*products, plan, vectors)]
    operands += [] if before is None else [pltpu.with_memory_space_constraint(before, pltpu.HBM)]
    vmem = pl.BlockSpec(memory_space=pltpu.VMEM)
    elsewhere = pl.BlockSpec(memory_space=pl.ANY)
    count = len(products) + 2
    chunks_here = range(part * each, (part + 1) * each)

    def run(*refs):
        output_kernel(order, values, chunks_here, *refs[:count], *refs[-4:])

    return pl.pallas_call(
        run,
        out_shape=[jax.ShapeDtypeStruct((rows * half, width), BF16), pltpu.VMEM((8, 128), F32)],
        in_specs=[vmem] * count + [elsewhere] * (len(operands) - count + len(after)),
        out_specs=[elsewhere, vmem],
        input_output_aliases={} if before is None else {count: 0},
        scratch_shapes=[pltpu.VMEM((2 * half * each, width), BF16), pltpu.SemaphoreType.DMA((each,))],
        compiler_params=pltpu.CompilerParams(vmem_limit_bytes=VMEM_LIMIT),
        cost_estimate=pl.CostEstimate(flops=0, bytes_accessed=0, transcendentals=0),
        name="output",
    )(*operands, *after)


def reversed_bits(number, bits):
    return sum((((number >> b) & 1) << (bits - 1 - b)) for b in range(bits))


def chunks(bits, values, piece, group):
    block = values // OFFSETS
    size = block >> bits
    for actual in range(1 << bits):
        place = reversed_bits(piece ^ actual, bits) * OFFSETS * size
        for offset in range(OFFSETS):
            at = pl.multiple_of(place + (group ^ offset) * size, size)
            yield offset * block + actual * size, at, size


def pack(rows):
    high, low = split(rows)
    return jnp.concatenate([high.astype(F32), low.astype(F32)], 0).astype(BF16)


def unpack(block):
    return block[:8].astype(F32) + block[8:].astype(F32)


def merge_kernel(bits, near, near_other, far_other, sums, bias, keep, send, total):
    values = near.shape[0]
    summed = near[...] + near_other[...].astype(F32) + far_other[...].astype(F32)
    for source, at, size in chunks(bits, values, piece_index(), group_index()):
        total[pl.ds(at, size), :] = summed[source : source + size]
    part = keep.shape[0]
    keep[...] = total[:part]
    send[: values - part] = total[values - (values - part) :].astype(BF16)
    second = lax.broadcasted_iota(jnp.int32, bias.shape, 0) == 1
    send[values - part :] = pack(sums[...] + jnp.where(second, bias[...], 0.0))


def halve_kernel(mine, own_sent, other, keep, send):
    rows = mine.shape[0]
    total = mine[...] + other[:rows].astype(F32)
    part = keep.shape[0]
    keep[...] = total[:part]
    rest = send.shape[0] - EXTRA
    send[:rest] = total[rows - rest :].astype(BF16)
    send[rest:] = pack(unpack(own_sent[own_sent.shape[0] - EXTRA :]) + unpack(other[rows:]))


def whole_kernel(mine, other, send):
    rows = mine.shape[0] - EXTRA
    send[:rows] = (mine[:rows].astype(F32) + other[:rows].astype(F32)).astype(BF16)
    send[rows:] = pack(unpack(mine[rows:]) + unpack(other[rows:]))


def last_kernel(mine, other, block, sums):
    rows = block.shape[0]
    block[...] = (mine[:rows].astype(F32) + other[:rows].astype(F32)).astype(BF16)
    sums[...] = unpack(mine[rows:]) + unpack(other[rows:])


def share_kernel(block, sums, weight_low, keep, *sends):
    product = dot(block[...], weight_low[...], NT)
    rows = keep.shape[0]
    keep[...] = product[:rows]
    for at, send in enumerate(sends):
        send[:rows] = product[(at + 1) * rows : (at + 2) * rows].astype(BF16)
        send[rows:] = pack(sums[...])


def combine_kernel(keep, sums, *refs):
    others, (out, total) = refs[:-2], refs[-2:]
    rows = keep.shape[0]
    out[...] = functools.reduce(jnp.add, [keep[...]] + [o[:rows].astype(F32) for o in others]).astype(BF16)
    total[...] = functools.reduce(jnp.add, [sums[...]] + [unpack(o[rows:]) for o in others])


def added_kernel(mine, other, out):
    out[...] = (mine[...].astype(F32) + other[...].astype(F32)).astype(out.dtype)


def joined_kernel(mine, one, two, out):
    rows = one.shape[0]
    out[:rows] = (mine[:rows] + one[...].astype(F32)).astype(out.dtype)
    out[rows:] = (mine[rows:] + two[...].astype(F32)).astype(out.dtype)


def weight_kernel(bits, order, *refs):
    slots = refs[: len(order)]
    turned, vectors, sums, out, token, full = refs[len(order) :]
    token[...] = jnp.zeros(token.shape, F32)
    values = full.shape[0]
    placed = {m: slot for m, slot in zip(order, slots)}
    size = values // OFFSETS >> bits
    for m in range(1 << bits):
        for offset in range(OFFSETS):
            at = (group_index() ^ offset) * (values // OFFSETS) + (piece_index() ^ m) * size
            full[pl.ds(pl.multiple_of(at, size), size), :] = placed[m][offset * size : (offset + 1) * size]
    line = sums[pl.ds(group_index() + 2, 1), :values]
    scores = jnp.concatenate([vectors[:8], vectors[:8]], 0)
    first = lax.broadcasted_iota(jnp.int32, (8, values), 0) == 0
    through = dot(turned[...], pack(jnp.where(first, jnp.broadcast_to(line, first.shape), 0.0)), NT)
    high, low = split(through)
    out[...] = dot(turned[...], full[...]) + dot(high, scores) + dot(low, scores)


def table_grad_kernel(bits, order, offsets, *refs):
    slots = refs[: len(order)]
    scorers = refs[len(order) : len(order) + len(offsets)]
    sums, out, score_out, bias_out, table, full, rows_ref = refs[len(order) + len(offsets) :]
    values = full.shape[0]
    width = out.shape[1]
    high, low = split(sums[2 : 2 + OFFSETS, :values])
    for scorer, m in zip(scorers, offsets):
        rows_ref[group_index() ^ m] = scorer[...]
    right = jnp.concatenate([rows_ref[k, :1] for k in range(OFFSETS)], 0)
    right_high, right_low = split(right)
    left = jnp.concatenate([x.astype(F32) for x in (high, low, high, low)], 0).astype(BF16)
    right = jnp.concatenate([x.astype(F32) for x in (right_high, right_high, right_low, right_low)], 0).astype(BF16)
    full[...] = dot(left, right, TN)
    for slot, m in zip(slots, order):
        size = slot.shape[0]
        table[pl.ds(pl.multiple_of((piece_index() ^ m) * size, size), size), :] = slot[...].astype(F32)
    rows = out.shape[0]
    at = pl.multiple_of(row_index() * rows, rows)
    inside = row_index() * rows - group_index() * table.shape[0]
    out[...] = table[pl.ds(pl.multiple_of(inside, rows), rows), :] + full[pl.ds(at, rows), :]
    shard = score_out.shape[1]
    source = lax.broadcasted_iota(jnp.int32, (width, shard), 0)
    column = lax.broadcasted_iota(jnp.int32, (width, shard), 1) + row_index() * shard
    here = (source == column).astype(BF16)
    ends = functools.reduce(jnp.add, [dot(part, here) for part in thirds(sums[...])])
    score_out[...] = ends[:1]
    bias_out[...] = ends[1:2]


def bits_of(count):
    return [1 << at for at in reversed(range(count.bit_length() - 1))]


def body(byte_values, segment_ids, valid, table, conv_weight, conv_bias, score_weight, cotangent):
    rows_count, tract_count = lax.axis_size("rows"), lax.axis_size("tract")
    rows_at = lax.axis_index("rows")
    values, width = table.shape[0] * rows_count, table.shape[1]
    rows, length = byte_values.shape
    half = length // 2
    copies = rows_count // OFFSETS
    order = [0, 2, 1, 3]
    group_bits = [2 * copies, copies]
    near_bits = [bit for bit in bits_of(rows_count) if bit < copies]

    score_slots = gather_slots(score_weight[None], "rows", bits_of(rows_count))
    bias_slots = gather_slots(conv_bias[None], "rows", near_bits)
    weight = conv_weight
    if copies > 1:
        near_by = [[g * copies + c for c in range(copies)] for g in range(OFFSETS)]
        weight = lax.all_gather(conv_weight, "rows", axis=0, tiled=True, axis_index_groups=near_by)
    parts = 4
    shard = (1, conv_bias.shape[0])
    weight_low, shard_low, score_slots[0], bias_slots[0], ids, tail = call(
        functools.partial(load_kernel, rows),
        [(weight.shape, BF16), (table.shape, BF16), (shard, F32), (shard, F32), ((3 * rows, length), F32),
         ((3 * rows, 128), jnp.int32)],
        (weight,), (table,), (score_weight[None],), (conv_bias[None],), (byte_values,), (segment_ids,), (valid,),
        scratch=[pltpu.VMEM((parts, weight.shape[0] // parts, width), F32), pltpu.VMEM(table.shape, F32),
                 pltpu.VMEM((3, rows, length), jnp.int32), pltpu.SemaphoreType.DMA((6 + parts,))],
        name="load",
    )
    scorer, scored = call(
        functools.partial(scorer_kernel, list(score_slots), list(bias_slots)),
        [((EXTRA, width), BF16), ((8, width), F32)], *score_slots.values(), *bias_slots.values(), weight_low, name="scorer",
    )
    scorers = gather_slots(scored, "rows", group_bits)
    scorers = [scorers[m * copies] for m in order]
    tail = call(kept_kernel, [(tail.shape, jnp.int32)], tail, name="tail", after=[scored])[0]
    before = lax.ppermute(tail, "tract", [(i, i + 1) for i in range(tract_count - 1)])
    planes, hot = call(
        planes_kernel, [((3 * rows, SPAN * half), F32), ((values, 2 * rows * half + 128), BF16)],
        ids, before, name="planes", after=[scored],
    )
    table_slots = {0: shard_low}
    for bit in bits_of(rows_count):
        for m in list(table_slots):
            value = table_slots[m]
            if m:
                value = call(kept_kernel, [(table.shape, BF16)], value, name="table_low", after=[planes, scorers[1]])[0]
            table_slots[m | bit] = swap(value, "rows", bit)
    product, table_low, turned = call(
        functools.partial(table_kernel, list(table_slots)),
        [((values, width), BF16), ((values, width), BF16), ((width, values), BF16)],
        *table_slots.values(), weight_low, name="products", after=[scored],
    )

    cot = cotangent.reshape(rows * half, width)
    far, *far_sent, plan, vectors = call(
        functools.partial(far_kernel, order, [2, 3], values),
        [((values, width), F32), ((values // 2, width), BF16), ((values // 2, width), BF16), ((PLANES, rows, half), F32), ((EXTRA, width), BF16)],
        *scorers, table_low, planes, scorer, cot,
        scratch=[pltpu.VMEM((OFFSETS, 8, values), F32), pltpu.VMEM((2 * values, width), F32)], name="far",
    )
    far_sent = [swap(half_sent, "rows", copies) for half_sent in far_sent]
    far = call(joined_kernel, [((values, width), BF16)], far, *far_sent, name="far_sum")[0]
    far_other = swap(far, "rows", 2 * copies)
    near, near_sent, bias_part = call(
        functools.partial(near_kernel, [0, 1], values),
        [((values, width), F32), ((values, width), BF16), ((8, width), F32)], plan, cot,
        scratch=[pltpu.VMEM((2 * values + EXTRA, width), F32)], name="near", after=[far],
    )
    near_other = swap(near_sent, "rows", copies)

    products = {0: product, 1: swap(product, "rows", copies), 2: swap(product, "rows", 2 * copies)}
    inner = call(
        functools.partial(inner_kernel, [0, 1], values), [((REACH, rows, half), F32)],
        products[0], products[1], plan, vectors, cot, name="inner_near", after=[near_sent], cost=LONG,
    )[0]
    passed = call(kept_kernel, [((values, width), BF16)], products[2], name="passed", after=[near_sent])[0]
    products[3] = swap(passed, "rows", copies)
    inner = call(
        functools.partial(inner_kernel, [2, 3], values), [((REACH, rows, half), F32)],
        products[2], products[3], plan, vectors, cot, inner, name="inner_far",
    )[0]
    products = [products[m] for m in order]
    sums = call(
        functools.partial(score_kernel, order, values), [((8, width), F32)], *products, inner, plan, vectors, hot,
        scratch=[pltpu.VMEM((8, hot.shape[1]), F32), pltpu.VMEM((OFFSETS, 8, values), F32)], name="scores",
    )[0]

    exchanges = [("tract", 1 << at) for at in range(tract_count.bit_length() - 1)]
    exchanges += [("rows", 1 << at) for at in range(copies.bit_length() - 1)]
    halved, rest = exchanges[:HALVINGS], exchanges[HALVINGS:]
    size = values // 2
    keep, send = call(
        functools.partial(merge_kernel, HALVINGS), [((size, width), F32), ((size + EXTRA, width), BF16)],
        near, near_other, far_other, sums, bias_part, scratch=[pltpu.VMEM((values, width), F32)], name="merge",
    )
    out = None

    def fill(out, parts, after):
        for part in parts:
            out, token = output_part(out, part, 4, order, values, products, plan, vectors, after)
        return out, token

    for at, (axis, bit) in enumerate(halved):
        other = swap(send, axis, bit)
        out, token = fill(out, [0, 1] if at == 0 else [2], [send])
        last = at + 1 == HALVINGS
        size = size if last else size // 2
        keep, send = call(
            halve_kernel, [((size, width), F32), ((size + EXTRA, width), BF16)], keep, send, other, name="halve", after=[token],
        )
    out, token = fill(out, [3], [send])
    for axis, bit in rest[:-1]:
        other = swap(send, axis, bit)
        send = call(whole_kernel, [(send.shape, BF16)], send, other, name="whole")[0]
    other = swap(send, *rest[-1])
    block, sums = call(last_kernel, [((size, width), BF16), ((8, width), F32)], send, other, name="last", after=[token])

    part = size // OFFSETS
    table_keep, *table_sends = call(
        share_kernel, [((part, width), F32)] + [((part + EXTRA, width), BF16)] * (OFFSETS - 1), block, sums, weight_low, name="share",
    )
    table_others = [swap(send, "rows", (at + 1) * copies) for at, send in enumerate(table_sends)]
    blocks = {0: block} | {m: swap(block, "tract", m) for m in range(1, 1 << HALVINGS)}
    table_piece, sums = call(
        combine_kernel, [((part, width), BF16), ((8, width), F32)], table_keep, sums, *table_others, name="combine",
    )
    table_pieces = {0: table_piece} | {m: swap(table_piece, "tract", m) for m in range(1, 1 << HALVINGS)}
    if copies > 1:
        turned = lax.dynamic_slice_in_dim(turned, rows_at % copies * (width // copies), width // copies, 0)
    weight_grad, token = call(
        functools.partial(weight_kernel, HALVINGS, list(blocks)), [((conv_weight.shape[0], width), F32), ((8, 128), F32)],
        *blocks.values(), turned, vectors, sums, scratch=[pltpu.VMEM((values, width), BF16)], name="weights", final=True,
    )
    table_grad, score_grad, bias_grad = call(
        functools.partial(table_grad_kernel, HALVINGS, list(table_pieces), order),
        [(table.shape, F32), (shard, F32), (shard, F32)], *table_pieces.values(), *scorers, sums,
        scratch=[pltpu.VMEM((values // OFFSETS, width), F32), pltpu.VMEM((values, width), F32), pltpu.VMEM((OFFSETS, 8, width), F32)],
        name="table_grad", final=True, after=[token],
    )
    return out.reshape(cotangent.shape), table_grad, weight_grad, bias_grad[0], score_grad[0]


def solution(mesh):
    return jax.shard_map(
        body,
        mesh=mesh,
        in_specs=(
            P("rows", "tract"), P("rows", "tract"), P("rows", "tract"), P("rows", None),
            P("rows", None), P("rows"), P("rows"), P("rows", "tract", None),
        ),
        out_specs=(P("rows", "tract", None), P("rows", None), P("rows", None), P("rows"), P("rows")),
        check_vma=False,
    )
```

```python
import functools

import jax
import jax.numpy as jnp
from jax import lax
from jax.experimental import pallas as pl
from jax.experimental.pallas import tpu as pltpu
from jax.sharding import PartitionSpec as P

F32 = jnp.float32
BF16 = jnp.bfloat16
OFFSETS = 4
REACH = 5
SPAN = 8
EXTRA = 16
PIECES = 4
EDGE = 3
VMEM_LIMIT = 16 * 1024 * 1024
SENT = 48
LONG = 10**11
NT = (((1,), (1,)), ((), ()))
TN = (((0,), (0,)), ((), ()))
NN = (((1,), (0,)), ((), ()))


def dot(a, b, dims=NN, precision=None):
    return lax.dot_general(a, b, dims, precision=precision, preferred_element_type=F32)


def exact(a, b, dims=NN):
    return dot(a, b, dims, lax.Precision.HIGHEST)


def call(kernel, outs, *operands, scratch=(), cost=0, name=None, after=(), final=0, copied=False):
    vmem = pl.BlockSpec(memory_space=pltpu.VMEM)
    hbm = pl.BlockSpec(memory_space=pltpu.HBM)
    stored = [isinstance(operand, tuple) for operand in operands]
    held = [
        pltpu.with_memory_space_constraint(operand[0] if far else operand, pltpu.HBM if far else pltpu.VMEM)
        for operand, far in zip(operands, stored)
    ]
    count = len(operands)

    def run(*refs):
        kernel(*refs[:count], *refs[count + len(after) :])

    return pl.pallas_call(
        run if after else kernel,
        out_shape=[jax.ShapeDtypeStruct(*o) if at < final else pltpu.VMEM(*o) for at, o in enumerate(outs)],
        in_specs=[hbm if far else vmem for far in stored] + [pl.BlockSpec(memory_space=pl.ANY)] * len(after),
        out_specs=[hbm if at < final and copied else vmem for at in range(len(outs))],
        scratch_shapes=list(scratch),
        compiler_params=pltpu.CompilerParams(vmem_limit_bytes=VMEM_LIMIT),
        cost_estimate=pl.CostEstimate(flops=cost, bytes_accessed=0, transcendentals=0),
        name=name,
    )(*held, *after)


def swap(value, axis, bit):
    count = lax.axis_size(axis)
    return lax.ppermute(value, axis, [(i, i ^ bit) for i in range(count)])


def stack_kernel(*refs):
    out = refs[-1]
    rows = refs[0].shape[0]
    for at, value in enumerate(refs[:-1]):
        out[at * rows : (at + 1) * rows] = value[...]


def stacked(*values, name, after=()):
    rows, width = values[0].shape
    return call(stack_kernel, [((len(values) * rows, width), values[0].dtype)], *values, name=name, after=after)[0]


def slots_of(bits):
    order = [0]
    for bit in bits:
        order = order + [m | bit for m in order]
    return order


def gathered(value, axis, bits, name, after=()):
    for bit in bits[:-1]:
        value = stacked(value, swap(value, axis, bit), name=name, after=after)
    return value, swap(value, axis, bits[-1])


def pieces_of(refs, count):
    each = count // len(refs)
    rows = refs[0].shape[0] // each
    return [ref.at[pl.ds(at * rows, rows), :] for ref in refs for at in range(each)]


def row_index():
    return lax.axis_index("rows")


def group_index():
    return lax.axis_index("rows") // (lax.axis_size("rows") // OFFSETS)


def piece_index():
    return lax.axis_index("tract") % PIECES


def load_kernel(rows, *refs):
    weight, table, score, bias = refs[:4]
    ids = refs[4:7]
    weight_low, table_low, score_here, bias_here, together = refs[7:12]
    weight_here, table_here, ids_here, sems = refs[12:]
    parts = weight_here.shape[0]
    size = weight_here.shape[1]
    copies = [pltpu.make_async_copy(source, ids_here.at[at], sems.at[at]) for at, source in enumerate(ids)]
    copies.append(pltpu.make_async_copy(table, table_here, sems.at[3]))
    copies.append(pltpu.make_async_copy(score, score_here, sems.at[4]))
    copies.append(pltpu.make_async_copy(bias, bias_here, sems.at[5]))
    copies += [
        pltpu.make_async_copy(weight.at[pl.ds(at * size, size), :], weight_here.at[at], sems.at[6 + at]) for at in range(parts)
    ]
    for copy in copies:
        copy.start()
    for at in range(3):
        copies[at].wait()
        together[at * rows : (at + 1) * rows, :] = ids_here[at].astype(F32)
    copies[3].wait()
    table_low[...] = table_here[...].astype(BF16)
    copies[4].wait()
    copies[5].wait()
    for at in range(parts):
        copies[6 + at].wait()
        weight_low[at * size : (at + 1) * size, :] = weight_here[at].astype(BF16)


def pair_kernel(first, second, out):
    out[:8] = first[:8]
    out[8:] = second[:8]


def kept_kernel(*refs):
    half = len(refs) // 2
    for value, out in zip(refs[:half], refs[half:]):
        out[...] = value[...]


def placed(parts, width):
    total = None
    for part, at in parts:
        shard = part.shape[1]
        source = lax.broadcasted_iota(jnp.int32, (shard, width), 0) + at * shard
        column = lax.broadcasted_iota(jnp.int32, (shard, width), 1)
        row = jnp.broadcast_to(part[...], (8, shard)).astype(BF16)
        got = dot(row, (source == column).astype(BF16))
        total = got if total is None else total + got
    return total


def scorer_kernel(order, near_order, *refs):
    scores = pieces_of(refs[:2], len(order))
    biases = refs[2 : 2 + len(near_order)]
    weight_low, scorer, out = refs[2 + len(near_order) :]
    width = scorer.shape[1]
    full = placed([(part, row_index() ^ m) for part, m in zip(scores, order)], width)
    bias = placed([(part, row_index() ^ m) for part, m in zip(biases, near_order)], width)
    full = jnp.concatenate([full, full], 0).astype(BF16)
    scorer[...] = full
    at = lax.broadcasted_iota(jnp.int32, bias.shape, 0)
    out[...] = jnp.zeros(out.shape, F32)
    out[:8] = jnp.where(at == 0, dot(full, weight_low[...], NT)[:8], bias)


def table_kernel(order, first, second, table_low):
    slots = pieces_of((first, second), len(order))
    rows = slots[0].shape[0]
    for slot, m in zip(slots, order):
        at = pl.multiple_of((row_index() ^ m) * rows, rows)
        table_low[pl.ds(at, rows), :] = slot[...]


def products_kernel(table_low, weight_low, product, table_turned):
    product[...] = dot(table_low[...], weight_low[...]).astype(BF16)
    table_turned[...] = table_low[...].T


def planes_kernel(ids, before, out, hot):
    length = ids.shape[1]
    rows = ids.shape[0] // 3
    half = length // 2
    tail = 128
    ids = ids[...].astype(BF16)
    earlier = before[:, length - tail :].astype(BF16)
    for m in range(SPAN):
        target = 2 * lax.broadcasted_iota(jnp.int32, (length, half), 1) + 1 - m
        source = lax.broadcasted_iota(jnp.int32, (length, half), 0)
        got = dot(ids, (source == target).astype(BF16))
        if m > 1:
            target = 2 * lax.broadcasted_iota(jnp.int32, (tail, half), 1) + 1 - m + tail
            source = lax.broadcasted_iota(jnp.int32, (tail, half), 0)
            got = got + dot(earlier, (source == target).astype(BF16))
        out[:, m * half : (m + 1) * half] = got
    values = hot.shape[0]
    name = names(values, half)
    for side in range(2):
        for row in range(rows):
            code = out[row : row + 1, side * half : (side + 1) * half]
            hot[:, (side * rows + row) * half : (side * rows + row + 1) * half] = one_hot(name, code)
    edge = gathered_edges([out[:rows, (SPAN - 2 + side) * half : (SPAN - 1 + side) * half] for side in range(2)])
    hot[:, 2 * rows * half :] = one_hot(name, edge)


def names(values, lanes):
    shape = (values // 16, 16, lanes)
    return (lax.broadcasted_iota(jnp.int32, shape, 0) * 16 + lax.broadcasted_iota(jnp.int32, shape, 1)).astype(F32).astype(BF16)


def one_hot(name, code):
    code = jnp.broadcast_to(code, name.shape[1:]).astype(BF16)
    return jnp.where(name == code[None], jnp.ones(name.shape, BF16), jnp.zeros(name.shape, BF16)).reshape(-1, name.shape[2])


def gathered_edges(planes):
    rows, lanes = planes[0].shape
    lane = lax.broadcasted_iota(jnp.int32, (rows, lanes), 1)
    row = lax.broadcasted_iota(jnp.int32, (rows, lanes), 0)
    total = jnp.zeros((rows, lanes), F32)
    for side, plane in enumerate(planes):
        for at in range(EDGE):
            place = (side * rows + row) * EDGE + at
            total = total + jnp.where(lane == place, plane[:, at : at + 1], 0.0)
    return jnp.sum(total, 0, keepdims=True)


class Window:
    def __init__(self, mask):
        self.mask = mask
        self.keep, self.divide = [], []
        for side in range(2):
            keep = [self.mask[k, side] for k in range(OFFSETS)]
            counts, total = [], 0.0
            for k in range(OFFSETS):
                total = total + keep[k]
                counts.append(1.0 / jnp.maximum(total, 1.0))
            self.keep.append(keep)
            self.divide.append(counts)

    def pooled(self, side, values):
        means, total = [], 0.0
        for k in range(OFFSETS):
            total = total + self.keep[side][k] * values[side + k]
            means.append(total * self.divide[side][k])
        return means

    def spread(self, sides):
        result = [0.0] * REACH
        for side in range(2):
            carried = 0.0
            for k in reversed(range(OFFSETS)):
                carried = carried + sides[side][k] * self.divide[side][k]
                result[side + k] = result[side + k] + self.keep[side][k] * carried
        return result


def window_of(planes, rows):
    half = planes.shape[1] // SPAN

    def part(which, m):
        return planes[which * rows : (which + 1) * rows, m * half : (m + 1) * half]

    segments = [part(1, m) for m in range(SPAN)]
    valid = [part(2, m) for m in range(SPAN)]
    mask = {
        (k, j): (segments[j + k] == segments[j]).astype(F32) * valid[j + k]
        for k in range(OFFSETS)
        for j in range(REACH)
    }
    return [part(0, m) for m in range(SPAN)], Window(mask)


CODES = 0
WEIGHTS = CODES + SPAN
MASKS = WEIGHTS + OFFSETS * REACH
PROBS = MASKS + OFFSETS * REACH
AVERAGE = PROBS + 2 * OFFSETS
PLANES = AVERAGE + 1


def lookup(row, codes):
    index = codes.astype(jnp.int32)
    lanes = 128
    low = jnp.bitwise_and(index, lanes - 1)
    parts = [
        jnp.take_along_axis(
            jnp.broadcast_to(row[:, at : at + lanes], codes.shape), low, axis=1
        )
        for at in range(0, row.shape[1], lanes)
    ]
    return jnp.where(index >= lanes, parts[1], parts[0])


def packed_row(ref, plane, row):
    return jnp.broadcast_to(ref[plane, pl.ds(row, 1), :], (16, ref.shape[2])).astype(BF16)


def spread_rows(plan, k, row, values):
    lanes = plan.shape[2]
    blocks = values // 16
    name = names(values, lanes)
    total = jnp.zeros((blocks, 16, lanes), BF16)
    for j in range(REACH):
        code = packed_row(plan, CODES + k + j, row)
        weight = packed_row(plan, WEIGHTS + k * REACH + j, row)
        total = jnp.where(name == code[None], total + weight[None], total)
    return total.reshape(values, lanes)


def accumulate(plan, total_ref, ks, cot, values, extra=None):
    rows, half = plan.shape[1:]
    for chunk in range(rows // 2):
        pieces = [
            jnp.concatenate(
                [
                    spread_rows(plan, k, 2 * chunk, values),
                    spread_rows(plan, k, 2 * chunk + 1, values),
                ],
                1,
            )
            for k in ks
        ]
        if extra is not None:
            pieces.append(extra(chunk))
        left = jnp.concatenate(pieces, 0)
        part = dot(left, cot[2 * chunk * half : 2 * (chunk + 1) * half, :])
        if chunk == 0:
            total_ref[...] = part
        else:
            total_ref[...] += part


def split(value):
    high = value.astype(BF16)
    return high, (value - high.astype(F32)).astype(BF16)


def thirds(value):
    high = value.astype(BF16)
    rest = value - high.astype(F32)
    middle = rest.astype(BF16)
    return high, middle, (rest - middle.astype(F32)).astype(BF16)


def far_kernel(order, slot, values, *refs):
    scorers = pieces_of(refs[:2], len(order))
    table_low, planes, scorer, cot = refs[2:6]
    sent_first, sent_second, plan, vectors, table, total = refs[6:]
    rows = plan.shape[1]
    every = jnp.concatenate([s[:8] for s in scorers], 0)
    parts = thirds(every)
    found = dot(jnp.concatenate(parts, 0), table_low[...], NT)
    count = every.shape[0]
    found = found[:count] + found[count : 2 * count] + found[2 * count :]
    for at, m in enumerate(order):
        table[group_index() ^ m] = found[at * 8 : (at + 1) * 8]
    codes, window = window_of(planes[...], rows)
    bias = functools.reduce(jnp.add, [s[1:2] for s in scorers])
    both = [scorer[:8].astype(F32), jnp.broadcast_to(bias, (8, bias.shape[1]))]
    vectors[...] = jnp.concatenate(both, 0).astype(BF16)
    shared = jnp.sum(both[0] * both[1], 1, keepdims=True)[:1]
    conv_scores = [shared] * REACH
    for k in range(OFFSETS):
        row = table[k, :1, :]
        for m in range(k, k + REACH):
            conv_scores[m - k] = conv_scores[m - k] + window.mask[k, m - k] * lookup(row, codes[m])
    for m in range(SPAN):
        plan[CODES + m] = codes[m]
    shares = []
    for side in range(2):
        block = window.pooled(side, conv_scores)
        top = functools.reduce(jnp.maximum, block)
        exps = [jnp.exp(b - top) for b in block]
        inverse = 1.0 / functools.reduce(jnp.add, exps)
        shares.append([e * inverse for e in exps])
        for k in range(OFFSETS):
            plan[PROBS + side * OFFSETS + k] = shares[side][k]
    mixing = [0.5 * e for e in window.spread(shares)]
    plan[AVERAGE] = functools.reduce(jnp.add, mixing)
    for k in range(OFFSETS):
        for j in range(REACH):
            plan[MASKS + k * REACH + j] = window.mask[k, j]
            plan[WEIGHTS + k * REACH + j] = window.mask[k, j] * mixing[j]
    accumulate(plan, total, [group_index() ^ slot], cot, values)
    for at, sent in enumerate((sent_first, sent_second)):
        sent[...] = total[at * values // 2 : (at + 1) * values // 2].astype(BF16)


def block_kernel(slot, values, plan, cot, out):
    accumulate(plan, out, [group_index() ^ slot], cot, values)


def average_line(plan, chunk):
    return jnp.concatenate([plan[AVERAGE, row : row + 1, :] for row in (2 * chunk, 2 * chunk + 1)], 1)


def near_kernel(slots, values, plan, cot, own, sent, bias_out, total):
    half = plan.shape[2]

    def extra(chunk):
        line = jnp.broadcast_to(average_line(plan, chunk), (EXTRA, 2 * half))
        high, low = split(line)
        at = lax.broadcasted_iota(jnp.int32, line.shape, 0)
        return jnp.where(at == 0, high.astype(F32), jnp.where(at == 1, low.astype(F32), 0.0)).astype(BF16)

    accumulate(plan, total, [group_index() ^ m for m in slots], cot, values, extra)
    own[...] = total[:values]
    sent[...] = total[values : 2 * values].astype(BF16)
    end = total[len(slots) * values :]
    bias_out[...] = jnp.broadcast_to(end[:1] + end[1:2], (8, end.shape[1]))


def inner_kernel(order, values, *refs):
    products = pieces_of(refs[:1], len(order))
    plan, vectors, cot = refs[1:4]
    before, out = (refs[-2] if len(refs) > 5 else None), refs[-1]
    rows, half = plan.shape[1:]
    blocks = values // 16
    name = names(values, half)
    for chunk in range(rows // 2):
        here = cot[2 * chunk * half : 2 * (chunk + 1) * half, :]
        base = dot(vectors[8:], here, NT) if before is None else None
        found = {}
        for slot, m in zip(products, order):
            k = group_index() ^ m
            each = dot(slot[...], here, NT).astype(BF16)
            for side in range(2):
                row = 2 * chunk + side
                mine = each[:, side * half : (side + 1) * half].reshape(blocks, 16, half)
                for j in range(REACH):
                    code = packed_row(plan, CODES + k + j, row)
                    picked = jnp.zeros((16, half), BF16)
                    for at in range(blocks):
                        picked = jnp.where(name[at] == code, mine[at], picked)
                    mask = plan[MASKS + k * REACH + j, row : row + 1, :]
                    found[j, side] = found.get((j, side), 0.0) + picked.astype(F32) * mask
        for side in range(2):
            row = 2 * chunk + side
            for j in range(REACH):
                if before is None:
                    start = base[:1, side * half : (side + 1) * half]
                else:
                    start = before[j, row : row + 1, :]
                out[j, row : row + 1, :] = jnp.sum(found[j, side], 0, keepdims=True) + start


def score_kernel(order, values, *refs):
    products = pieces_of(refs[:2], len(order))
    inner_ref, plan, vectors, hot = refs[2:6]
    out, flat, rows_ref = refs[6:]
    rows, half = plan.shape[1:]
    biases = vectors[8:]
    window = Window({(k, j): plan[MASKS + k * REACH + j] for k in range(OFFSETS) for j in range(REACH)})
    inner_rows = [0.5 * inner_ref[j] for j in range(REACH)]
    sides = []
    for side in range(2):
        inner = window.pooled(side, inner_rows)
        share = [plan[PROBS + side * OFFSETS + k] for k in range(OFFSETS)]
        mean = functools.reduce(jnp.add, [s * i for s, i in zip(share, inner)])
        sides.append([s * (i - mean) for s, i in zip(share, inner)])
    grads = window.spread(sides)
    overall = jnp.sum(jnp.sum(functools.reduce(jnp.add, grads), 1, keepdims=True), 0, keepdims=True)
    lane = lax.broadcasted_iota(jnp.int32, (rows, half), 1)
    flat[...] = jnp.zeros(flat.shape, F32)
    for k in range(OFFSETS):
        edges = []
        for side in range(2):
            inside = jnp.zeros((rows, half), F32)
            edge = jnp.zeros((rows, half), F32)
            for m in range(side, SPAN, 2):
                if not 0 <= m - k < REACH:
                    continue
                value = grads[m - k] * window.mask[k, m - k]
                steps = m // 2
                if steps:
                    inside = inside + jnp.where(lane < half - steps, pltpu.roll(value, half - steps, 1), 0.0)
                    moved = pltpu.roll(value, EDGE - steps, 1) if steps < EDGE else value
                    edge = edge + jnp.where((lane >= EDGE - steps) & (lane < EDGE), moved, 0.0)
                else:
                    inside = inside + value
            for row in range(rows):
                at = (side * rows + row) * half
                flat[k : k + 1, at : at + half] = inside[row : row + 1, :]
            edges.append(edge)
        flat[k : k + 1, 2 * rows * half :] = gathered_edges(edges)
    high, low = split(flat[...])
    both = jnp.concatenate([high.astype(F32), low.astype(F32)], 0).astype(BF16)
    lines = dot(both, hot[...], NT)
    lines = lines[:8] + lines[8:]
    for k in range(OFFSETS):
        rows_ref[k] = jnp.broadcast_to(lines[k : k + 1], (8, values))
    width = biases.shape[1]
    score_grad = jnp.zeros((1, width), F32)
    for slot, m in zip(products, order):
        got = dot(pack(rows_ref[group_index() ^ m]), slot[...])
        score_grad = score_grad + got[:1] + got[8:9]
    out[...] = jnp.zeros(out.shape, F32)
    out[:1] = score_grad + overall * biases[:1].astype(F32)
    out[1:2] = overall * vectors[:1].astype(F32)
    for k in range(OFFSETS):
        out[2 + k : 3 + k, :values] = lines[k : k + 1]


def output_kernel(order, values, chunks_here, *refs):
    products = pieces_of(refs[:2], len(order))
    plan, vectors = refs[2:4]
    out, token, staged, sems = refs[-4:]
    token[...] = jnp.zeros(token.shape, F32)
    half = plan.shape[2]
    step = 2 * half
    biases = vectors[8:].astype(F32)
    at = lax.broadcasted_iota(jnp.int32, (8, step), 0)
    first = lax.broadcasted_iota(jnp.int32, biases.shape, 0)
    biases = jnp.where(first < 2, biases, 0.0)
    copies = []
    for place, chunk in enumerate(chunks_here):
        high, low = split(jnp.broadcast_to(average_line(plan, chunk), (8, step)))
        both = jnp.where(at == 0, high.astype(F32), jnp.where(at == 1, low.astype(F32), 0.0))
        total = dot(both, biases, TN)
        for slot, m in zip(products, order):
            k = group_index() ^ m
            left = jnp.concatenate([spread_rows(plan, k, row, values) for row in (2 * chunk, 2 * chunk + 1)], 1)
            total = total + dot(left, slot[...], TN)
        staged[place * step : (place + 1) * step, :] = total.astype(BF16)
        copies.append(
            pltpu.make_async_copy(
                staged.at[pl.ds(place * step, step), :], out.at[pl.ds(chunk * step, step), :], sems.at[place]
            )
        )
        copies[-1].start()
    for copy in copies:
        copy.wait()


def output_part(before, part, parts, order, values, products, plan, vectors, after):
    rows, half = plan.shape[1:]
    width = vectors.shape[1]
    each = rows // 2 // parts
    operands = [pltpu.with_memory_space_constraint(x, pltpu.VMEM) for x in (*products, plan, vectors)]
    operands += [] if before is None else [pltpu.with_memory_space_constraint(before, pltpu.HBM)]
    vmem = pl.BlockSpec(memory_space=pltpu.VMEM)
    elsewhere = pl.BlockSpec(memory_space=pl.ANY)
    count = len(products) + 2
    chunks_here = range(part * each, (part + 1) * each)

    def run(*refs):
        output_kernel(order, values, chunks_here, *refs[:count], *refs[-4:])

    return pl.pallas_call(
        run,
        out_shape=[jax.ShapeDtypeStruct((rows * half, width), BF16), pltpu.VMEM((8, 128), F32)],
        in_specs=[vmem] * count + [elsewhere] * (len(operands) - count + len(after)),
        out_specs=[elsewhere, vmem],
        input_output_aliases={} if before is None else {count: 0},
        scratch_shapes=[pltpu.VMEM((2 * half * each, width), BF16), pltpu.SemaphoreType.DMA((each,))],
        compiler_params=pltpu.CompilerParams(vmem_limit_bytes=VMEM_LIMIT),
        cost_estimate=pl.CostEstimate(flops=0, bytes_accessed=0, transcendentals=0),
        name="output",
    )(*operands, *after)


def chunks(values, piece, group):
    block = values // OFFSETS
    size = block // PIECES
    for actual in range(PIECES):
        for offset in range(OFFSETS):
            at = pl.multiple_of((piece ^ actual) * OFFSETS * size + (group ^ offset) * size, size)
            yield offset * block + actual * size, at, size


def pack(rows):
    high, low = split(rows)
    return jnp.concatenate([high.astype(F32), low.astype(F32)], 0).astype(BF16)


def unpack(block):
    return block[:8].astype(F32) + block[8:].astype(F32)


def merge_kernel(near, near_other, far_other, sums, bias, keep, *refs):
    sends, total = refs[:-1], refs[-1]
    values = near.shape[0]
    summed = near[...] + near_other[...].astype(F32) + far_other[...].astype(F32)
    for source, at, size in chunks(values, piece_index(), group_index()):
        total[pl.ds(at, size), :] = summed[source : source + size]
    part = keep.shape[0]
    second = lax.broadcasted_iota(jnp.int32, bias.shape, 0) == 1
    small = pack(sums[...] + jnp.where(second, bias[...], 0.0))
    keep[...] = total[:part]
    for at, send in enumerate(sends):
        send[:part] = total[(at + 1) * part : (at + 2) * part].astype(BF16)
        send[part:] = small


def slice_kernel(keep, own, *refs):
    others, send = refs[:-1], refs[-1]
    part = keep.shape[0]
    total = functools.reduce(jnp.add, [keep[...]] + [o[:part].astype(F32) for o in others])
    small = [unpack(x[part:]) for x in (own, *others)]
    while len(small) > 1:
        small = [small[at] + small[at + 1] for at in range(0, len(small), 2)]
    send[:part] = total.astype(BF16)
    send[part:] = pack(small[0])


def whole_kernel(mine, other, send):
    rows = mine.shape[0] - EXTRA
    send[:rows] = (mine[:rows].astype(F32) + other[:rows].astype(F32)).astype(BF16)
    send[rows:] = pack(unpack(mine[rows:]) + unpack(other[rows:]))


def last_kernel(mine, other, block, sums):
    rows = block.shape[0]
    block[...] = (mine[:rows].astype(F32) + other[:rows].astype(F32)).astype(BF16)
    sums[...] = unpack(mine[rows:]) + unpack(other[rows:])


def share_kernel(block, sums, weight_low, keep, send):
    product = dot(block[...], weight_low[...], NT)
    rows = keep.shape[0]
    keep[...] = product[:rows]
    send[:rows] = product[rows:].astype(BF16)
    send[rows:] = pack(sums[...])


def half_kernel(keep, sums, other, rest, send, total):
    rows = rest.shape[0]
    both = keep[...] + other[: 2 * rows].astype(F32)
    total[...] = sums[...] + unpack(other[2 * rows :])
    rest[...] = both[:rows]
    send[:rows] = both[rows:].astype(BF16)
    send[rows:] = pack(total[...])


def combine_kernel(keep, sums, other, out, total):
    rows = keep.shape[0]
    out[...] = (keep[...] + other[:rows].astype(F32)).astype(BF16)
    total[...] = sums[...] + unpack(other[rows:])


def added_kernel(mine, other, out):
    out[...] = (mine[...].astype(F32) + other[...].astype(F32)).astype(out.dtype)


def joined_kernel(mine, one, two, out):
    rows = one.shape[0]
    out[:rows] = (mine[:rows] + one[...].astype(F32)).astype(out.dtype)
    out[rows:] = (mine[rows:] + two[...].astype(F32)).astype(out.dtype)


def weight_kernel(order, *refs):
    slots = refs[: len(order)]
    turned, vectors, sums, out, token, full, staged, sems = refs[len(order) :]
    token[...] = jnp.zeros(token.shape, F32)
    values = full.shape[0]
    placed = {m: slot for m, slot in zip(order, slots)}
    size = values // OFFSETS // PIECES
    for m in range(PIECES):
        for offset in range(OFFSETS):
            at = (group_index() ^ offset) * (values // OFFSETS) + (piece_index() ^ m) * size
            full[pl.ds(pl.multiple_of(at, size), size), :] = placed[m][offset * size : (offset + 1) * size]
    line = sums[pl.ds(group_index() + 2, 1), :values]
    scores = jnp.concatenate([vectors[:8], vectors[:8]], 0)
    first = lax.broadcasted_iota(jnp.int32, (8, values), 0) == 0
    both = pack(jnp.where(first, jnp.broadcast_to(line, first.shape), 0.0))
    parts = sems.shape[0]
    step = turned.shape[0] // parts
    copies = []
    for part in range(parts):
        here = turned[part * step : (part + 1) * step]
        high, low = split(dot(here, both, NT))
        staged[part] = dot(here, full[...]) + dot(high, scores) + dot(low, scores)
        copies.append(pltpu.make_async_copy(staged.at[part], out.at[pl.ds(part * step, step), :], sems.at[part]))
        copies[-1].start()
    for copy in copies:
        copy.wait()


def table_grad_kernel(order, offsets, *refs):
    slots = refs[: len(order)]
    scorers = pieces_of(refs[len(order) : len(order) + 2], len(offsets))
    sums, out, score_out, bias_out, table, full, rows_ref = refs[len(order) + 2 :]
    values = full.shape[0]
    width = out.shape[1]
    high, low = split(sums[2 : 2 + OFFSETS, :values])
    for scorer, m in zip(scorers, offsets):
        rows_ref[group_index() ^ m] = scorer[:8]
    right = jnp.concatenate([rows_ref[k, :1] for k in range(OFFSETS)], 0)
    right_high, right_low = split(right)
    left = jnp.concatenate([x.astype(F32) for x in (high, low, high, low)], 0).astype(BF16)
    right = jnp.concatenate([x.astype(F32) for x in (right_high, right_high, right_low, right_low)], 0).astype(BF16)
    full[...] = dot(left, right, TN)
    for slot, m in zip(slots, order):
        size = slot.shape[0]
        table[pl.ds(pl.multiple_of((piece_index() ^ m) * size, size), size), :] = slot[...].astype(F32)
    rows = out.shape[0]
    at = pl.multiple_of(row_index() * rows, rows)
    inside = row_index() * rows - group_index() * table.shape[0]
    out[...] = table[pl.ds(pl.multiple_of(inside, rows), rows), :] + full[pl.ds(at, rows), :]
    shard = score_out.shape[1]
    source = lax.broadcasted_iota(jnp.int32, (width, shard), 0)
    column = lax.broadcasted_iota(jnp.int32, (width, shard), 1) + row_index() * shard
    here = (source == column).astype(BF16)
    ends = functools.reduce(jnp.add, [dot(part, here) for part in thirds(sums[...])])
    score_out[...] = ends[:1]
    bias_out[...] = ends[1:2]


def bits_of(count):
    return [1 << at for at in reversed(range(count.bit_length() - 1))]


def body(byte_values, segment_ids, valid, table, conv_weight, conv_bias, score_weight, cotangent):
    rows_count, tract_count = lax.axis_size("rows"), lax.axis_size("tract")
    rows_at = lax.axis_index("rows")
    values, width = table.shape[0] * rows_count, table.shape[1]
    rows, length = byte_values.shape
    half = length // 2
    copies = rows_count // OFFSETS
    order = [0, 2, 1, 3]
    group_bits = [2 * copies, copies]
    near_bits = [bit for bit in bits_of(rows_count) if bit < copies]

    row_bits = bits_of(rows_count)
    far_score = swap(score_weight[None], "rows", row_bits[0])
    near_order = slots_of(near_bits)
    biases = [conv_bias[None]]
    for bit in near_bits:
        biases = biases + [swap(value, "rows", bit) for value in biases]
    weight = conv_weight
    if copies > 1:
        near_by = [[g * copies + c for c in range(copies)] for g in range(OFFSETS)]
        weight = lax.all_gather(conv_weight, "rows", axis=0, tiled=True, axis_index_groups=near_by)
    parts = 4
    shard = (1, conv_bias.shape[0])
    weight_low, table_low, score, biases[0], ids = call(
        functools.partial(load_kernel, rows),
        [(weight.shape, BF16), (table.shape, BF16), (shard, F32), (shard, F32), ((3 * rows, length), F32)],
        (weight,), (table,), (score_weight[None],), (conv_bias[None],), (byte_values,), (segment_ids,), (valid,),
        scratch=[pltpu.VMEM((parts, weight.shape[0] // parts, width), F32), pltpu.VMEM(table.shape, F32),
                 pltpu.VMEM((3, rows, length), jnp.int32), pltpu.SemaphoreType.DMA((6 + parts,))],
        name="load",
    )
    scores = gathered(stacked(score, far_score, name="score"), "rows", row_bits[1:], "score")
    scorer, scored = call(
        functools.partial(scorer_kernel, slots_of(row_bits), near_order),
        [((EXTRA, width), BF16), ((SENT, width), F32)], *scores, *biases, weight_low, name="scorer",
    )
    far_scored = swap(scored, "rows", group_bits[0])
    table_low = stacked(table_low, name="table_low", after=[far_score])
    far_table = swap(table_low, "rows", row_bits[0])
    table_low = stacked(table_low, far_table, name="table_pair", after=[scored])
    table_low = call(
        functools.partial(table_kernel, slots_of(row_bits)), [((values, width), BF16)],
        *gathered(table_low, "rows", row_bits[1:], "table_pair"), name="table",
    )[0]
    product, turned = call(
        products_kernel, [((values, width), BF16), ((width, values), BF16)], table_low, weight_low, name="products", after=[],
    )
    tail = stacked(ids, name="tail", after=[product])
    before = lax.ppermute(tail, "tract", [(i, i + 1) for i in range(tract_count - 1)])
    planes, hot = call(
        planes_kernel, [((3 * rows, SPAN * half), F32), ((values, 2 * rows * half + 128), BF16)], ids, before, name="planes",
    )
    scorers = call(pair_kernel, [((16, width), F32)], scored, far_scored, name="scored")[0]
    scorers = scorers, swap(scorers, "rows", group_bits[1])

    cot = cotangent.reshape(rows * half, width)
    *far_sent, plan, vectors = call(
        functools.partial(far_kernel, order, 3, values),
        [((values // 2, width), BF16), ((values // 2, width), BF16), ((PLANES, rows, half), F32), ((EXTRA, width), BF16)],
        *scorers, table_low, planes, scorer, cot,
        scratch=[pltpu.VMEM((OFFSETS, 8, values), F32), pltpu.VMEM((values, width), F32)], name="far",
    )
    far = call(functools.partial(block_kernel, 2, values), [((values, width), F32)], plan, cot, name="far_own")[0]
    far_sent = [swap(half_sent, "rows", copies) for half_sent in far_sent]
    far = call(joined_kernel, [((values, width), BF16)], far, *far_sent, name="far_sum")[0]
    far_other = swap(far, "rows", 2 * copies)
    near, near_sent, bias_part = call(
        functools.partial(near_kernel, [0, 1], values),
        [((values, width), F32), ((values, width), BF16), ((8, width), F32)], plan, cot,
        scratch=[pltpu.VMEM((2 * values + EXTRA, width), F32)], name="near", after=[far],
    )
    near_other = swap(near_sent, "rows", copies)

    far_product = swap(product, "rows", 2 * copies)
    product = stacked(product, far_product, name="passed", after=[near_sent])
    products = product, swap(product, "rows", copies)
    inner = call(
        functools.partial(inner_kernel, [0, 2], values), [((REACH, rows, half), F32)],
        products[0], plan, vectors, cot, name="inner_near", cost=LONG,
    )[0]
    inner = call(
        functools.partial(inner_kernel, [1, 3], values), [((REACH, rows, half), F32)],
        products[1], plan, vectors, cot, inner, name="inner_far",
    )[0]
    sums = call(
        functools.partial(score_kernel, order, values), [((8, width), F32)], *products, inner, plan, vectors, hot,
        scratch=[pltpu.VMEM((8, hot.shape[1]), F32), pltpu.VMEM((OFFSETS, 8, values), F32)], name="scores",
    )[0]

    rest = [("tract", 1 << at) for at in range(PIECES.bit_length() - 1, tract_count.bit_length() - 1)]
    rest += [("rows", 1 << at) for at in range(copies.bit_length() - 1)]
    size = values // PIECES
    keep, *sends = call(
        merge_kernel, [((size, width), F32)] + [((size + EXTRA, width), BF16)] * (PIECES - 1),
        near, near_other, far_other, sums, bias_part, scratch=[pltpu.VMEM((values, width), F32)], name="merge",
    )
    others = [swap(send, "tract", at + 1) for at, send in enumerate(sends)]
    parts = 2

    def fill(out, which, after):
        for part in which:
            out, token = output_part(out, part, parts, order, values, products, plan, vectors, [after])
        return out, token

    out, token = fill(None, [0], keep)
    send = call(slice_kernel, [((size + EXTRA, width), BF16)], keep, sends[0], *others, name="slice", after=[token])[0]
    out, token = fill(out, [1], send)
    for axis, bit in rest[:-1]:
        other = swap(send, axis, bit)
        send = call(whole_kernel, [(send.shape, BF16)], send, other, name="whole")[0]
    other = swap(send, *rest[-1])
    block, sums = call(last_kernel, [((size, width), BF16), ((8, width), F32)], send, other, name="last", after=[token])

    part = size // OFFSETS
    keep, send = call(
        share_kernel, [((2 * part, width), F32), ((2 * part + EXTRA, width), BF16)], block, sums, weight_low, name="share",
    )
    other = swap(send, "rows", group_bits[0])
    blocks = {0: block} | {m: swap(block, "tract", m) for m in range(1, PIECES)}
    keep, send, sums = call(
        half_kernel, [((part, width), F32), ((part + EXTRA, width), BF16), ((8, width), F32)], keep, sums, other, name="half",
    )
    other = swap(send, "rows", group_bits[1])
    table_piece, sums = call(combine_kernel, [((part, width), BF16), ((8, width), F32)], keep, sums, other, name="combine")
    table_pieces = {0: table_piece} | {m: swap(table_piece, "tract", m) for m in range(1, PIECES)}
    if copies > 1:
        turned = lax.dynamic_slice_in_dim(turned, rows_at % copies * (width // copies), width // copies, 0)
    weight_rows = conv_weight.shape[0]
    steps = 3
    weight_grad, token = call(
        functools.partial(weight_kernel, list(blocks)), [((weight_rows, width), F32), ((8, 128), F32)],
        *blocks.values(), turned, vectors, sums,
        scratch=[pltpu.VMEM((values, width), BF16), pltpu.VMEM((steps, weight_rows // steps, width), F32),
                 pltpu.SemaphoreType.DMA((steps,))], name="weights", final=1, copied=True,
    )
    table_grad, score_grad, bias_grad = call(
        functools.partial(table_grad_kernel, list(table_pieces), order),
        [(table.shape, F32), (shard, F32), (shard, F32)], *table_pieces.values(), *scorers, sums,
        scratch=[pltpu.VMEM((values // OFFSETS, width), F32), pltpu.VMEM((values, width), F32), pltpu.VMEM((OFFSETS, 8, width), F32)],
        name="table_grad", final=3, after=[token],
    )
    return out.reshape(cotangent.shape), table_grad, weight_grad, bias_grad[0], score_grad[0]


def solution(mesh):
    return jax.shard_map(
        body,
        mesh=mesh,
        in_specs=(
            P("rows", "tract"), P("rows", "tract"), P("rows", "tract"), P("rows", None),
            P("rows", None), P("rows"), P("rows"), P("rows", "tract", None),
        ),
        out_specs=(P("rows", "tract", None), P("rows", None), P("rows", None), P("rows"), P("rows")),
        check_vma=False,
    )
```

```python
import functools

import jax
import jax.numpy as jnp
from jax import lax
from jax.experimental import pallas as pl
from jax.experimental.pallas import tpu as pltpu
from jax.sharding import PartitionSpec as P

F32 = jnp.float32
BF16 = jnp.bfloat16
OFFSETS = 4
REACH = 5
SPAN = 8
EXTRA = 16
PIECES = 4
EDGE = 3
VMEM_LIMIT = 16 * 1024 * 1024
SENT = 48
LONG = 10**11
NT = (((1,), (1,)), ((), ()))
TN = (((0,), (0,)), ((), ()))
NN = (((1,), (0,)), ((), ()))


def dot(a, b, dims=NN, precision=None):
    return lax.dot_general(a, b, dims, precision=precision, preferred_element_type=F32)


def exact(a, b, dims=NN):
    return dot(a, b, dims, lax.Precision.HIGHEST)


def call(kernel, outs, *operands, scratch=(), cost=0, name=None, after=(), final=0, copied=False):
    vmem = pl.BlockSpec(memory_space=pltpu.VMEM)
    hbm = pl.BlockSpec(memory_space=pltpu.HBM)
    stored = [isinstance(operand, tuple) for operand in operands]
    held = [
        pltpu.with_memory_space_constraint(operand[0] if far else operand, pltpu.HBM if far else pltpu.VMEM)
        for operand, far in zip(operands, stored)
    ]
    count = len(operands)

    def run(*refs):
        kernel(*refs[:count], *refs[count + len(after) :])

    return pl.pallas_call(
        run if after else kernel,
        out_shape=[jax.ShapeDtypeStruct(*o) if at < final else pltpu.VMEM(*o) for at, o in enumerate(outs)],
        in_specs=[hbm if far else vmem for far in stored] + [pl.BlockSpec(memory_space=pl.ANY)] * len(after),
        out_specs=[hbm if at < final and copied else vmem for at in range(len(outs))],
        scratch_shapes=list(scratch),
        compiler_params=pltpu.CompilerParams(vmem_limit_bytes=VMEM_LIMIT),
        cost_estimate=pl.CostEstimate(flops=cost, bytes_accessed=0, transcendentals=0),
        name=name,
    )(*held, *after)


def swap(value, axis, bit):
    count = lax.axis_size(axis)
    return lax.ppermute(value, axis, [(i, i ^ bit) for i in range(count)])


def stack_kernel(*refs):
    out = refs[-1]
    rows = refs[0].shape[0]
    for at, value in enumerate(refs[:-1]):
        out[at * rows : (at + 1) * rows] = value[...]


def stacked(*values, name, after=()):
    rows, width = values[0].shape
    return call(stack_kernel, [((len(values) * rows, width), values[0].dtype)], *values, name=name, after=after)[0]


def slots_of(bits):
    order = [0]
    for bit in bits:
        order = order + [m | bit for m in order]
    return order


def gathered(value, axis, bits, name, after=()):
    for bit in bits[:-1]:
        value = stacked(value, swap(value, axis, bit), name=name, after=after)
    return value, swap(value, axis, bits[-1])


def pieces_of(refs, count):
    each = count // len(refs)
    rows = refs[0].shape[0] // each
    return [ref.at[pl.ds(at * rows, rows), :] for ref in refs for at in range(each)]


def row_index():
    return lax.axis_index("rows")


def group_index():
    return lax.axis_index("rows") // (lax.axis_size("rows") // OFFSETS)


def piece_index():
    return lax.axis_index("tract") % PIECES


def load_kernel(rows, *refs):
    sources = refs[:6]
    table_low, score_here, bias_here, together, table_here, ids_here, sems = refs[6:]
    targets = [table_here, score_here, bias_here] + [ids_here.at[at] for at in range(3)]
    copies = [pltpu.make_async_copy(source, target, sems.at[at]) for at, (source, target) in enumerate(zip(sources, targets))]
    for copy in copies:
        copy.start()
    for copy in copies:
        copy.wait()
    table_low[...] = table_here[...].astype(BF16)
    for at in range(3):
        together[at * rows : (at + 1) * rows, :] = ids_here[at].astype(F32)


def weight_low_kernel(weight, out, here, sems):
    parts, size = here.shape[:2]
    copies = [
        pltpu.make_async_copy(weight.at[pl.ds(at * size, size), :], here.at[at], sems.at[at]) for at in range(parts)
    ]
    for copy in copies:
        copy.start()
    for at in range(parts):
        copies[at].wait()
        out[at * size : (at + 1) * size, :] = here[at].astype(BF16)


def pair_kernel(first, second, out):
    out[:8] = first[:8]
    out[8:] = second[:8]


def kept_kernel(*refs):
    half = len(refs) // 2
    for value, out in zip(refs[:half], refs[half:]):
        out[...] = value[...]


def placed(parts, width):
    total = None
    for part, at in parts:
        shard = part.shape[1]
        source = lax.broadcasted_iota(jnp.int32, (shard, width), 0) + at * shard
        column = lax.broadcasted_iota(jnp.int32, (shard, width), 1)
        row = jnp.broadcast_to(part[...], (8, shard)).astype(BF16)
        got = dot(row, (source == column).astype(BF16))
        total = got if total is None else total + got
    return total


def scorer_kernel(order, near_order, *refs):
    scores = pieces_of(refs[:2], len(order))
    biases = refs[2 : 2 + len(near_order)]
    weight_low, scorer, out = refs[2 + len(near_order) :]
    width = scorer.shape[1]
    full = placed([(part, row_index() ^ m) for part, m in zip(scores, order)], width)
    bias = placed([(part, row_index() ^ m) for part, m in zip(biases, near_order)], width)
    full = jnp.concatenate([full, full], 0).astype(BF16)
    scorer[...] = full
    at = lax.broadcasted_iota(jnp.int32, bias.shape, 0)
    out[...] = jnp.zeros(out.shape, F32)
    out[:8] = jnp.where(at == 0, dot(full, weight_low[...], NT)[:8], bias)


def table_kernel(order, first, second, table_low):
    slots = pieces_of((first, second), len(order))
    rows = slots[0].shape[0]
    for slot, m in zip(slots, order):
        at = pl.multiple_of((row_index() ^ m) * rows, rows)
        table_low[pl.ds(at, rows), :] = slot[...]


def products_kernel(table_low, weight_low, product, table_turned):
    product[...] = dot(table_low[...], weight_low[...]).astype(BF16)
    table_turned[...] = table_low[...].T


def planes_kernel(ids, out, hot):
    length = ids.shape[1]
    rows = ids.shape[0] // 3
    half = length // 2
    own = ids[...].astype(BF16)
    for m in range(SPAN):
        target = 2 * lax.broadcasted_iota(jnp.int32, (length, half), 1) + 1 - m
        source = lax.broadcasted_iota(jnp.int32, (length, half), 0)
        out[:, m * half : (m + 1) * half] = dot(own, (source == target).astype(BF16))
    name = names(hot.shape[0], half)
    for side in range(2):
        for row in range(rows):
            code = out[row : row + 1, side * half : (side + 1) * half]
            hot[:, (side * rows + row) * half : (side * rows + row + 1) * half] = one_hot(name, code)


def halo_kernel(planes, before, out):
    tail = 128
    earlier = before[:, before.shape[1] - tail :].astype(BF16)
    half = planes.shape[1] // SPAN
    for m in range(SPAN):
        part = planes[:, m * half : (m + 1) * half]
        if m > 1:
            target = 2 * lax.broadcasted_iota(jnp.int32, (tail, half), 1) + 1 - m + tail
            source = lax.broadcasted_iota(jnp.int32, (tail, half), 0)
            part = part + dot(earlier, (source == target).astype(BF16))
        out[:, m * half : (m + 1) * half] = part


def names(values, lanes):
    shape = (values // 16, 16, lanes)
    return (lax.broadcasted_iota(jnp.int32, shape, 0) * 16 + lax.broadcasted_iota(jnp.int32, shape, 1)).astype(F32).astype(BF16)


def one_hot(name, code):
    code = jnp.broadcast_to(code, name.shape[1:]).astype(BF16)
    return jnp.where(name == code[None], jnp.ones(name.shape, BF16), jnp.zeros(name.shape, BF16)).reshape(-1, name.shape[2])


def gathered_edges(planes):
    rows, lanes = planes[0].shape
    lane = lax.broadcasted_iota(jnp.int32, (rows, lanes), 1)
    row = lax.broadcasted_iota(jnp.int32, (rows, lanes), 0)
    total = jnp.zeros((rows, lanes), F32)
    for side, plane in enumerate(planes):
        for at in range(EDGE):
            place = (side * rows + row) * EDGE + at
            total = total + jnp.where(lane == place, plane[:, at : at + 1], 0.0)
    return jnp.sum(total, 0, keepdims=True)


class Window:
    def __init__(self, mask):
        self.mask = mask
        self.keep, self.divide = [], []
        for side in range(2):
            keep = [self.mask[k, side] for k in range(OFFSETS)]
            counts, total = [], 0.0
            for k in range(OFFSETS):
                total = total + keep[k]
                counts.append(1.0 / jnp.maximum(total, 1.0))
            self.keep.append(keep)
            self.divide.append(counts)

    def pooled(self, side, values):
        means, total = [], 0.0
        for k in range(OFFSETS):
            total = total + self.keep[side][k] * values[side + k]
            means.append(total * self.divide[side][k])
        return means

    def spread(self, sides):
        result = [0.0] * REACH
        for side in range(2):
            carried = 0.0
            for k in reversed(range(OFFSETS)):
                carried = carried + sides[side][k] * self.divide[side][k]
                result[side + k] = result[side + k] + self.keep[side][k] * carried
        return result


def window_of(planes, rows):
    segments = [plane[rows : 2 * rows] for plane in planes]
    valid = [plane[2 * rows :] for plane in planes]
    mask = {
        (k, j): (segments[j + k] == segments[j]).astype(F32) * valid[j + k]
        for k in range(OFFSETS)
        for j in range(REACH)
    }
    return [plane[:rows] for plane in planes], Window(mask)


CODES = 0
WEIGHTS = CODES + SPAN
MASKS = WEIGHTS + OFFSETS * REACH
PROBS = MASKS + OFFSETS * REACH
AVERAGE = PROBS + 2 * OFFSETS
PLANES = AVERAGE + 1


def lookup(row, codes):
    index = codes.astype(jnp.int32)
    lanes = 128
    low = jnp.bitwise_and(index, lanes - 1)
    parts = [
        jnp.take_along_axis(
            jnp.broadcast_to(row[:, at : at + lanes], codes.shape), low, axis=1
        )
        for at in range(0, row.shape[1], lanes)
    ]
    return jnp.where(index >= lanes, parts[1], parts[0])


def packed_row(ref, plane, row):
    return jnp.broadcast_to(ref[plane, pl.ds(row, 1), :], (16, ref.shape[2])).astype(BF16)


def spread_rows(plan, k, row, values):
    lanes = plan.shape[2]
    blocks = values // 16
    name = names(values, lanes)
    total = jnp.zeros((blocks, 16, lanes), BF16)
    for j in range(REACH):
        code = packed_row(plan, CODES + k + j, row)
        weight = packed_row(plan, WEIGHTS + k * REACH + j, row)
        total = jnp.where(name == code[None], total + weight[None], total)
    return total.reshape(values, lanes)


def accumulate(plan, total_ref, ks, cot, values, extra=None):
    rows, half = plan.shape[1:]
    for chunk in range(rows // 2):
        pieces = [
            jnp.concatenate(
                [
                    spread_rows(plan, k, 2 * chunk, values),
                    spread_rows(plan, k, 2 * chunk + 1, values),
                ],
                1,
            )
            for k in ks
        ]
        if extra is not None:
            pieces.append(extra(chunk))
        left = jnp.concatenate(pieces, 0)
        part = dot(left, cot[2 * chunk * half : 2 * (chunk + 1) * half, :])
        if chunk == 0:
            total_ref[...] = part
        else:
            total_ref[...] += part


def split(value):
    high = value.astype(BF16)
    return high, (value - high.astype(F32)).astype(BF16)


def thirds(value):
    high = value.astype(BF16)
    rest = value - high.astype(F32)
    middle = rest.astype(BF16)
    return high, middle, (rest - middle.astype(F32)).astype(BF16)


def far_kernel(order, slot, values, *refs):
    scorers = pieces_of(refs[:2], len(order))
    table_low, planes, scorer, cot = refs[2:6]
    sent_first, sent_second, plan, vectors, table, total = refs[6:]
    rows = plan.shape[1]
    every = jnp.concatenate([s[:8] for s in scorers], 0)
    parts = thirds(every)
    found = dot(jnp.concatenate(parts, 0), table_low[...], NT)
    count = every.shape[0]
    found = found[:count] + found[count : 2 * count] + found[2 * count :]
    for at, m in enumerate(order):
        table[group_index() ^ m] = found[at * 8 : (at + 1) * 8]
    half = planes.shape[1] // SPAN
    codes, window = window_of([planes[:, m * half : (m + 1) * half] for m in range(SPAN)], rows)
    bias = functools.reduce(jnp.add, [s[1:2] for s in scorers])
    both = [scorer[:8].astype(F32), jnp.broadcast_to(bias, (8, bias.shape[1]))]
    vectors[...] = jnp.concatenate(both, 0).astype(BF16)
    shared = jnp.sum(both[0] * both[1], 1, keepdims=True)[:1]
    conv_scores = [shared] * REACH
    for k in range(OFFSETS):
        row = table[k, :1, :]
        for m in range(k, k + REACH):
            conv_scores[m - k] = conv_scores[m - k] + window.mask[k, m - k] * lookup(row, codes[m])
    for m in range(SPAN):
        plan[CODES + m] = codes[m]
    shares = []
    for side in range(2):
        block = window.pooled(side, conv_scores)
        top = functools.reduce(jnp.maximum, block)
        exps = [jnp.exp(b - top) for b in block]
        inverse = 1.0 / functools.reduce(jnp.add, exps)
        shares.append([e * inverse for e in exps])
        for k in range(OFFSETS):
            plan[PROBS + side * OFFSETS + k] = shares[side][k]
    mixing = [0.5 * e for e in window.spread(shares)]
    plan[AVERAGE] = functools.reduce(jnp.add, mixing)
    for k in range(OFFSETS):
        for j in range(REACH):
            plan[MASKS + k * REACH + j] = window.mask[k, j]
            plan[WEIGHTS + k * REACH + j] = window.mask[k, j] * mixing[j]
    accumulate(plan, total, [group_index() ^ slot], cot, values)
    for at, sent in enumerate((sent_first, sent_second)):
        sent[...] = total[at * values // 2 : (at + 1) * values // 2].astype(BF16)


def block_kernel(slot, values, plan, cot, out):
    accumulate(plan, out, [group_index() ^ slot], cot, values)


def average_line(plan, chunk):
    return jnp.concatenate([plan[AVERAGE, row : row + 1, :] for row in (2 * chunk, 2 * chunk + 1)], 1)


def near_kernel(slots, values, plan, cot, own, sent, bias_out, total):
    half = plan.shape[2]

    def extra(chunk):
        line = jnp.broadcast_to(average_line(plan, chunk), (EXTRA, 2 * half))
        high, low = split(line)
        at = lax.broadcasted_iota(jnp.int32, line.shape, 0)
        return jnp.where(at == 0, high.astype(F32), jnp.where(at == 1, low.astype(F32), 0.0)).astype(BF16)

    accumulate(plan, total, [group_index() ^ m for m in slots], cot, values, extra)
    own[...] = total[:values]
    sent[...] = total[values : 2 * values].astype(BF16)
    end = total[len(slots) * values :]
    bias_out[...] = jnp.broadcast_to(end[:1] + end[1:2], (8, end.shape[1]))


def inner_kernel(order, values, products, plan, vectors, cot, *refs):
    before, out = (refs[0] if len(refs) > 1 else None), refs[-1]
    rows, half = plan.shape[1:]
    blocks = values // 16
    name = names(values, half)
    left = products[...]
    if before is None:
        left = jnp.concatenate([left, vectors[...]], 0)
    for chunk in range(rows // 2):
        here = cot[2 * chunk * half : 2 * (chunk + 1) * half, :]
        both = dot(left, here, NT)
        found = {}
        for place, m in enumerate(order):
            k = group_index() ^ m
            each = both[place * values : (place + 1) * values].astype(BF16)
            for side in range(2):
                row = 2 * chunk + side
                mine = each[:, side * half : (side + 1) * half].reshape(blocks, 16, half)
                for j in range(REACH):
                    code = packed_row(plan, CODES + k + j, row)
                    picked = jnp.zeros((16, half), BF16)
                    for at in range(blocks):
                        picked = jnp.where(name[at] == code, mine[at], picked)
                    mask = plan[MASKS + k * REACH + j, row : row + 1, :]
                    found[j, side] = found.get((j, side), 0.0) + picked.astype(F32) * mask
        for side in range(2):
            row = 2 * chunk + side
            for j in range(REACH):
                if before is None:
                    at = len(order) * values + 8
                    start = both[at : at + 1, side * half : (side + 1) * half]
                else:
                    start = before[j, row : row + 1, :]
                out[j, row : row + 1, :] = jnp.sum(found[j, side], 0, keepdims=True) + start


def score_kernel(order, values, *refs):
    products = pieces_of(refs[:2], len(order))
    inner_ref, plan, vectors, hot = refs[2:6]
    out, flat, rows_ref = refs[6:]
    rows, half = plan.shape[1:]
    biases = vectors[8:]
    window = Window({(k, j): plan[MASKS + k * REACH + j] for k in range(OFFSETS) for j in range(REACH)})
    inner_rows = [0.5 * inner_ref[j] for j in range(REACH)]
    sides = []
    for side in range(2):
        inner = window.pooled(side, inner_rows)
        share = [plan[PROBS + side * OFFSETS + k] for k in range(OFFSETS)]
        mean = functools.reduce(jnp.add, [s * i for s, i in zip(share, inner)])
        sides.append([s * (i - mean) for s, i in zip(share, inner)])
    grads = window.spread(sides)
    overall = jnp.sum(jnp.sum(functools.reduce(jnp.add, grads), 1, keepdims=True), 0, keepdims=True)
    lane = lax.broadcasted_iota(jnp.int32, (rows, half), 1)
    flat[...] = jnp.zeros(flat.shape, F32)
    for k in range(OFFSETS):
        edges = []
        for side in range(2):
            inside = jnp.zeros((rows, half), F32)
            edge = jnp.zeros((rows, half), F32)
            for m in range(side, SPAN, 2):
                if not 0 <= m - k < REACH:
                    continue
                value = grads[m - k] * window.mask[k, m - k]
                steps = m // 2
                if steps:
                    inside = inside + jnp.where(lane < half - steps, pltpu.roll(value, half - steps, 1), 0.0)
                    moved = pltpu.roll(value, EDGE - steps, 1) if steps < EDGE else value
                    edge = edge + jnp.where((lane >= EDGE - steps) & (lane < EDGE), moved, 0.0)
                else:
                    inside = inside + value
            for row in range(rows):
                at = (side * rows + row) * half
                flat[k : k + 1, at : at + half] = inside[row : row + 1, :]
            edges.append(edge)
        flat[k : k + 1, 2 * rows * half :] = gathered_edges(edges)
    high, low = split(flat[...])
    both = jnp.concatenate([high.astype(F32), low.astype(F32)], 0).astype(BF16)
    edge = gathered_edges([plan[CODES + SPAN - 2 + side] for side in range(2)])
    lines = dot(both[:, : hot.shape[1]], hot[...], NT) + dot(both[:, hot.shape[1] :], one_hot(names(values, half), edge), NT)
    lines = lines[:8] + lines[8:]
    for k in range(OFFSETS):
        rows_ref[k] = jnp.broadcast_to(lines[k : k + 1], (8, values))
    width = biases.shape[1]
    score_grad = jnp.zeros((1, width), F32)
    for slot, m in zip(products, order):
        got = dot(pack(rows_ref[group_index() ^ m]), slot[...])
        score_grad = score_grad + got[:1] + got[8:9]
    out[...] = jnp.zeros(out.shape, F32)
    out[:1] = score_grad + overall * biases[:1].astype(F32)
    out[1:2] = overall * vectors[:1].astype(F32)
    for k in range(OFFSETS):
        out[2 + k : 3 + k, :values] = lines[k : k + 1]


def output_kernel(order, values, chunks_here, *refs):
    products = pieces_of(refs[:2], len(order))
    plan, vectors = refs[2:4]
    out, token, staged, sems = refs[-4:]
    token[...] = jnp.zeros(token.shape, F32)
    half = plan.shape[2]
    step = 2 * half
    biases = vectors[8:].astype(F32)
    at = lax.broadcasted_iota(jnp.int32, (8, step), 0)
    first = lax.broadcasted_iota(jnp.int32, biases.shape, 0)
    biases = jnp.where(first < 2, biases, 0.0)
    copies = []
    for place, chunk in enumerate(chunks_here):
        high, low = split(jnp.broadcast_to(average_line(plan, chunk), (8, step)))
        both = jnp.where(at == 0, high.astype(F32), jnp.where(at == 1, low.astype(F32), 0.0))
        total = dot(both, biases, TN)
        for slot, m in zip(products, order):
            k = group_index() ^ m
            left = jnp.concatenate([spread_rows(plan, k, row, values) for row in (2 * chunk, 2 * chunk + 1)], 1)
            total = total + dot(left, slot[...], TN)
        staged[place * step : (place + 1) * step, :] = total.astype(BF16)
        copies.append(
            pltpu.make_async_copy(
                staged.at[pl.ds(place * step, step), :], out.at[pl.ds(chunk * step, step), :], sems.at[place]
            )
        )
        copies[-1].start()
    for copy in copies:
        copy.wait()


def output_part(before, part, parts, order, values, products, plan, vectors, after):
    rows, half = plan.shape[1:]
    width = vectors.shape[1]
    each = rows // 2 // parts
    operands = [pltpu.with_memory_space_constraint(x, pltpu.VMEM) for x in (*products, plan, vectors)]
    operands += [] if before is None else [pltpu.with_memory_space_constraint(before, pltpu.HBM)]
    vmem = pl.BlockSpec(memory_space=pltpu.VMEM)
    elsewhere = pl.BlockSpec(memory_space=pl.ANY)
    count = len(products) + 2
    chunks_here = range(part * each, (part + 1) * each)

    def run(*refs):
        output_kernel(order, values, chunks_here, *refs[:count], *refs[-4:])

    return pl.pallas_call(
        run,
        out_shape=[jax.ShapeDtypeStruct((rows * half, width), BF16), pltpu.VMEM((8, 128), F32)],
        in_specs=[vmem] * count + [elsewhere] * (len(operands) - count + len(after)),
        out_specs=[elsewhere, vmem],
        input_output_aliases={} if before is None else {count: 0},
        scratch_shapes=[pltpu.VMEM((2 * half * each, width), BF16), pltpu.SemaphoreType.DMA((each,))],
        compiler_params=pltpu.CompilerParams(vmem_limit_bytes=VMEM_LIMIT),
        cost_estimate=pl.CostEstimate(flops=0, bytes_accessed=0, transcendentals=0),
        name="output",
    )(*operands, *after)


def chunks(values, piece, group):
    block = values // OFFSETS
    size = block // PIECES
    for actual in range(PIECES):
        for offset in range(OFFSETS):
            at = pl.multiple_of((piece ^ actual) * OFFSETS * size + (group ^ offset) * size, size)
            yield offset * block + actual * size, at, size


def pack(rows):
    high, low = split(rows)
    return jnp.concatenate([high.astype(F32), low.astype(F32)], 0).astype(BF16)


def unpack(block):
    return block[:8].astype(F32) + block[8:].astype(F32)


def small_sums(sums, bias):
    second = lax.broadcasted_iota(jnp.int32, bias.shape, 0) == 1
    return pack(sums[...] + jnp.where(second, bias[...], 0.0))


def sent_kernel(slots, near, far, sums, bias, *sends):
    size = near.shape[0] // PIECES
    for at, (slot, send) in enumerate(zip(slots, sends)):
        total = near[slot * size : (slot + 1) * size] + far[at * size : (at + 1) * size].astype(F32)
        send[:size] = total.astype(BF16)
        send[size:] = small_sums(sums, bias)


def rest_kernel(near, far, sums, bias, keep, send):
    size = keep.shape[0]
    keep[...] = near[:size] + far[:size].astype(F32)
    send[:size] = (near[2 * size : 3 * size] + far[size:].astype(F32)).astype(BF16)
    send[size:] = small_sums(sums, bias)


def slice_kernel(keep, own, *refs):
    others, send = refs[:-1], refs[-1]
    part = keep.shape[0]
    total = functools.reduce(jnp.add, [keep[...]] + [o[:part].astype(F32) for o in others])
    small = [unpack(x[part:]) for x in (own, *others)]
    while len(small) > 1:
        small = [small[at] + small[at + 1] for at in range(0, len(small), 2)]
    send[:part] = total.astype(BF16)
    send[part:] = pack(small[0])


def whole_kernel(mine, other, send):
    rows = mine.shape[0] - EXTRA
    send[:rows] = (mine[:rows].astype(F32) + other[:rows].astype(F32)).astype(BF16)
    send[rows:] = pack(unpack(mine[rows:]) + unpack(other[rows:]))


def last_kernel(mine, other, block, sums):
    rows = block.shape[0]
    block[...] = (mine[:rows].astype(F32) + other[:rows].astype(F32)).astype(BF16)
    sums[...] = unpack(mine[rows:]) + unpack(other[rows:])


def share_kernel(block, sums, weight_low, keep, send):
    product = dot(block[...], weight_low[...], NT)
    rows = keep.shape[0]
    keep[...] = product[:rows]
    send[:rows] = product[rows:].astype(BF16)
    send[rows:] = pack(sums[...])


def half_kernel(keep, sums, other, rest, send, total):
    rows = rest.shape[0]
    both = keep[...] + other[: 2 * rows].astype(F32)
    total[...] = sums[...] + unpack(other[2 * rows :])
    rest[...] = both[:rows]
    send[:rows] = both[rows:].astype(BF16)
    send[rows:] = pack(total[...])


def combine_kernel(keep, sums, other, out, total):
    rows = keep.shape[0]
    out[...] = (keep[...] + other[:rows].astype(F32)).astype(BF16)
    total[...] = sums[...] + unpack(other[rows:])


def added_kernel(mine, other, out):
    out[...] = (mine[...].astype(F32) + other[...].astype(F32)).astype(out.dtype)


def arrange(source, target, group):
    values = source.shape[0]
    for at, place, size in chunks(values, piece_index(), group):
        target[pl.ds(place, size), :] = source[at : at + size]


def far_sum_kernel(mine, one, two, first, second, total):
    rows = one.shape[0]
    halves = [mine[:rows] + one[...].astype(F32), mine[rows:] + two[...].astype(F32)]
    arrange(jnp.concatenate(halves, 0), total, group_index() ^ 2)
    size = total.shape[0] // PIECES
    for out, slots in ((first, (1, 3)), (second, (0, 2))):
        for at, slot in enumerate(slots):
            out[at * size : (at + 1) * size] = total[slot * size : (slot + 1) * size].astype(BF16)


def near_sum_kernel(near, other, total):
    arrange(near[...] + other[...].astype(F32), total, group_index())


def weight_kernel(order, offsets, *refs):
    slots = refs[: len(order)]
    turned, vectors, sums = refs[len(order) : len(order) + 3]
    scorers = pieces_of(refs[len(order) + 3 : len(order) + 5], len(offsets))
    out, score_out, bias_out, ranks, full, staged, rows_ref, ends, sems = refs[len(order) + 5 :]
    values, width = full.shape
    group, piece = group_index(), piece_index()
    block = values // OFFSETS
    size = block // PIECES
    copies = []

    def send(source, target):
        copies.append(pltpu.make_async_copy(source, target, sems.at[len(copies)]))
        copies[-1].start()

    for m, slot in zip(order, slots):
        for offset in range(OFFSETS):
            at = (group ^ offset) * block + (piece ^ m) * size
            full[pl.ds(pl.multiple_of(at, size), size), :] = slot[offset * size : (offset + 1) * size]
    line = sums[pl.ds(group + 2, 1), :values]
    scores = jnp.concatenate([vectors[:8], vectors[:8]], 0)
    first = lax.broadcasted_iota(jnp.int32, (8, values), 0) == 0
    both = pack(jnp.where(first, jnp.broadcast_to(line, first.shape), 0.0))
    parts, step = staged.shape[:2]
    for part in range(parts):
        here = turned[part * step : (part + 1) * step]
        high, low = split(dot(here, both, NT))
        staged[part] = dot(here, full[...]) + dot(high, scores) + dot(low, scores)
        send(staged.at[part], out.at[pl.ds(part * step, step), :])
    shard = score_out.shape[1]
    source = lax.broadcasted_iota(jnp.int32, (width, shard), 0)
    column = lax.broadcasted_iota(jnp.int32, (width, shard), 1) + row_index() * shard
    here = (source == column).astype(BF16)
    ends[...] = functools.reduce(jnp.add, [dot(part, here) for part in thirds(sums[...])])
    send(ends.at[pl.ds(0, 1), :], score_out)
    send(ends.at[pl.ds(1, 1), :], bias_out)
    for scorer, m in zip(scorers, offsets):
        rows_ref[group ^ m] = scorer[...]
    high, low = split(sums[2 : 2 + OFFSETS, :values])
    right_high, right_low = split(jnp.concatenate([rows_ref[k, :1] for k in range(OFFSETS)], 0))
    left = jnp.concatenate([x.astype(F32) for x in (high, low, high, low)], 0).astype(BF16)
    right = jnp.concatenate([x.astype(F32) for x in (right_high, right_high, right_low, right_low)], 0).astype(BF16)
    ranks[...] = dot(left, right, TN)
    for copy in copies:
        copy.wait()


def table_grad_kernel(order, *refs):
    slots, (ranks, out, table) = refs[: len(order)], refs[len(order) :]
    group, block = group_index(), table.shape[0]
    for slot, m in zip(slots, order):
        size = slot.shape[0]
        at = pl.multiple_of((piece_index() ^ m) * size, size)
        table[pl.ds(at, size), :] = slot[...].astype(F32) + ranks[pl.ds(pl.multiple_of(group * block, block) + at, size), :]
    rows = out.shape[0]
    inside = row_index() * rows - group * block
    out[...] = table[pl.ds(pl.multiple_of(inside, rows), rows), :]


def bits_of(count):
    return [1 << at for at in reversed(range(count.bit_length() - 1))]


def body(byte_values, segment_ids, valid, table, conv_weight, conv_bias, score_weight, cotangent):
    rows_count, tract_count = lax.axis_size("rows"), lax.axis_size("tract")
    rows_at = lax.axis_index("rows")
    values, width = table.shape[0] * rows_count, table.shape[1]
    rows, length = byte_values.shape
    half = length // 2
    copies = rows_count // OFFSETS
    order = [0, 2, 1, 3]
    group_bits = [2 * copies, copies]
    near_bits = [bit for bit in bits_of(rows_count) if bit < copies]

    row_bits = bits_of(rows_count)
    far_score = swap(score_weight[None], "rows", row_bits[0])
    near_order = slots_of(near_bits)
    biases = [conv_bias[None]]
    for bit in near_bits:
        biases = biases + [swap(value, "rows", bit) for value in biases]
    weight = conv_weight
    if copies > 1:
        near_by = [[g * copies + c for c in range(copies)] for g in range(OFFSETS)]
        weight = lax.all_gather(conv_weight, "rows", axis=0, tiled=True, axis_index_groups=near_by)
    shard = (1, conv_bias.shape[0])
    table_low, score, biases[0], ids = call(
        functools.partial(load_kernel, rows),
        [(table.shape, BF16), (shard, F32), (shard, F32), ((3 * rows, length), F32)],
        (table,), (score_weight[None],), (conv_bias[None],), (byte_values,), (segment_ids,), (valid,),
        scratch=[pltpu.VMEM(table.shape, F32), pltpu.VMEM((3, rows, length), jnp.int32), pltpu.SemaphoreType.DMA((6,))],
        name="load",
    )
    parts = 4
    weight_low = call(
        weight_low_kernel, [(weight.shape, BF16)], (weight,),
        scratch=[pltpu.VMEM((parts, weight.shape[0] // parts, width), F32), pltpu.SemaphoreType.DMA((parts,))],
        name="weight_low", after=[table_low],
    )[0]
    scores = gathered(stacked(score, far_score, name="score"), "rows", row_bits[1:], "score")
    scorer, scored = call(
        functools.partial(scorer_kernel, slots_of(row_bits), near_order),
        [((EXTRA, width), BF16), ((SENT, width), F32)], *scores, *biases, weight_low, name="scorer",
    )
    far_scored = swap(scored, "rows", group_bits[0])
    table_low = stacked(table_low, name="table_low", after=[far_score])
    far_table = swap(table_low, "rows", row_bits[0])
    table_low = stacked(table_low, far_table, name="table_pair", after=[scored])
    table_low = call(
        functools.partial(table_kernel, slots_of(row_bits)), [((values, width), BF16)],
        *gathered(table_low, "rows", row_bits[1:], "table_pair"), name="table",
    )[0]
    product, turned = call(
        products_kernel, [((values, width), BF16), ((width, values), BF16)], table_low, weight_low, name="products", after=[],
    )
    tail = stacked(ids, name="tail", after=[product])
    before = lax.ppermute(tail, "tract", [(i, i + 1) for i in range(tract_count - 1)])
    planes, hot = call(
        planes_kernel, [((3 * rows, SPAN * half), F32), ((values, 2 * rows * half), BF16)], ids, name="planes", after=[product],
    )
    planes = call(halo_kernel, [(planes.shape, F32)], planes, before, name="halo")[0]
    scorers = call(pair_kernel, [((16, width), F32)], scored, far_scored, name="scored")[0]
    scorers = scorers, swap(scorers, "rows", group_bits[1])

    cot = cotangent.reshape(rows * half, width)
    *far_sent, plan, vectors = call(
        functools.partial(far_kernel, order, 3, values),
        [((values // 2, width), BF16), ((values // 2, width), BF16), ((PLANES, rows, half), F32), ((EXTRA, width), BF16)],
        *scorers, table_low, planes, scorer, cot,
        scratch=[pltpu.VMEM((OFFSETS, 8, values), F32), pltpu.VMEM((values, width), F32)], name="far",
    )
    far = call(functools.partial(block_kernel, 2, values), [((values, width), F32)], plan, cot, name="far_own")[0]
    far_sent = [swap(half_sent, "rows", copies) for half_sent in far_sent]
    far = call(
        far_sum_kernel, [((values // 2, width), BF16)] * 2, far, *far_sent,
        scratch=[pltpu.VMEM((values, width), F32)], name="far_sum",
    )
    far_others = [swap(part, "rows", 2 * copies) for part in far]
    far_product = swap(product, "rows", 2 * copies)
    near, near_sent, bias_part = call(
        functools.partial(near_kernel, [0, 1], values),
        [((values, width), F32), ((values, width), BF16), ((8, width), F32)], plan, cot,
        scratch=[pltpu.VMEM((2 * values + EXTRA, width), F32)], name="near", after=[far_product],
    )
    near_other = swap(near_sent, "rows", copies)

    product = stacked(product, far_product, name="passed")
    products = product, swap(product, "rows", copies)
    inner = call(
        functools.partial(inner_kernel, [0, 2], values), [((REACH, rows, half), F32)],
        products[0], plan, vectors, cot, name="inner_near", cost=LONG,
    )[0]
    inner = call(
        functools.partial(inner_kernel, [1, 3], values), [((REACH, rows, half), F32)],
        products[1], plan, vectors, cot, inner, name="inner_far",
    )[0]
    sums = call(
        functools.partial(score_kernel, order, values), [((8, width), F32)], *products, inner, plan, vectors, hot,
        scratch=[pltpu.VMEM((8, hot.shape[1] + half), F32), pltpu.VMEM((OFFSETS, 8, values), F32)], name="scores",
    )[0]

    rest = [("tract", 1 << at) for at in range(PIECES.bit_length() - 1, tract_count.bit_length() - 1)]
    rest += [("rows", 1 << at) for at in range(copies.bit_length() - 1)]
    size = values // PIECES
    near = call(near_sum_kernel, [((values, width), F32)], near, near_other, name="near_sum")[0]
    sent = ((size + EXTRA, width), BF16)
    send_one, send_three = call(
        functools.partial(sent_kernel, (1, 3)), [sent, sent], near, far_others[0], sums, bias_part, name="merge",
    )
    keep, send_two = call(rest_kernel, [((size, width), F32), sent], near, far_others[1], sums, bias_part, name="rest")
    sends = [send_one, send_two, send_three]
    others = [swap(send, "tract", at + 1) for at, send in enumerate(sends)]
    parts = 2

    def fill(out, which, after):
        for part in which:
            out, token = output_part(out, part, parts, order, values, products, plan, vectors, [after])
        return out, token

    out, token = fill(None, [0], keep)
    send = call(slice_kernel, [((size + EXTRA, width), BF16)], keep, sends[0], *others, name="slice", after=[token])[0]
    out, token = fill(out, [1], send)
    for axis, bit in rest[:-1]:
        other = swap(send, axis, bit)
        send = call(whole_kernel, [(send.shape, BF16)], send, other, name="whole")[0]
    other = swap(send, *rest[-1])
    block, sums = call(last_kernel, [((size, width), BF16), ((8, width), F32)], send, other, name="last", after=[token])

    part = size // OFFSETS
    keep, send = call(
        share_kernel, [((2 * part, width), F32), ((2 * part + EXTRA, width), BF16)], block, sums, weight_low, name="share",
    )
    other = swap(send, "rows", group_bits[0])
    blocks = {0: block} | {m: swap(block, "tract", m) for m in range(1, PIECES)}
    keep, send, sums = call(
        half_kernel, [((part, width), F32), ((part + EXTRA, width), BF16), ((8, width), F32)], keep, sums, other, name="half",
    )
    other = swap(send, "rows", group_bits[1])
    table_piece, sums = call(combine_kernel, [((part, width), BF16), ((8, width), F32)], keep, sums, other, name="combine")
    table_pieces = {0: table_piece} | {m: swap(table_piece, "tract", m) for m in range(1, PIECES)}
    if copies > 1:
        turned = lax.dynamic_slice_in_dim(turned, rows_at % copies * (width // copies), width // copies, 0)
    weight_rows = conv_weight.shape[0]
    steps = 3
    weight_grad, score_grad, bias_grad, ranks = call(
        functools.partial(weight_kernel, list(blocks), order),
        [((weight_rows, width), F32), (shard, F32), (shard, F32), ((values, width), F32)],
        *blocks.values(), turned, vectors, sums, *scorers,
        scratch=[pltpu.VMEM((values, width), BF16), pltpu.VMEM((steps, weight_rows // steps, width), F32),
                 pltpu.VMEM((OFFSETS, 8, width), F32), pltpu.VMEM((8, shard[1]), F32), pltpu.SemaphoreType.DMA((steps + 2,))],
        name="weights", final=3, copied=True,
    )
    table_grad = call(
        functools.partial(table_grad_kernel, list(table_pieces)), [(table.shape, F32)], *table_pieces.values(), ranks,
        scratch=[pltpu.VMEM((values // OFFSETS, width), F32)], name="table_grad", final=1,
    )[0]
    return out.reshape(cotangent.shape), table_grad, weight_grad, bias_grad[0], score_grad[0]


def solution(mesh):
    return jax.shard_map(
        body,
        mesh=mesh,
        in_specs=(
            P("rows", "tract"), P("rows", "tract"), P("rows", "tract"), P("rows", None),
            P("rows", None), P("rows"), P("rows"), P("rows", "tract", None),
        ),
        out_specs=(P("rows", "tract", None), P("rows", None), P("rows", None), P("rows"), P("rows")),
        check_vma=False,
    )
```

```python
import functools

import jax
import jax.numpy as jnp
from jax import lax
from jax.experimental import pallas as pl
from jax.experimental.pallas import tpu as pltpu
from jax.sharding import PartitionSpec as P

F32 = jnp.float32
BF16 = jnp.bfloat16
OFFSETS = 4
REACH = 5
SPAN = 8
EXTRA = 16
SMALL = 8
PIECES = 4
EDGE = 3
VMEM_LIMIT = 16 * 1024 * 1024
SENT = 48
LONG = 10**11
NT = (((1,), (1,)), ((), ()))
TN = (((0,), (0,)), ((), ()))
NN = (((1,), (0,)), ((), ()))


def dot(a, b, dims=NN, precision=None):
    return lax.dot_general(a, b, dims, precision=precision, preferred_element_type=F32)


def exact(a, b, dims=NN):
    return dot(a, b, dims, lax.Precision.HIGHEST)


def call(kernel, outs, *operands, scratch=(), cost=0, name=None, after=(), final=0, copied=False):
    vmem = pl.BlockSpec(memory_space=pltpu.VMEM)
    hbm = pl.BlockSpec(memory_space=pltpu.HBM)
    stored = [isinstance(operand, tuple) for operand in operands]
    held = [
        pltpu.with_memory_space_constraint(operand[0] if far else operand, pltpu.HBM if far else pltpu.VMEM)
        for operand, far in zip(operands, stored)
    ]
    count = len(operands)

    def run(*refs):
        kernel(*refs[:count], *refs[count + len(after) :])

    return pl.pallas_call(
        run if after else kernel,
        out_shape=[jax.ShapeDtypeStruct(*o) if at < final else pltpu.VMEM(*o) for at, o in enumerate(outs)],
        in_specs=[hbm if far else vmem for far in stored] + [pl.BlockSpec(memory_space=pl.ANY)] * len(after),
        out_specs=[hbm if at < final and copied else vmem for at in range(len(outs))],
        scratch_shapes=list(scratch),
        compiler_params=pltpu.CompilerParams(vmem_limit_bytes=VMEM_LIMIT),
        cost_estimate=pl.CostEstimate(flops=cost, bytes_accessed=0, transcendentals=0),
        name=name,
    )(*held, *after)


def swap(value, axis, bit):
    count = lax.axis_size(axis)
    return lax.ppermute(value, axis, [(i, i ^ bit) for i in range(count)])


def stack_kernel(*refs):
    out = refs[-1]
    rows = refs[0].shape[0]
    for at, value in enumerate(refs[:-1]):
        out[at * rows : (at + 1) * rows] = value[...]


def stacked(*values, name, after=()):
    rows, width = values[0].shape
    return call(stack_kernel, [((len(values) * rows, width), values[0].dtype)], *values, name=name, after=after)[0]


def slots_of(bits):
    order = [0]
    for bit in bits:
        order = order + [m | bit for m in order]
    return order


def gathered(value, axis, bits, name, after=()):
    for bit in bits[:-1]:
        value = stacked(value, swap(value, axis, bit), name=name, after=after)
    return value, swap(value, axis, bits[-1])


def pieces_of(refs, count):
    each = count // len(refs)
    rows = refs[0].shape[0] // each
    return [ref.at[pl.ds(at * rows, rows), :] for ref in refs for at in range(each)]


def row_index():
    return lax.axis_index("rows")


def group_index():
    return lax.axis_index("rows") // (lax.axis_size("rows") // OFFSETS)


def piece_index():
    return lax.axis_index("tract") % PIECES


def load_kernel(rows, *refs):
    sources = refs[:6]
    table_low, score_here, bias_here, together, table_here, ids_here, sems = refs[6:]
    targets = [table_here, score_here, bias_here] + [ids_here.at[at] for at in range(3)]
    copies = [pltpu.make_async_copy(source, target, sems.at[at]) for at, (source, target) in enumerate(zip(sources, targets))]
    for copy in copies:
        copy.start()
    for copy in copies:
        copy.wait()
    table_low[...] = table_here[...].astype(BF16)
    for at in range(3):
        together[at * rows : (at + 1) * rows, :] = ids_here[at].astype(F32)


def weight_low_kernel(weight, out, here, sems):
    parts, size = here.shape[:2]
    copies = [
        pltpu.make_async_copy(weight.at[pl.ds(at * size, size), :], here.at[at], sems.at[at]) for at in range(parts)
    ]
    for copy in copies:
        copy.start()
    for at in range(parts):
        copies[at].wait()
        out[at * size : (at + 1) * size, :] = here[at].astype(BF16)


def pair_kernel(first, second, out):
    out[:8] = first[:8]
    out[8:] = second[:8]


def kept_kernel(*refs):
    half = len(refs) // 2
    for value, out in zip(refs[:half], refs[half:]):
        out[...] = value[...]


def placed(parts, width):
    total = None
    for part, at in parts:
        shard = part.shape[1]
        source = lax.broadcasted_iota(jnp.int32, (shard, width), 0) + at * shard
        column = lax.broadcasted_iota(jnp.int32, (shard, width), 1)
        row = jnp.broadcast_to(part[...], (8, shard)).astype(BF16)
        got = dot(row, (source == column).astype(BF16))
        total = got if total is None else total + got
    return total


def scorer_kernel(order, near_order, *refs):
    scores = pieces_of(refs[:2], len(order))
    biases = refs[2 : 2 + len(near_order)]
    weight_low, scorer, out = refs[2 + len(near_order) :]
    width = scorer.shape[1]
    full = placed([(part, row_index() ^ m) for part, m in zip(scores, order)], width)
    bias = placed([(part, row_index() ^ m) for part, m in zip(biases, near_order)], width)
    full = jnp.concatenate([full, full], 0).astype(BF16)
    scorer[...] = full
    at = lax.broadcasted_iota(jnp.int32, bias.shape, 0)
    out[...] = jnp.zeros(out.shape, F32)
    out[:8] = jnp.where(at == 0, dot(full, weight_low[...], NT)[:8], bias)


def table_kernel(order, first, second, table_low):
    slots = pieces_of((first, second), len(order))
    rows = slots[0].shape[0]
    for slot, m in zip(slots, order):
        at = pl.multiple_of((row_index() ^ m) * rows, rows)
        table_low[pl.ds(at, rows), :] = slot[...]


def products_kernel(table_low, weight_low, product, table_turned):
    product[...] = dot(table_low[...], weight_low[...]).astype(BF16)
    table_turned[...] = table_low[...].T


def planes_kernel(ids, out, hot):
    length = ids.shape[1]
    rows = ids.shape[0] // 3
    half = length // 2
    own = ids[...].astype(BF16)
    for m in range(SPAN):
        target = 2 * lax.broadcasted_iota(jnp.int32, (length, half), 1) + 1 - m
        source = lax.broadcasted_iota(jnp.int32, (length, half), 0)
        out[:, m * half : (m + 1) * half] = dot(own, (source == target).astype(BF16))
    name = names(hot.shape[0], half)
    for side in range(2):
        for row in range(rows):
            code = out[row : row + 1, side * half : (side + 1) * half]
            hot[:, (side * rows + row) * half : (side * rows + row + 1) * half] = one_hot(name, code)


def halo_kernel(planes, before, out):
    tail = 128
    earlier = before[:, before.shape[1] - tail :].astype(BF16)
    half = planes.shape[1] // SPAN
    for m in range(SPAN):
        part = planes[:, m * half : (m + 1) * half]
        if m > 1:
            target = 2 * lax.broadcasted_iota(jnp.int32, (tail, half), 1) + 1 - m + tail
            source = lax.broadcasted_iota(jnp.int32, (tail, half), 0)
            part = part + dot(earlier, (source == target).astype(BF16))
        out[:, m * half : (m + 1) * half] = part


def names(values, lanes):
    shape = (values // 16, 16, lanes)
    return (lax.broadcasted_iota(jnp.int32, shape, 0) * 16 + lax.broadcasted_iota(jnp.int32, shape, 1)).astype(F32).astype(BF16)


def one_hot(name, code):
    code = jnp.broadcast_to(code, name.shape[1:]).astype(BF16)
    return jnp.where(name == code[None], jnp.ones(name.shape, BF16), jnp.zeros(name.shape, BF16)).reshape(-1, name.shape[2])


def gathered_edges(planes):
    rows, lanes = planes[0].shape
    lane = lax.broadcasted_iota(jnp.int32, (rows, lanes), 1)
    row = lax.broadcasted_iota(jnp.int32, (rows, lanes), 0)
    total = jnp.zeros((rows, lanes), F32)
    for side, plane in enumerate(planes):
        for at in range(EDGE):
            place = (side * rows + row) * EDGE + at
            total = total + jnp.where(lane == place, plane[:, at : at + 1], 0.0)
    return jnp.sum(total, 0, keepdims=True)


class Window:
    def __init__(self, mask):
        self.mask = mask
        self.keep, self.divide = [], []
        for side in range(2):
            keep = [self.mask[k, side] for k in range(OFFSETS)]
            counts, total = [], 0.0
            for k in range(OFFSETS):
                total = total + keep[k]
                counts.append(1.0 / jnp.maximum(total, 1.0))
            self.keep.append(keep)
            self.divide.append(counts)

    def pooled(self, side, values):
        means, total = [], 0.0
        for k in range(OFFSETS):
            total = total + self.keep[side][k] * values[side + k]
            means.append(total * self.divide[side][k])
        return means

    def spread(self, sides):
        result = [0.0] * REACH
        for side in range(2):
            carried = 0.0
            for k in reversed(range(OFFSETS)):
                carried = carried + sides[side][k] * self.divide[side][k]
                result[side + k] = result[side + k] + self.keep[side][k] * carried
        return result


def window_of(planes, rows):
    segments = [plane[rows : 2 * rows] for plane in planes]
    valid = [plane[2 * rows :] for plane in planes]
    mask = {
        (k, j): (segments[j + k] == segments[j]).astype(F32) * valid[j + k]
        for k in range(OFFSETS)
        for j in range(REACH)
    }
    return [plane[:rows] for plane in planes], Window(mask)


CODES = 0
WEIGHTS = CODES + SPAN
MASKS = WEIGHTS + OFFSETS * REACH
PROBS = MASKS + OFFSETS * REACH
AVERAGE = PROBS + 2 * OFFSETS
PLANES = AVERAGE + 1


def lookup(row, codes):
    index = codes.astype(jnp.int32)
    lanes = 128
    low = jnp.bitwise_and(index, lanes - 1)
    parts = [
        jnp.take_along_axis(
            jnp.broadcast_to(row[:, at : at + lanes], codes.shape), low, axis=1
        )
        for at in range(0, row.shape[1], lanes)
    ]
    return jnp.where(index >= lanes, parts[1], parts[0])


def packed_row(ref, plane, row):
    return jnp.broadcast_to(ref[plane, pl.ds(row, 1), :], (16, ref.shape[2])).astype(BF16)


def spread_rows(plan, k, row, values):
    lanes = plan.shape[2]
    blocks = values // 16
    name = names(values, lanes)
    total = jnp.zeros((blocks, 16, lanes), BF16)
    for j in range(REACH):
        code = packed_row(plan, CODES + k + j, row)
        weight = packed_row(plan, WEIGHTS + k * REACH + j, row)
        total = jnp.where(name == code[None], total + weight[None], total)
    return total.reshape(values, lanes)


def accumulate(plan, total_ref, ks, cot, values, extra=None):
    rows, half = plan.shape[1:]
    for chunk in range(rows // 2):
        pieces = [
            jnp.concatenate(
                [
                    spread_rows(plan, k, 2 * chunk, values),
                    spread_rows(plan, k, 2 * chunk + 1, values),
                ],
                1,
            )
            for k in ks
        ]
        if extra is not None:
            pieces.append(extra(chunk))
        left = jnp.concatenate(pieces, 0)
        part = dot(left, cot[2 * chunk * half : 2 * (chunk + 1) * half, :])
        if chunk == 0:
            total_ref[...] = part
        else:
            total_ref[...] += part


def split(value):
    high = value.astype(BF16)
    return high, (value - high.astype(F32)).astype(BF16)


def thirds(value):
    high = value.astype(BF16)
    rest = value - high.astype(F32)
    middle = rest.astype(BF16)
    return high, middle, (rest - middle.astype(F32)).astype(BF16)


def far_kernel(order, slot, values, *refs):
    scorers = pieces_of(refs[:2], len(order))
    table_low, planes, scorer, cot = refs[2:6]
    sent_first, sent_second, plan, vectors, table, total = refs[6:]
    rows = plan.shape[1]
    every = jnp.concatenate([s[:8] for s in scorers], 0)
    parts = thirds(every)
    found = dot(jnp.concatenate(parts, 0), table_low[...], NT)
    count = every.shape[0]
    found = found[:count] + found[count : 2 * count] + found[2 * count :]
    for at, m in enumerate(order):
        table[group_index() ^ m] = found[at * 8 : (at + 1) * 8]
    half = planes.shape[1] // SPAN
    codes, window = window_of([planes[:, m * half : (m + 1) * half] for m in range(SPAN)], rows)
    bias = functools.reduce(jnp.add, [s[1:2] for s in scorers])
    both = [scorer[:8].astype(F32), jnp.broadcast_to(bias, (8, bias.shape[1]))]
    vectors[...] = jnp.concatenate(both, 0).astype(BF16)
    shared = jnp.sum(both[0] * both[1], 1, keepdims=True)[:1]
    conv_scores = [shared] * REACH
    for k in range(OFFSETS):
        row = table[k, :1, :]
        for m in range(k, k + REACH):
            conv_scores[m - k] = conv_scores[m - k] + window.mask[k, m - k] * lookup(row, codes[m])
    for m in range(SPAN):
        plan[CODES + m] = codes[m]
    shares = []
    for side in range(2):
        block = window.pooled(side, conv_scores)
        top = functools.reduce(jnp.maximum, block)
        exps = [jnp.exp(b - top) for b in block]
        inverse = 1.0 / functools.reduce(jnp.add, exps)
        shares.append([e * inverse for e in exps])
        for k in range(OFFSETS):
            plan[PROBS + side * OFFSETS + k] = shares[side][k]
    mixing = [0.5 * e for e in window.spread(shares)]
    plan[AVERAGE] = functools.reduce(jnp.add, mixing)
    for k in range(OFFSETS):
        for j in range(REACH):
            plan[MASKS + k * REACH + j] = window.mask[k, j]
            plan[WEIGHTS + k * REACH + j] = window.mask[k, j] * mixing[j]
    accumulate(plan, total, [group_index() ^ slot], cot, values)
    for at, sent in enumerate((sent_first, sent_second)):
        sent[...] = total[at * values // 2 : (at + 1) * values // 2].astype(BF16)


def block_kernel(slot, values, plan, cot, out):
    accumulate(plan, out, [group_index() ^ slot], cot, values)


def average_line(plan, chunk):
    return jnp.concatenate([plan[AVERAGE, row : row + 1, :] for row in (2 * chunk, 2 * chunk + 1)], 1)


def near_kernel(slots, values, plan, cot, own, sent, bias_out, total):
    half = plan.shape[2]

    def extra(chunk):
        line = jnp.broadcast_to(average_line(plan, chunk), (EXTRA, 2 * half))
        high, low = split(line)
        at = lax.broadcasted_iota(jnp.int32, line.shape, 0)
        return jnp.where(at == 0, high.astype(F32), jnp.where(at == 1, low.astype(F32), 0.0)).astype(BF16)

    accumulate(plan, total, [group_index() ^ m for m in slots], cot, values, extra)
    own[...] = total[:values]
    sent[...] = total[values : 2 * values].astype(BF16)
    end = total[len(slots) * values :]
    bias_out[...] = jnp.broadcast_to(end[:1] + end[1:2], (8, end.shape[1]))


def inner_kernel(order, values, products, plan, vectors, cot, *refs):
    before, out = (refs[0] if len(refs) > 1 else None), refs[-1]
    rows, half = plan.shape[1:]
    blocks = values // 16
    name = names(values, half)
    left = products[...]
    if before is None:
        left = jnp.concatenate([left, vectors[...]], 0)
    for chunk in range(rows // 2):
        here = cot[2 * chunk * half : 2 * (chunk + 1) * half, :]
        both = dot(left, here, NT)
        found = {}
        for place, m in enumerate(order):
            k = group_index() ^ m
            each = both[place * values : (place + 1) * values].astype(BF16)
            for side in range(2):
                row = 2 * chunk + side
                mine = each[:, side * half : (side + 1) * half].reshape(blocks, 16, half)
                for j in range(REACH):
                    code = packed_row(plan, CODES + k + j, row)
                    picked = jnp.zeros((16, half), BF16)
                    for at in range(blocks):
                        picked = jnp.where(name[at] == code, mine[at], picked)
                    mask = plan[MASKS + k * REACH + j, row : row + 1, :]
                    found[j, side] = found.get((j, side), 0.0) + picked.astype(F32) * mask
        for side in range(2):
            row = 2 * chunk + side
            for j in range(REACH):
                if before is None:
                    at = len(order) * values + 8
                    start = both[at : at + 1, side * half : (side + 1) * half]
                else:
                    start = before[j, row : row + 1, :]
                out[j, row : row + 1, :] = jnp.sum(found[j, side], 0, keepdims=True) + start


def score_kernel(values, inner_ref, plan, vectors, hot, out, flat):
    rows, half = plan.shape[1:]
    window = Window({(k, j): plan[MASKS + k * REACH + j] for k in range(OFFSETS) for j in range(REACH)})
    inner_rows = [0.5 * inner_ref[j] for j in range(REACH)]
    sides = []
    for side in range(2):
        inner = window.pooled(side, inner_rows)
        share = [plan[PROBS + side * OFFSETS + k] for k in range(OFFSETS)]
        mean = functools.reduce(jnp.add, [s * i for s, i in zip(share, inner)])
        sides.append([s * (i - mean) for s, i in zip(share, inner)])
    grads = window.spread(sides)
    overall = jnp.sum(jnp.sum(functools.reduce(jnp.add, grads), 1, keepdims=True), 0, keepdims=True)
    lane = lax.broadcasted_iota(jnp.int32, (rows, half), 1)
    flat[...] = jnp.zeros(flat.shape, F32)
    for k in range(OFFSETS):
        edges = []
        for side in range(2):
            inside = jnp.zeros((rows, half), F32)
            edge = jnp.zeros((rows, half), F32)
            for m in range(side, SPAN, 2):
                if not 0 <= m - k < REACH:
                    continue
                value = grads[m - k] * window.mask[k, m - k]
                steps = m // 2
                if steps:
                    inside = inside + jnp.where(lane < half - steps, pltpu.roll(value, half - steps, 1), 0.0)
                    moved = pltpu.roll(value, EDGE - steps, 1) if steps < EDGE else value
                    edge = edge + jnp.where((lane >= EDGE - steps) & (lane < EDGE), moved, 0.0)
                else:
                    inside = inside + value
            for row in range(rows):
                at = (side * rows + row) * half
                flat[k : k + 1, at : at + half] = inside[row : row + 1, :]
            edges.append(edge)
        flat[k : k + 1, 2 * rows * half :] = gathered_edges(edges)
    high, low = split(flat[...])
    both = jnp.concatenate([high.astype(F32), low.astype(F32)], 0).astype(BF16)
    edge = gathered_edges([plan[CODES + SPAN - 2 + side] for side in range(2)])
    lines = dot(both[:, : hot.shape[1]], hot[...], NT) + dot(both[:, hot.shape[1] :], one_hot(names(values, half), edge), NT)
    lines = lines[:8] + lines[8:]
    width = vectors.shape[1]
    out[...] = jnp.zeros(out.shape, F32)
    out[:1] = overall * vectors[:1].astype(F32)
    for k in range(OFFSETS + 1):
        row, lane = small_place(k, values, width)
        part = lines[k : k + 1] if k < OFFSETS else jnp.broadcast_to(overall, (1, values))
        out[row : row + 1, lane : lane + values] = part


def output_kernel(order, values, chunks_here, *refs):
    products = pieces_of(refs[:2], len(order))
    plan, vectors = refs[2:4]
    out, token, staged, sems = refs[-4:]
    token[...] = jnp.zeros(token.shape, F32)
    half = plan.shape[2]
    step = 2 * half
    biases = vectors[8:].astype(F32)
    at = lax.broadcasted_iota(jnp.int32, (8, step), 0)
    first = lax.broadcasted_iota(jnp.int32, biases.shape, 0)
    biases = jnp.where(first < 2, biases, 0.0)
    copies = []
    for place, chunk in enumerate(chunks_here):
        high, low = split(jnp.broadcast_to(average_line(plan, chunk), (8, step)))
        both = jnp.where(at == 0, high.astype(F32), jnp.where(at == 1, low.astype(F32), 0.0))
        total = dot(both, biases, TN)
        for slot, m in zip(products, order):
            k = group_index() ^ m
            left = jnp.concatenate([spread_rows(plan, k, row, values) for row in (2 * chunk, 2 * chunk + 1)], 1)
            total = total + dot(left, slot[...], TN)
        staged[place * step : (place + 1) * step, :] = total.astype(BF16)
        copies.append(
            pltpu.make_async_copy(
                staged.at[pl.ds(place * step, step), :], out.at[pl.ds(chunk * step, step), :], sems.at[place]
            )
        )
        copies[-1].start()
    for copy in copies:
        copy.wait()


def output_part(before, part, parts, order, values, products, plan, vectors, after):
    rows, half = plan.shape[1:]
    width = vectors.shape[1]
    each = rows // 2 // parts
    operands = [pltpu.with_memory_space_constraint(x, pltpu.VMEM) for x in (*products, plan, vectors)]
    operands += [] if before is None else [pltpu.with_memory_space_constraint(before, pltpu.HBM)]
    vmem = pl.BlockSpec(memory_space=pltpu.VMEM)
    elsewhere = pl.BlockSpec(memory_space=pl.ANY)
    count = len(products) + 2
    chunks_here = range(part * each, (part + 1) * each)

    def run(*refs):
        output_kernel(order, values, chunks_here, *refs[:count], *refs[-4:])

    return pl.pallas_call(
        run,
        out_shape=[jax.ShapeDtypeStruct((rows * half, width), BF16), pltpu.VMEM((8, 128), F32)],
        in_specs=[vmem] * count + [elsewhere] * (len(operands) - count + len(after)),
        out_specs=[elsewhere, vmem],
        input_output_aliases={} if before is None else {count: 0},
        scratch_shapes=[pltpu.VMEM((2 * half * each, width), BF16), pltpu.SemaphoreType.DMA((each,))],
        compiler_params=pltpu.CompilerParams(vmem_limit_bytes=VMEM_LIMIT),
        cost_estimate=pl.CostEstimate(flops=0, bytes_accessed=0, transcendentals=0),
        name="output",
    )(*operands, *after)


def chunks(values, piece, group):
    block = values // OFFSETS
    size = block // PIECES
    for actual in range(PIECES):
        for offset in range(OFFSETS):
            at = pl.multiple_of((piece ^ actual) * OFFSETS * size + (group ^ offset) * size, size)
            yield offset * block + actual * size, at, size


def pack(rows):
    high, low = split(rows)
    return jnp.concatenate([high.astype(F32), low.astype(F32)], 0).astype(BF16)


def small_place(at, values, width):
    per = width // values
    return 1 + at // per, at % per * values


def small_pack(rows):
    high, low = split(rows)
    return jnp.concatenate([high.astype(F32), low.astype(F32)], 0).astype(BF16)


def small_unpack(block):
    return block[: SMALL // 2].astype(F32) + block[SMALL // 2 :].astype(F32)


def small_sums(sums, bias):
    first = lax.broadcasted_iota(jnp.int32, sums.shape, 0) == 0
    return small_pack(sums[...] + jnp.where(first, bias[: sums.shape[0]], 0.0))


def sent_kernel(slots, near, far, sums, bias, *sends):
    size = near.shape[0] // PIECES
    for at, (slot, send) in enumerate(zip(slots, sends)):
        total = near[slot * size : (slot + 1) * size] + far[at * size : (at + 1) * size].astype(F32)
        send[:size] = total.astype(BF16)
        send[size:] = small_sums(sums, bias)


def rest_kernel(near, far, sums, bias, keep, send):
    size = keep.shape[0]
    keep[...] = near[:size] + far[:size].astype(F32)
    send[:size] = (near[2 * size : 3 * size] + far[size:].astype(F32)).astype(BF16)
    send[size:] = small_sums(sums, bias)


def slice_kernel(keep, own, *refs):
    others, send = refs[:-1], refs[-1]
    part = keep.shape[0]
    total = functools.reduce(jnp.add, [keep[...]] + [o[:part].astype(F32) for o in others])
    small = [small_unpack(x[part:]) for x in (own, *others)]
    while len(small) > 1:
        small = [small[at] + small[at + 1] for at in range(0, len(small), 2)]
    send[:part] = total.astype(BF16)
    send[part:] = small_pack(small[0])


def whole_kernel(mine, other, send):
    rows = mine.shape[0] - SMALL
    send[:rows] = (mine[:rows].astype(F32) + other[:rows].astype(F32)).astype(BF16)
    send[rows:] = small_pack(small_unpack(mine[rows:]) + small_unpack(other[rows:]))


def last_kernel(mine, other, block, sums):
    rows = block.shape[0]
    block[...] = (mine[:rows].astype(F32) + other[:rows].astype(F32)).astype(BF16)
    sums[...] = small_unpack(mine[rows:]) + small_unpack(other[rows:])


def share_kernel(block, sums, weight_low, keep, send):
    product = dot(block[...], weight_low[...], NT)
    rows = keep.shape[0]
    keep[...] = product[:rows]
    send[:rows] = product[rows:].astype(BF16)
    send[rows:] = small_pack(sums[...])


def half_kernel(keep, sums, other, rest, send, total):
    rows = rest.shape[0]
    both = keep[...] + other[: 2 * rows].astype(F32)
    total[...] = sums[...] + small_unpack(other[2 * rows :])
    rest[...] = both[:rows]
    send[:rows] = both[rows:].astype(BF16)
    send[rows:] = small_pack(total[...])


def combine_kernel(keep, sums, other, out, total):
    rows = keep.shape[0]
    out[...] = (keep[...] + other[:rows].astype(F32)).astype(BF16)
    total[...] = sums[...] + small_unpack(other[rows:])


def added_kernel(mine, other, out):
    out[...] = (mine[...].astype(F32) + other[...].astype(F32)).astype(out.dtype)


def arrange(source, target, group):
    values = source.shape[0]
    for at, place, size in chunks(values, piece_index(), group):
        target[pl.ds(place, size), :] = source[at : at + size]


def far_sum_kernel(mine, one, two, first, second, total):
    rows = one.shape[0]
    halves = [mine[:rows] + one[...].astype(F32), mine[rows:] + two[...].astype(F32)]
    arrange(jnp.concatenate(halves, 0), total, group_index() ^ 2)
    size = total.shape[0] // PIECES
    for out, slots in ((first, (1, 3)), (second, (0, 2))):
        for at, slot in enumerate(slots):
            out[at * size : (at + 1) * size] = total[slot * size : (slot + 1) * size].astype(BF16)


def near_sum_kernel(near, other, total):
    arrange(near[...] + other[...].astype(F32), total, group_index())


def weight_kernel(order, offsets, *refs):
    slots = refs[: len(order)]
    turned, vectors, sums = refs[len(order) : len(order) + 3]
    scorers = pieces_of(refs[len(order) + 3 : len(order) + 5], len(offsets))
    products = pieces_of(refs[len(order) + 5 : len(order) + 7], len(offsets))
    out, score_out, bias_out, ranks, full, staged, rows_ref, lines, ends, sems = refs[len(order) + 7 :]
    values, width = full.shape
    group, piece = group_index(), piece_index()
    block = values // OFFSETS
    size = block // PIECES
    copies = []

    def send(source, target):
        copies.append(pltpu.make_async_copy(source, target, sems.at[len(copies)]))
        copies[-1].start()

    for m, slot in zip(order, slots):
        for offset in range(OFFSETS):
            at = (group ^ offset) * block + (piece ^ m) * size
            full[pl.ds(pl.multiple_of(at, size), size), :] = slot[offset * size : (offset + 1) * size]
    for k in range(OFFSETS):
        row, lane = small_place(k, values, width)
        lines[k : k + 1] = sums[row : row + 1, lane : lane + values]
    line = lines[pl.ds(group, 1), :]
    scores = jnp.concatenate([vectors[:8], vectors[:8]], 0)
    first = lax.broadcasted_iota(jnp.int32, (8, values), 0) == 0
    both = pack(jnp.where(first, jnp.broadcast_to(line, first.shape), 0.0))
    parts, step = staged.shape[:2]
    for part in range(parts):
        here = turned[part * step : (part + 1) * step]
        high, low = split(dot(here, both, NT))
        staged[part] = dot(here, full[...]) + dot(high, scores) + dot(low, scores)
        send(staged.at[part], out.at[pl.ds(part * step, step), :])
    shard = score_out.shape[1]
    source = lax.broadcasted_iota(jnp.int32, (width, shard), 0)
    column = lax.broadcasted_iota(jnp.int32, (width, shard), 1) + row_index() * shard
    here = (source == column).astype(BF16)
    row, lane = small_place(OFFSETS, values, width)
    score_grad = sums[row : row + 1, lane : lane + 1] * vectors[8:9].astype(F32)
    for product, m in zip(products, offsets):
        got = dot(pack(jnp.broadcast_to(lines[pl.ds(group ^ m, 1), :], (8, values))), product[...])
        score_grad = score_grad + got[:1] + got[8:9]
    at = lax.broadcasted_iota(jnp.int32, (8, width), 0)
    small = jnp.where(at == 0, score_grad, jnp.where(at == 1, sums[:1], 0.0))
    ends[...] = functools.reduce(jnp.add, [dot(part, here) for part in thirds(small)])
    send(ends.at[pl.ds(0, 1), :], score_out)
    send(ends.at[pl.ds(1, 1), :], bias_out)
    for scorer, m in zip(scorers, offsets):
        rows_ref[group ^ m] = scorer[...]
    high, low = split(lines[:OFFSETS])
    right_high, right_low = split(jnp.concatenate([rows_ref[k, :1] for k in range(OFFSETS)], 0))
    left = jnp.concatenate([x.astype(F32) for x in (high, low, high, low)], 0).astype(BF16)
    right = jnp.concatenate([x.astype(F32) for x in (right_high, right_high, right_low, right_low)], 0).astype(BF16)
    ranks[...] = dot(left, right, TN)
    for copy in copies:
        copy.wait()


def table_grad_kernel(order, *refs):
    slots, (ranks, out, table) = refs[: len(order)], refs[len(order) :]
    group, block = group_index(), table.shape[0]
    for slot, m in zip(slots, order):
        size = slot.shape[0]
        at = pl.multiple_of((piece_index() ^ m) * size, size)
        table[pl.ds(at, size), :] = slot[...].astype(F32) + ranks[pl.ds(pl.multiple_of(group * block, block) + at, size), :]
    rows = out.shape[0]
    inside = row_index() * rows - group * block
    out[...] = table[pl.ds(pl.multiple_of(inside, rows), rows), :]


def bits_of(count):
    return [1 << at for at in reversed(range(count.bit_length() - 1))]


def body(byte_values, segment_ids, valid, table, conv_weight, conv_bias, score_weight, cotangent):
    rows_count, tract_count = lax.axis_size("rows"), lax.axis_size("tract")
    rows_at = lax.axis_index("rows")
    values, width = table.shape[0] * rows_count, table.shape[1]
    rows, length = byte_values.shape
    half = length // 2
    copies = rows_count // OFFSETS
    order = [0, 2, 1, 3]
    group_bits = [2 * copies, copies]
    near_bits = [bit for bit in bits_of(rows_count) if bit < copies]

    row_bits = bits_of(rows_count)
    far_score = swap(score_weight[None], "rows", row_bits[0])
    near_order = slots_of(near_bits)
    biases = [conv_bias[None]]
    for bit in near_bits:
        biases = biases + [swap(value, "rows", bit) for value in biases]
    weight = conv_weight
    if copies > 1:
        near_by = [[g * copies + c for c in range(copies)] for g in range(OFFSETS)]
        weight = lax.all_gather(conv_weight, "rows", axis=0, tiled=True, axis_index_groups=near_by)
    shard = (1, conv_bias.shape[0])
    table_low, score, biases[0], ids = call(
        functools.partial(load_kernel, rows),
        [(table.shape, BF16), (shard, F32), (shard, F32), ((3 * rows, length), F32)],
        (table,), (score_weight[None],), (conv_bias[None],), (byte_values,), (segment_ids,), (valid,),
        scratch=[pltpu.VMEM(table.shape, F32), pltpu.VMEM((3, rows, length), jnp.int32), pltpu.SemaphoreType.DMA((6,))],
        name="load",
    )
    parts = 4
    weight_low = call(
        weight_low_kernel, [(weight.shape, BF16)], (weight,),
        scratch=[pltpu.VMEM((parts, weight.shape[0] // parts, width), F32), pltpu.SemaphoreType.DMA((parts,))],
        name="weight_low", after=[table_low],
    )[0]
    scores = gathered(stacked(score, far_score, name="score"), "rows", row_bits[1:], "score")
    scorer, scored = call(
        functools.partial(scorer_kernel, slots_of(row_bits), near_order),
        [((EXTRA, width), BF16), ((SENT, width), F32)], *scores, *biases, weight_low, name="scorer",
    )
    far_scored = swap(scored, "rows", group_bits[0])
    table_low = stacked(table_low, name="table_low", after=[far_score])
    far_table = swap(table_low, "rows", row_bits[0])
    table_low = stacked(table_low, far_table, name="table_pair", after=[scored])
    table_low = call(
        functools.partial(table_kernel, slots_of(row_bits)), [((values, width), BF16)],
        *gathered(table_low, "rows", row_bits[1:], "table_pair"), name="table",
    )[0]
    product, turned = call(
        products_kernel, [((values, width), BF16), ((width, values), BF16)], table_low, weight_low, name="products", after=[],
    )
    tail = stacked(ids, name="tail", after=[product])
    before = lax.ppermute(tail, "tract", [(i, i + 1) for i in range(tract_count - 1)])
    planes, hot = call(
        planes_kernel, [((3 * rows, SPAN * half), F32), ((values, 2 * rows * half), BF16)], ids, name="planes", after=[product],
    )
    planes = call(halo_kernel, [(planes.shape, F32)], planes, before, name="halo")[0]
    scorers = call(pair_kernel, [((16, width), F32)], scored, far_scored, name="scored")[0]
    scorers = scorers, swap(scorers, "rows", group_bits[1])

    cot = cotangent.reshape(rows * half, width)
    *far_sent, plan, vectors = call(
        functools.partial(far_kernel, order, 3, values),
        [((values // 2, width), BF16), ((values // 2, width), BF16), ((PLANES, rows, half), F32), ((EXTRA, width), BF16)],
        *scorers, table_low, planes, scorer, cot,
        scratch=[pltpu.VMEM((OFFSETS, 8, values), F32), pltpu.VMEM((values, width), F32)], name="far",
    )
    far = call(functools.partial(block_kernel, 2, values), [((values, width), F32)], plan, cot, name="far_own")[0]
    far_sent = [swap(half_sent, "rows", copies) for half_sent in far_sent]
    far = call(
        far_sum_kernel, [((values // 2, width), BF16)] * 2, far, *far_sent,
        scratch=[pltpu.VMEM((values, width), F32)], name="far_sum",
    )
    far_others = [swap(part, "rows", 2 * copies) for part in far]
    far_product = swap(product, "rows", 2 * copies)
    near, near_sent, bias_part = call(
        functools.partial(near_kernel, [0, 1], values),
        [((values, width), F32), ((values, width), BF16), ((8, width), F32)], plan, cot,
        scratch=[pltpu.VMEM((2 * values + EXTRA, width), F32)], name="near", after=[far_product, far[1]],
    )
    near_other = swap(near_sent, "rows", copies)

    product = stacked(product, far_product, name="passed")
    products = product, swap(product, "rows", copies)
    inner = call(
        functools.partial(inner_kernel, [0, 2], values), [((REACH, rows, half), F32)],
        products[0], plan, vectors, cot, name="inner_near", cost=LONG,
    )[0]
    inner = call(
        functools.partial(inner_kernel, [1, 3], values), [((REACH, rows, half), F32)],
        products[1], plan, vectors, cot, inner, name="inner_far",
    )[0]
    sums = call(
        functools.partial(score_kernel, values), [((SMALL // 2, width), F32)], inner, plan, vectors, hot,
        scratch=[pltpu.VMEM((8, hot.shape[1] + half), F32)], name="scores",
    )[0]

    rest = [("tract", 1 << at) for at in range(PIECES.bit_length() - 1, tract_count.bit_length() - 1)]
    rest += [("rows", 1 << at) for at in range(copies.bit_length() - 1)]
    size = values // PIECES
    near = call(near_sum_kernel, [((values, width), F32)], near, near_other, name="near_sum")[0]
    sent = ((size + SMALL, width), BF16)
    send_one, send_three = call(
        functools.partial(sent_kernel, (1, 3)), [sent, sent], near, far_others[0], sums, bias_part, name="merge",
    )
    keep, send_two = call(rest_kernel, [((size, width), F32), sent], near, far_others[1], sums, bias_part, name="rest")
    sends = [send_one, send_two, send_three]
    others = [swap(send, "tract", at + 1) for at, send in enumerate(sends)]
    parts = 2

    def fill(out, which, after):
        for part in which:
            out, token = output_part(out, part, parts, order, values, products, plan, vectors, [after])
        return out, token

    out, token = fill(None, [0], keep)
    send = call(slice_kernel, [((size + SMALL, width), BF16)], keep, sends[0], *others, name="slice", after=[token])[0]
    out, token = fill(out, [1], send)
    for axis, bit in rest[:-1]:
        other = swap(send, axis, bit)
        send = call(whole_kernel, [(send.shape, BF16)], send, other, name="whole")[0]
    other = swap(send, *rest[-1])
    block, sums = call(last_kernel, [((size, width), BF16), ((SMALL // 2, width), F32)], send, other, name="last", after=[token])

    part = size // OFFSETS
    keep, send = call(
        share_kernel, [((2 * part, width), F32), ((2 * part + SMALL, width), BF16)], block, sums, weight_low, name="share",
    )
    other = swap(send, "rows", group_bits[0])
    blocks = {0: block} | {m: swap(block, "tract", m) for m in range(1, PIECES)}
    keep, send, sums = call(
        half_kernel, [((part, width), F32), ((part + SMALL, width), BF16), ((SMALL // 2, width), F32)], keep, sums, other, name="half",
    )
    other = swap(send, "rows", group_bits[1])
    table_piece, sums = call(combine_kernel, [((part, width), BF16), ((SMALL // 2, width), F32)], keep, sums, other, name="combine")
    table_pieces = {0: table_piece} | {m: swap(table_piece, "tract", m) for m in range(1, PIECES)}
    if copies > 1:
        turned = lax.dynamic_slice_in_dim(turned, rows_at % copies * (width // copies), width // copies, 0)
    weight_rows = conv_weight.shape[0]
    steps = 3
    weight_grad, score_grad, bias_grad, ranks = call(
        functools.partial(weight_kernel, list(blocks), order),
        [((weight_rows, width), F32), (shard, F32), (shard, F32), ((values, width), F32)],
        *blocks.values(), turned, vectors, sums, *scorers, *products,
        scratch=[pltpu.VMEM((values, width), BF16), pltpu.VMEM((steps, weight_rows // steps, width), F32),
                 pltpu.VMEM((OFFSETS, 8, width), F32), pltpu.VMEM((8, values), F32), pltpu.VMEM((8, shard[1]), F32),
                 pltpu.SemaphoreType.DMA((steps + 2,))],
        name="weights", final=3, copied=True,
    )
    table_grad = call(
        functools.partial(table_grad_kernel, list(table_pieces)), [(table.shape, F32)], *table_pieces.values(), ranks,
        scratch=[pltpu.VMEM((values // OFFSETS, width), F32)], name="table_grad", final=1,
    )[0]
    return out.reshape(cotangent.shape), table_grad, weight_grad, bias_grad[0], score_grad[0]


def solution(mesh):
    return jax.shard_map(
        body,
        mesh=mesh,
        in_specs=(
            P("rows", "tract"), P("rows", "tract"), P("rows", "tract"), P("rows", None),
            P("rows", None), P("rows"), P("rows"), P("rows", "tract", None),
        ),
        out_specs=(P("rows", "tract", None), P("rows", None), P("rows", None), P("rows"), P("rows")),
        check_vma=False,
    )
```

```python
import functools

import jax
import jax.numpy as jnp
from jax import lax
from jax.experimental import pallas as pl
from jax.experimental.pallas import tpu as pltpu
from jax.sharding import PartitionSpec as P

F32 = jnp.float32
BF16 = jnp.bfloat16
OFFSETS = 4
REACH = 5
SPAN = 8
EXTRA = 16
SMALL = 8
PIECES = 4
EDGE = 3
VMEM_LIMIT = 16 * 1024 * 1024
SENT = 48
LONG = 10**11
NT = (((1,), (1,)), ((), ()))
TN = (((0,), (0,)), ((), ()))
NN = (((1,), (0,)), ((), ()))


def dot(a, b, dims=NN, precision=None):
    return lax.dot_general(a, b, dims, precision=precision, preferred_element_type=F32)


def exact(a, b, dims=NN):
    return dot(a, b, dims, lax.Precision.HIGHEST)


def call(kernel, outs, *operands, scratch=(), cost=0, name=None, after=(), final=0, copied=False):
    vmem = pl.BlockSpec(memory_space=pltpu.VMEM)
    hbm = pl.BlockSpec(memory_space=pltpu.HBM)
    stored = [isinstance(operand, tuple) for operand in operands]
    held = [
        pltpu.with_memory_space_constraint(operand[0] if far else operand, pltpu.HBM if far else pltpu.VMEM)
        for operand, far in zip(operands, stored)
    ]
    count = len(operands)

    def run(*refs):
        kernel(*refs[:count], *refs[count + len(after) :])

    return pl.pallas_call(
        run if after else kernel,
        out_shape=[jax.ShapeDtypeStruct(*o) if at < final else pltpu.VMEM(*o) for at, o in enumerate(outs)],
        in_specs=[hbm if far else vmem for far in stored] + [pl.BlockSpec(memory_space=pl.ANY)] * len(after),
        out_specs=[hbm if at < final and copied else vmem for at in range(len(outs))],
        scratch_shapes=list(scratch),
        compiler_params=pltpu.CompilerParams(vmem_limit_bytes=VMEM_LIMIT),
        cost_estimate=pl.CostEstimate(flops=cost, bytes_accessed=0, transcendentals=0),
        name=name,
    )(*held, *after)


def swap(value, axis, bit):
    count = lax.axis_size(axis)
    return lax.ppermute(value, axis, [(i, i ^ bit) for i in range(count)])


def stack_kernel(*refs):
    out = refs[-1]
    rows = refs[0].shape[0]
    for at, value in enumerate(refs[:-1]):
        out[at * rows : (at + 1) * rows] = value[...]


def stacked(*values, name, after=()):
    rows, width = values[0].shape
    return call(stack_kernel, [((len(values) * rows, width), values[0].dtype)], *values, name=name, after=after)[0]


def slots_of(bits):
    order = [0]
    for bit in bits:
        order = order + [m | bit for m in order]
    return order


def gathered(value, axis, bits, name, after=()):
    for bit in bits[:-1]:
        value = stacked(value, swap(value, axis, bit), name=name, after=after)
    return value, swap(value, axis, bits[-1])


def pieces_of(refs, count):
    each = count // len(refs)
    rows = refs[0].shape[0] // each
    return [ref.at[pl.ds(at * rows, rows), :] for ref in refs for at in range(each)]


def row_index():
    return lax.axis_index("rows")


def group_index():
    return lax.axis_index("rows") // (lax.axis_size("rows") // OFFSETS)


def piece_index():
    return lax.axis_index("tract") % PIECES


def load_kernel(rows, *refs):
    sources = refs[:6]
    table_low, score_here, bias_here, together, table_here, ids_here, sems = refs[6:]
    targets = [table_here, score_here, bias_here] + [ids_here.at[at] for at in range(3)]
    copies = [pltpu.make_async_copy(source, target, sems.at[at]) for at, (source, target) in enumerate(zip(sources, targets))]
    for copy in copies:
        copy.start()
    for copy in copies:
        copy.wait()
    table_low[...] = table_here[...].astype(BF16)
    for at in range(3):
        together[at * rows : (at + 1) * rows, :] = ids_here[at].astype(F32)


def weight_low_kernel(weight, out, here, sems):
    parts, size = here.shape[:2]
    copies = [
        pltpu.make_async_copy(weight.at[pl.ds(at * size, size), :], here.at[at], sems.at[at]) for at in range(parts)
    ]
    for copy in copies:
        copy.start()
    for at in range(parts):
        copies[at].wait()
        out[at * size : (at + 1) * size, :] = here[at].astype(BF16)


def pair_kernel(first, second, out):
    out[:8] = first[:8]
    out[8:] = second[:8]


def kept_kernel(*refs):
    half = len(refs) // 2
    for value, out in zip(refs[:half], refs[half:]):
        out[...] = value[...]


def placed(parts, width):
    total = None
    for part, at in parts:
        shard = part.shape[1]
        source = lax.broadcasted_iota(jnp.int32, (shard, width), 0) + at * shard
        column = lax.broadcasted_iota(jnp.int32, (shard, width), 1)
        row = jnp.broadcast_to(part[...], (8, shard)).astype(BF16)
        got = dot(row, (source == column).astype(BF16))
        total = got if total is None else total + got
    return total


def scorer_kernel(order, near_order, *refs):
    scores = pieces_of(refs[:2], len(order))
    biases = refs[2 : 2 + len(near_order)]
    weight_low, scorer, out = refs[2 + len(near_order) :]
    width = scorer.shape[1]
    full = placed([(part, row_index() ^ m) for part, m in zip(scores, order)], width)
    bias = placed([(part, row_index() ^ m) for part, m in zip(biases, near_order)], width)
    full = jnp.concatenate([full, full], 0).astype(BF16)
    scorer[...] = full
    at = lax.broadcasted_iota(jnp.int32, bias.shape, 0)
    out[...] = jnp.zeros(out.shape, F32)
    out[:8] = jnp.where(at == 0, dot(full, weight_low[...], NT)[:8], bias)


def table_kernel(order, first, second, table_low):
    slots = pieces_of((first, second), len(order))
    rows = slots[0].shape[0]
    for slot, m in zip(slots, order):
        at = pl.multiple_of((row_index() ^ m) * rows, rows)
        table_low[pl.ds(at, rows), :] = slot[...]


def products_kernel(table_low, weight_low, product, table_turned):
    product[...] = dot(table_low[...], weight_low[...]).astype(BF16)
    table_turned[...] = table_low[...].T


def planes_kernel(ids, out, hot):
    length = ids.shape[1]
    rows = ids.shape[0] // 3
    half = length // 2
    own = ids[...].astype(BF16)
    for m in range(SPAN):
        target = 2 * lax.broadcasted_iota(jnp.int32, (length, half), 1) + 1 - m
        source = lax.broadcasted_iota(jnp.int32, (length, half), 0)
        out[:, m * half : (m + 1) * half] = dot(own, (source == target).astype(BF16))
    name = names(hot.shape[0], half)
    for side in range(2):
        for row in range(rows):
            code = out[row : row + 1, side * half : (side + 1) * half]
            hot[:, (side * rows + row) * half : (side * rows + row + 1) * half] = one_hot(name, code)


def halo_kernel(planes, before, out):
    tail = 128
    earlier = before[:, before.shape[1] - tail :].astype(BF16)
    half = planes.shape[1] // SPAN
    for m in range(SPAN):
        part = planes[:, m * half : (m + 1) * half]
        if m > 1:
            target = 2 * lax.broadcasted_iota(jnp.int32, (tail, half), 1) + 1 - m + tail
            source = lax.broadcasted_iota(jnp.int32, (tail, half), 0)
            part = part + dot(earlier, (source == target).astype(BF16))
        out[:, m * half : (m + 1) * half] = part


def names(values, lanes):
    shape = (values // 16, 16, lanes)
    return (lax.broadcasted_iota(jnp.int32, shape, 0) * 16 + lax.broadcasted_iota(jnp.int32, shape, 1)).astype(F32).astype(BF16)


def one_hot(name, code):
    code = jnp.broadcast_to(code, name.shape[1:]).astype(BF16)
    return jnp.where(name == code[None], jnp.ones(name.shape, BF16), jnp.zeros(name.shape, BF16)).reshape(-1, name.shape[2])


def gathered_edges(planes):
    rows, lanes = planes[0].shape
    lane = lax.broadcasted_iota(jnp.int32, (rows, lanes), 1)
    row = lax.broadcasted_iota(jnp.int32, (rows, lanes), 0)
    total = jnp.zeros((rows, lanes), F32)
    for side, plane in enumerate(planes):
        for at in range(EDGE):
            place = (side * rows + row) * EDGE + at
            total = total + jnp.where(lane == place, plane[:, at : at + 1], 0.0)
    return jnp.sum(total, 0, keepdims=True)


class Window:
    def __init__(self, mask):
        self.mask = mask
        self.keep, self.divide = [], []
        for side in range(2):
            keep = [self.mask[k, side] for k in range(OFFSETS)]
            counts, total = [], 0.0
            for k in range(OFFSETS):
                total = total + keep[k]
                counts.append(1.0 / jnp.maximum(total, 1.0))
            self.keep.append(keep)
            self.divide.append(counts)

    def pooled(self, side, values):
        means, total = [], 0.0
        for k in range(OFFSETS):
            total = total + self.keep[side][k] * values[side + k]
            means.append(total * self.divide[side][k])
        return means

    def spread(self, sides):
        result = [0.0] * REACH
        for side in range(2):
            carried = 0.0
            for k in reversed(range(OFFSETS)):
                carried = carried + sides[side][k] * self.divide[side][k]
                result[side + k] = result[side + k] + self.keep[side][k] * carried
        return result


def window_of(planes, rows):
    segments = [plane[rows : 2 * rows] for plane in planes]
    valid = [plane[2 * rows :] for plane in planes]
    mask = {
        (k, j): (segments[j + k] == segments[j]).astype(F32) * valid[j + k]
        for k in range(OFFSETS)
        for j in range(REACH)
    }
    return [plane[:rows] for plane in planes], Window(mask)


CODES = 0
WEIGHTS = CODES + SPAN
MASKS = WEIGHTS + OFFSETS * REACH
PROBS = MASKS + OFFSETS * REACH
AVERAGE = PROBS + 2 * OFFSETS
PLANES = AVERAGE + 1


def lookup(row, codes):
    index = codes.astype(jnp.int32)
    lanes = 128
    low = jnp.bitwise_and(index, lanes - 1)
    parts = [
        jnp.take_along_axis(
            jnp.broadcast_to(row[:, at : at + lanes], codes.shape), low, axis=1
        )
        for at in range(0, row.shape[1], lanes)
    ]
    return jnp.where(index >= lanes, parts[1], parts[0])


def packed_row(ref, plane, row):
    return jnp.broadcast_to(ref[plane, pl.ds(row, 1), :], (16, ref.shape[2])).astype(BF16)


def spread_rows(plan, k, row, values):
    lanes = plan.shape[2]
    blocks = values // 16
    name = names(values, lanes)
    total = jnp.zeros((blocks, 16, lanes), BF16)
    for j in range(REACH):
        code = packed_row(plan, CODES + k + j, row)
        weight = packed_row(plan, WEIGHTS + k * REACH + j, row)
        total = jnp.where(name == code[None], total + weight[None], total)
    return total.reshape(values, lanes)


def accumulate(plan, total_ref, ks, cot, values, extra=None):
    rows, half = plan.shape[1:]
    for chunk in range(rows // 2):
        pieces = [
            jnp.concatenate(
                [
                    spread_rows(plan, k, 2 * chunk, values),
                    spread_rows(plan, k, 2 * chunk + 1, values),
                ],
                1,
            )
            for k in ks
        ]
        if extra is not None:
            pieces.append(extra(chunk))
        left = jnp.concatenate(pieces, 0)
        part = dot(left, cot[2 * chunk * half : 2 * (chunk + 1) * half, :])
        if chunk == 0:
            total_ref[...] = part
        else:
            total_ref[...] += part


def split(value):
    high = value.astype(BF16)
    return high, (value - high.astype(F32)).astype(BF16)


def thirds(value):
    high = value.astype(BF16)
    rest = value - high.astype(F32)
    middle = rest.astype(BF16)
    return high, middle, (rest - middle.astype(F32)).astype(BF16)


def far_kernel(order, slot, values, *refs):
    scorers = pieces_of(refs[:2], len(order))
    table_low, planes, scorer, cot = refs[2:6]
    sent_first, sent_second, plan, vectors, table, total = refs[6:]
    rows = plan.shape[1]
    every = jnp.concatenate([s[:8] for s in scorers], 0)
    parts = thirds(every)
    found = dot(jnp.concatenate(parts, 0), table_low[...], NT)
    count = every.shape[0]
    found = found[:count] + found[count : 2 * count] + found[2 * count :]
    for at, m in enumerate(order):
        table[group_index() ^ m] = found[at * 8 : (at + 1) * 8]
    half = planes.shape[1] // SPAN
    codes, window = window_of([planes[:, m * half : (m + 1) * half] for m in range(SPAN)], rows)
    bias = functools.reduce(jnp.add, [s[1:2] for s in scorers])
    both = [scorer[:8].astype(F32), jnp.broadcast_to(bias, (8, bias.shape[1]))]
    vectors[...] = jnp.concatenate(both, 0).astype(BF16)
    shared = jnp.sum(both[0] * both[1], 1, keepdims=True)[:1]
    conv_scores = [shared] * REACH
    for k in range(OFFSETS):
        row = table[k, :1, :]
        for m in range(k, k + REACH):
            conv_scores[m - k] = conv_scores[m - k] + window.mask[k, m - k] * lookup(row, codes[m])
    for m in range(SPAN):
        plan[CODES + m] = codes[m]
    shares = []
    for side in range(2):
        block = window.pooled(side, conv_scores)
        top = functools.reduce(jnp.maximum, block)
        exps = [jnp.exp(b - top) for b in block]
        inverse = 1.0 / functools.reduce(jnp.add, exps)
        shares.append([e * inverse for e in exps])
        for k in range(OFFSETS):
            plan[PROBS + side * OFFSETS + k] = shares[side][k]
    mixing = [0.5 * e for e in window.spread(shares)]
    plan[AVERAGE] = functools.reduce(jnp.add, mixing)
    for k in range(OFFSETS):
        for j in range(REACH):
            plan[MASKS + k * REACH + j] = window.mask[k, j]
            plan[WEIGHTS + k * REACH + j] = window.mask[k, j] * mixing[j]
    accumulate(plan, total, [group_index() ^ slot], cot, values)
    for at, sent in enumerate((sent_first, sent_second)):
        sent[...] = total[at * values // 2 : (at + 1) * values // 2].astype(BF16)


def block_kernel(slot, values, plan, cot, out):
    accumulate(plan, out, [group_index() ^ slot], cot, values)


def average_line(plan, chunk):
    return jnp.concatenate([plan[AVERAGE, row : row + 1, :] for row in (2 * chunk, 2 * chunk + 1)], 1)


def near_kernel(slots, values, plan, cot, own, sent, bias_out, total):
    half = plan.shape[2]

    def extra(chunk):
        line = jnp.broadcast_to(average_line(plan, chunk), (EXTRA, 2 * half))
        high, low = split(line)
        at = lax.broadcasted_iota(jnp.int32, line.shape, 0)
        return jnp.where(at == 0, high.astype(F32), jnp.where(at == 1, low.astype(F32), 0.0)).astype(BF16)

    accumulate(plan, total, [group_index() ^ m for m in slots], cot, values, extra)
    own[...] = total[:values]
    sent[...] = total[values : 2 * values].astype(BF16)
    end = total[len(slots) * values :]
    bias_out[...] = jnp.broadcast_to(end[:1] + end[1:2], (8, end.shape[1]))


def inner_kernel(order, values, products, plan, vectors, cot, *refs):
    before, out = (refs[0] if len(refs) > 1 else None), refs[-1]
    rows, half = plan.shape[1:]
    blocks = values // 16
    name = names(values, half)
    left = products[...]
    if before is None:
        left = jnp.concatenate([left, vectors[...]], 0)
    for chunk in range(rows // 2):
        here = cot[2 * chunk * half : 2 * (chunk + 1) * half, :]
        both = dot(left, here, NT)
        found = {}
        for place, m in enumerate(order):
            k = group_index() ^ m
            each = both[place * values : (place + 1) * values].astype(BF16)
            for side in range(2):
                row = 2 * chunk + side
                mine = each[:, side * half : (side + 1) * half].reshape(blocks, 16, half)
                for j in range(REACH):
                    code = packed_row(plan, CODES + k + j, row)
                    picked = jnp.zeros((16, half), BF16)
                    for at in range(blocks):
                        picked = jnp.where(name[at] == code, mine[at], picked)
                    mask = plan[MASKS + k * REACH + j, row : row + 1, :]
                    found[j, side] = found.get((j, side), 0.0) + picked.astype(F32) * mask
        for side in range(2):
            row = 2 * chunk + side
            for j in range(REACH):
                if before is None:
                    at = len(order) * values + 8
                    start = both[at : at + 1, side * half : (side + 1) * half]
                else:
                    start = before[j, row : row + 1, :]
                out[j, row : row + 1, :] = jnp.sum(found[j, side], 0, keepdims=True) + start


def score_kernel(values, inner_ref, plan, vectors, hot, out, flat):
    rows, half = plan.shape[1:]
    window = Window({(k, j): plan[MASKS + k * REACH + j] for k in range(OFFSETS) for j in range(REACH)})
    inner_rows = [0.5 * inner_ref[j] for j in range(REACH)]
    sides = []
    for side in range(2):
        inner = window.pooled(side, inner_rows)
        share = [plan[PROBS + side * OFFSETS + k] for k in range(OFFSETS)]
        mean = functools.reduce(jnp.add, [s * i for s, i in zip(share, inner)])
        sides.append([s * (i - mean) for s, i in zip(share, inner)])
    grads = window.spread(sides)
    overall = jnp.sum(jnp.sum(functools.reduce(jnp.add, grads), 1, keepdims=True), 0, keepdims=True)
    lane = lax.broadcasted_iota(jnp.int32, (rows, half), 1)
    flat[...] = jnp.zeros(flat.shape, F32)
    for k in range(OFFSETS):
        edges = []
        for side in range(2):
            inside = jnp.zeros((rows, half), F32)
            edge = jnp.zeros((rows, half), F32)
            for m in range(side, SPAN, 2):
                if not 0 <= m - k < REACH:
                    continue
                value = grads[m - k] * window.mask[k, m - k]
                steps = m // 2
                if steps:
                    inside = inside + jnp.where(lane < half - steps, pltpu.roll(value, half - steps, 1), 0.0)
                    moved = pltpu.roll(value, EDGE - steps, 1) if steps < EDGE else value
                    edge = edge + jnp.where((lane >= EDGE - steps) & (lane < EDGE), moved, 0.0)
                else:
                    inside = inside + value
            for row in range(rows):
                at = (side * rows + row) * half
                flat[k : k + 1, at : at + half] = inside[row : row + 1, :]
            edges.append(edge)
        flat[k : k + 1, 2 * rows * half :] = gathered_edges(edges)
    high, low = split(flat[...])
    both = jnp.concatenate([high.astype(F32), low.astype(F32)], 0).astype(BF16)
    edge = gathered_edges([plan[CODES + SPAN - 2 + side] for side in range(2)])
    lines = dot(both[:, : hot.shape[1]], hot[...], NT) + dot(both[:, hot.shape[1] :], one_hot(names(values, half), edge), NT)
    lines = lines[:8] + lines[8:]
    width = vectors.shape[1]
    out[...] = jnp.zeros(out.shape, F32)
    out[:1] = overall * vectors[:1].astype(F32)
    for k in range(OFFSETS + 1):
        row, lane = small_place(k, values, width)
        part = lines[k : k + 1] if k < OFFSETS else jnp.broadcast_to(overall, (1, values))
        out[row : row + 1, lane : lane + values] = part


def output_kernel(order, values, chunks_here, *refs):
    products = pieces_of(refs[:2], len(order))
    plan, vectors = refs[2:4]
    out, token, staged, sems = refs[-4:]
    token[...] = jnp.zeros(token.shape, F32)
    half = plan.shape[2]
    step = 2 * half
    biases = vectors[8:].astype(F32)
    at = lax.broadcasted_iota(jnp.int32, (8, step), 0)
    first = lax.broadcasted_iota(jnp.int32, biases.shape, 0)
    biases = jnp.where(first < 2, biases, 0.0)
    copies = []
    for place, chunk in enumerate(chunks_here):
        high, low = split(jnp.broadcast_to(average_line(plan, chunk), (8, step)))
        both = jnp.where(at == 0, high.astype(F32), jnp.where(at == 1, low.astype(F32), 0.0))
        total = dot(both, biases, TN)
        for slot, m in zip(products, order):
            k = group_index() ^ m
            left = jnp.concatenate([spread_rows(plan, k, row, values) for row in (2 * chunk, 2 * chunk + 1)], 1)
            total = total + dot(left, slot[...], TN)
        staged[place * step : (place + 1) * step, :] = total.astype(BF16)
        copies.append(
            pltpu.make_async_copy(
                staged.at[pl.ds(place * step, step), :], out.at[pl.ds(chunk * step, step), :], sems.at[place]
            )
        )
        copies[-1].start()
    for copy in copies:
        copy.wait()


def output_part(before, part, parts, order, values, products, plan, vectors, after):
    rows, half = plan.shape[1:]
    width = vectors.shape[1]
    each = rows // 2 // parts
    operands = [pltpu.with_memory_space_constraint(x, pltpu.VMEM) for x in (*products, plan, vectors)]
    operands += [] if before is None else [pltpu.with_memory_space_constraint(before, pltpu.HBM)]
    vmem = pl.BlockSpec(memory_space=pltpu.VMEM)
    elsewhere = pl.BlockSpec(memory_space=pl.ANY)
    count = len(products) + 2
    chunks_here = range(part * each, (part + 1) * each)

    def run(*refs):
        output_kernel(order, values, chunks_here, *refs[:count], *refs[-4:])

    return pl.pallas_call(
        run,
        out_shape=[jax.ShapeDtypeStruct((rows * half, width), BF16), pltpu.VMEM((8, 128), F32)],
        in_specs=[vmem] * count + [elsewhere] * (len(operands) - count + len(after)),
        out_specs=[elsewhere, vmem],
        input_output_aliases={} if before is None else {count: 0},
        scratch_shapes=[pltpu.VMEM((2 * half * each, width), BF16), pltpu.SemaphoreType.DMA((each,))],
        compiler_params=pltpu.CompilerParams(vmem_limit_bytes=VMEM_LIMIT),
        cost_estimate=pl.CostEstimate(flops=0, bytes_accessed=0, transcendentals=0),
        name="output",
    )(*operands, *after)


def chunks(values, piece, group):
    block = values // OFFSETS
    size = block // PIECES
    for actual in range(PIECES):
        for offset in range(OFFSETS):
            at = pl.multiple_of((piece ^ actual) * OFFSETS * size + (group ^ offset) * size, size)
            yield offset * block + actual * size, at, size


def pack(rows):
    high, low = split(rows)
    return jnp.concatenate([high.astype(F32), low.astype(F32)], 0).astype(BF16)


def small_place(at, values, width):
    per = width // values
    return 1 + at // per, at % per * values


def small_pack(rows):
    high, low = split(rows)
    return jnp.concatenate([high.astype(F32), low.astype(F32)], 0).astype(BF16)


def small_unpack(block):
    return block[: SMALL // 2].astype(F32) + block[SMALL // 2 :].astype(F32)


def small_sums(sums, bias):
    first = lax.broadcasted_iota(jnp.int32, sums.shape, 0) == 0
    return small_pack(sums[...] + jnp.where(first, bias[: sums.shape[0]], 0.0))


def sent_kernel(slots, near, far, sums, bias, *sends):
    size = near.shape[0] // PIECES
    for at, (slot, send) in enumerate(zip(slots, sends)):
        total = near[slot * size : (slot + 1) * size] + far[at * size : (at + 1) * size].astype(F32)
        send[:size] = total.astype(BF16)
        send[size:] = small_sums(sums, bias)


def rest_kernel(near, far, sums, bias, keep, send):
    size = keep.shape[0]
    keep[...] = near[:size] + far[:size].astype(F32)
    send[:size] = (near[2 * size : 3 * size] + far[size:].astype(F32)).astype(BF16)
    send[size:] = small_sums(sums, bias)


def slice_kernel(keep, own, *refs):
    others, send = refs[:-1], refs[-1]
    part = keep.shape[0]
    total = functools.reduce(jnp.add, [keep[...]] + [o[:part].astype(F32) for o in others])
    small = [small_unpack(x[part:]) for x in (own, *others)]
    while len(small) > 1:
        small = [small[at] + small[at + 1] for at in range(0, len(small), 2)]
    send[:part] = total.astype(BF16)
    send[part:] = small_pack(small[0])


def whole_kernel(mine, other, send):
    rows = mine.shape[0] - SMALL
    send[:rows] = (mine[:rows].astype(F32) + other[:rows].astype(F32)).astype(BF16)
    send[rows:] = small_pack(small_unpack(mine[rows:]) + small_unpack(other[rows:]))


def last_kernel(mine, other, block, sums):
    rows = block.shape[0]
    block[...] = (mine[:rows].astype(F32) + other[:rows].astype(F32)).astype(BF16)
    sums[...] = small_unpack(mine[rows:]) + small_unpack(other[rows:])


def turned_kernel(value, out):
    out[...] = value[...].T


def share_kernel(block, sums, weight_turned, keep, send):
    product = dot(block[...], weight_turned[...])
    rows = keep.shape[0]
    keep[...] = product[:rows]
    send[:rows] = product[rows:].astype(BF16)
    send[rows:] = small_pack(sums[...])


def half_kernel(keep, sums, other, rest, send, total):
    rows = rest.shape[0]
    both = keep[...] + other[: 2 * rows].astype(F32)
    total[...] = sums[...] + small_unpack(other[2 * rows :])
    rest[...] = both[:rows]
    send[:rows] = both[rows:].astype(BF16)
    send[rows:] = small_pack(total[...])


def combine_kernel(keep, sums, other, out, total):
    rows = keep.shape[0]
    out[...] = (keep[...] + other[:rows].astype(F32)).astype(BF16)
    total[...] = sums[...] + small_unpack(other[rows:])


def added_kernel(mine, other, out):
    out[...] = (mine[...].astype(F32) + other[...].astype(F32)).astype(out.dtype)


def arrange(source, target, group):
    values = source.shape[0]
    for at, place, size in chunks(values, piece_index(), group):
        target[pl.ds(place, size), :] = source[at : at + size]


def far_sum_kernel(mine, one, two, first, second, total):
    rows = one.shape[0]
    halves = [mine[:rows] + one[...].astype(F32), mine[rows:] + two[...].astype(F32)]
    arrange(jnp.concatenate(halves, 0), total, group_index() ^ 2)
    size = total.shape[0] // PIECES
    for out, slots in ((first, (1, 3)), (second, (0, 2))):
        for at, slot in enumerate(slots):
            out[at * size : (at + 1) * size] = total[slot * size : (slot + 1) * size].astype(BF16)


def near_sum_kernel(near, other, total):
    arrange(near[...] + other[...].astype(F32), total, group_index())


def weight_kernel(order, offsets, *refs):
    slots = refs[: len(order)]
    turned, vectors, sums = refs[len(order) : len(order) + 3]
    scorers = pieces_of(refs[len(order) + 3 : len(order) + 5], len(offsets))
    products = pieces_of(refs[len(order) + 5 : len(order) + 7], len(offsets))
    out, score_out, bias_out, ranks, full, staged, rows_ref, lines, ends, sems = refs[len(order) + 7 :]
    values, width = full.shape
    group, piece = group_index(), piece_index()
    block = values // OFFSETS
    size = block // PIECES
    copies = []

    def send(source, target):
        copies.append(pltpu.make_async_copy(source, target, sems.at[len(copies)]))
        copies[-1].start()

    for m, slot in zip(order, slots):
        for offset in range(OFFSETS):
            at = (group ^ offset) * block + (piece ^ m) * size
            full[pl.ds(pl.multiple_of(at, size), size), :] = slot[offset * size : (offset + 1) * size]
    for k in range(OFFSETS):
        row, lane = small_place(k, values, width)
        lines[k : k + 1] = sums[row : row + 1, lane : lane + values]
    line = lines[pl.ds(group, 1), :]
    scores = vectors[:1].astype(F32)
    first = lax.broadcasted_iota(jnp.int32, (8, values), 0) == 0
    both = pack(jnp.where(first, jnp.broadcast_to(line, first.shape), 0.0))
    parts, step = staged.shape[:2]
    for part in range(parts):
        here = turned[part * step : (part + 1) * step]
        through = dot(here, both, NT)
        staged[part] = dot(here, full[...]) + (through[:, :1] + through[:, 8:9]) * scores
        send(staged.at[part], out.at[pl.ds(part * step, step), :])
    shard = score_out.shape[1]
    source = lax.broadcasted_iota(jnp.int32, (width, shard), 0)
    column = lax.broadcasted_iota(jnp.int32, (width, shard), 1) + row_index() * shard
    here = (source == column).astype(BF16)
    row, lane = small_place(OFFSETS, values, width)
    score_grad = sums[row : row + 1, lane : lane + 1] * vectors[8:9].astype(F32)
    for product, m in zip(products, offsets):
        got = dot(pack(jnp.broadcast_to(lines[pl.ds(group ^ m, 1), :], (8, values))), product[...])
        score_grad = score_grad + got[:1] + got[8:9]
    at = lax.broadcasted_iota(jnp.int32, (8, width), 0)
    small = jnp.where(at == 0, score_grad, jnp.where(at == 1, sums[:1], 0.0))
    ends[...] = functools.reduce(jnp.add, [dot(part, here) for part in thirds(small)])
    send(ends.at[pl.ds(0, 1), :], score_out)
    send(ends.at[pl.ds(1, 1), :], bias_out)
    for scorer, m in zip(scorers, offsets):
        rows_ref[group ^ m] = scorer[...]
    high, low = split(lines[:OFFSETS])
    right_high, right_low = split(jnp.concatenate([rows_ref[k, :1] for k in range(OFFSETS)], 0))
    left = jnp.concatenate([x.astype(F32) for x in (high, low, high, low)], 0).astype(BF16)
    right = jnp.concatenate([x.astype(F32) for x in (right_high, right_high, right_low, right_low)], 0).astype(BF16)
    ranks[...] = dot(left, right, TN)
    for copy in copies:
        copy.wait()


def table_grad_kernel(order, *refs):
    slots, (ranks, out, table) = refs[: len(order)], refs[len(order) :]
    group, block = group_index(), table.shape[0]
    for slot, m in zip(slots, order):
        size = slot.shape[0]
        at = pl.multiple_of((piece_index() ^ m) * size, size)
        table[pl.ds(at, size), :] = slot[...].astype(F32) + ranks[pl.ds(pl.multiple_of(group * block, block) + at, size), :]
    rows = out.shape[0]
    inside = row_index() * rows - group * block
    out[...] = table[pl.ds(pl.multiple_of(inside, rows), rows), :]


def bits_of(count):
    return [1 << at for at in reversed(range(count.bit_length() - 1))]


def body(byte_values, segment_ids, valid, table, conv_weight, conv_bias, score_weight, cotangent):
    rows_count, tract_count = lax.axis_size("rows"), lax.axis_size("tract")
    rows_at = lax.axis_index("rows")
    values, width = table.shape[0] * rows_count, table.shape[1]
    rows, length = byte_values.shape
    half = length // 2
    copies = rows_count // OFFSETS
    order = [0, 2, 1, 3]
    group_bits = [2 * copies, copies]
    near_bits = [bit for bit in bits_of(rows_count) if bit < copies]

    row_bits = bits_of(rows_count)
    far_score = swap(score_weight[None], "rows", row_bits[0])
    near_order = slots_of(near_bits)
    biases = [conv_bias[None]]
    for bit in near_bits:
        biases = biases + [swap(value, "rows", bit) for value in biases]
    weight = conv_weight
    if copies > 1:
        near_by = [[g * copies + c for c in range(copies)] for g in range(OFFSETS)]
        weight = lax.all_gather(conv_weight, "rows", axis=0, tiled=True, axis_index_groups=near_by)
    shard = (1, conv_bias.shape[0])
    table_low, score, biases[0], ids = call(
        functools.partial(load_kernel, rows),
        [(table.shape, BF16), (shard, F32), (shard, F32), ((3 * rows, length), F32)],
        (table,), (score_weight[None],), (conv_bias[None],), (byte_values,), (segment_ids,), (valid,),
        scratch=[pltpu.VMEM(table.shape, F32), pltpu.VMEM((3, rows, length), jnp.int32), pltpu.SemaphoreType.DMA((6,))],
        name="load",
    )
    parts = 4
    weight_low = call(
        weight_low_kernel, [(weight.shape, BF16)], (weight,),
        scratch=[pltpu.VMEM((parts, weight.shape[0] // parts, width), F32), pltpu.SemaphoreType.DMA((parts,))],
        name="weight_low", after=[table_low],
    )[0]
    scores = gathered(stacked(score, far_score, name="score"), "rows", row_bits[1:], "score")
    scorer, scored = call(
        functools.partial(scorer_kernel, slots_of(row_bits), near_order),
        [((EXTRA, width), BF16), ((SENT, width), F32)], *scores, *biases, weight_low, name="scorer",
    )
    far_scored = swap(scored, "rows", group_bits[0])
    table_low = stacked(table_low, name="table_low", after=[far_score])
    far_table = swap(table_low, "rows", row_bits[0])
    table_low = stacked(table_low, far_table, name="table_pair", after=[scored])
    table_low = call(
        functools.partial(table_kernel, slots_of(row_bits)), [((values, width), BF16)],
        *gathered(table_low, "rows", row_bits[1:], "table_pair"), name="table",
    )[0]
    product, turned = call(
        products_kernel, [((values, width), BF16), ((width, values), BF16)], table_low, weight_low, name="products", after=[],
    )
    tail = stacked(ids, name="tail", after=[product])
    before = lax.ppermute(tail, "tract", [(i, i + 1) for i in range(tract_count - 1)])
    planes, hot = call(
        planes_kernel, [((3 * rows, SPAN * half), F32), ((values, 2 * rows * half), BF16)], ids, name="planes", after=[product],
    )
    planes = call(halo_kernel, [(planes.shape, F32)], planes, before, name="halo")[0]
    scorers = call(pair_kernel, [((16, width), F32)], scored, far_scored, name="scored")[0]
    scorers = scorers, swap(scorers, "rows", group_bits[1])

    cot = cotangent.reshape(rows * half, width)
    *far_sent, plan, vectors = call(
        functools.partial(far_kernel, order, 3, values),
        [((values // 2, width), BF16), ((values // 2, width), BF16), ((PLANES, rows, half), F32), ((EXTRA, width), BF16)],
        *scorers, table_low, planes, scorer, cot,
        scratch=[pltpu.VMEM((OFFSETS, 8, values), F32), pltpu.VMEM((values, width), F32)], name="far",
    )
    far = call(functools.partial(block_kernel, 2, values), [((values, width), F32)], plan, cot, name="far_own")[0]
    far_sent = [swap(half_sent, "rows", copies) for half_sent in far_sent]
    far = call(
        far_sum_kernel, [((values // 2, width), BF16)] * 2, far, *far_sent,
        scratch=[pltpu.VMEM((values, width), F32)], name="far_sum",
    )
    far_others = [swap(part, "rows", 2 * copies) for part in far]
    far_product = swap(product, "rows", 2 * copies)
    near, near_sent, bias_part = call(
        functools.partial(near_kernel, [0, 1], values),
        [((values, width), F32), ((values, width), BF16), ((8, width), F32)], plan, cot,
        scratch=[pltpu.VMEM((2 * values + EXTRA, width), F32)], name="near", after=[far_product, far[1]],
    )
    near_other = swap(near_sent, "rows", copies)

    product = stacked(product, far_product, name="passed")
    products = product, swap(product, "rows", copies)
    inner = call(
        functools.partial(inner_kernel, [0, 2], values), [((REACH, rows, half), F32)],
        products[0], plan, vectors, cot, name="inner_near", cost=LONG,
    )[0]
    inner = call(
        functools.partial(inner_kernel, [1, 3], values), [((REACH, rows, half), F32)],
        products[1], plan, vectors, cot, inner, name="inner_far",
    )[0]
    sums = call(
        functools.partial(score_kernel, values), [((SMALL // 2, width), F32)], inner, plan, vectors, hot,
        scratch=[pltpu.VMEM((8, hot.shape[1] + half), F32)], name="scores",
    )[0]

    rest = [("tract", 1 << at) for at in range(PIECES.bit_length() - 1, tract_count.bit_length() - 1)]
    rest += [("rows", 1 << at) for at in range(copies.bit_length() - 1)]
    size = values // PIECES
    near = call(near_sum_kernel, [((values, width), F32)], near, near_other, name="near_sum")[0]
    sent = ((size + SMALL, width), BF16)
    send_one, send_three = call(
        functools.partial(sent_kernel, (1, 3)), [sent, sent], near, far_others[0], sums, bias_part, name="merge",
    )
    keep, send_two = call(rest_kernel, [((size, width), F32), sent], near, far_others[1], sums, bias_part, name="rest")
    sends = [send_one, send_two, send_three]
    others = [swap(send, "tract", at + 1) for at, send in enumerate(sends)]
    parts = 2

    def fill(out, which, after):
        for part in which:
            out, token = output_part(out, part, parts, order, values, products, plan, vectors, [after])
        return out, token

    out, token = fill(None, [0], keep)
    send = call(slice_kernel, [((size + SMALL, width), BF16)], keep, sends[2], *others, name="slice", after=[token])[0]
    out, token = fill(out, [1], send)
    weight_turned = call(turned_kernel, [(weight_low.shape, BF16)], weight_low, name="turned", after=[token])[0]
    for axis, bit in rest[:-1]:
        other = swap(send, axis, bit)
        send = call(whole_kernel, [(send.shape, BF16)], send, other, name="whole")[0]
    other = swap(send, *rest[-1])
    block, sums = call(last_kernel, [((size, width), BF16), ((SMALL // 2, width), F32)], send, other, name="last", after=[token])

    part = size // OFFSETS
    keep, send = call(
        share_kernel, [((2 * part, width), F32), ((2 * part + SMALL, width), BF16)], block, sums, weight_turned, name="share",
    )
    other = swap(send, "rows", group_bits[0])
    blocks = {0: block} | {m: swap(block, "tract", m) for m in range(1, PIECES)}
    keep, send, sums = call(
        half_kernel, [((part, width), F32), ((part + SMALL, width), BF16), ((SMALL // 2, width), F32)], keep, sums, other, name="half",
    )
    other = swap(send, "rows", group_bits[1])
    table_piece, sums = call(combine_kernel, [((part, width), BF16), ((SMALL // 2, width), F32)], keep, sums, other, name="combine")
    table_pieces = {0: table_piece} | {m: swap(table_piece, "tract", m) for m in range(1, PIECES)}
    if copies > 1:
        turned = lax.dynamic_slice_in_dim(turned, rows_at % copies * (width // copies), width // copies, 0)
    weight_rows = conv_weight.shape[0]
    steps = 3
    weight_grad, score_grad, bias_grad, ranks = call(
        functools.partial(weight_kernel, list(blocks), order),
        [((weight_rows, width), F32), (shard, F32), (shard, F32), ((values, width), F32)],
        *blocks.values(), turned, vectors, sums, *scorers, *products,
        scratch=[pltpu.VMEM((values, width), BF16), pltpu.VMEM((steps, weight_rows // steps, width), F32),
                 pltpu.VMEM((OFFSETS, 8, width), F32), pltpu.VMEM((8, values), F32), pltpu.VMEM((8, shard[1]), F32),
                 pltpu.SemaphoreType.DMA((steps + 2,))],
        name="weights", final=3, copied=True,
    )
    table_grad = call(
        functools.partial(table_grad_kernel, list(table_pieces)), [(table.shape, F32)], *table_pieces.values(), ranks,
        scratch=[pltpu.VMEM((values // OFFSETS, width), F32)], name="table_grad", final=1,
    )[0]
    return out.reshape(cotangent.shape), table_grad, weight_grad, bias_grad[0], score_grad[0]


def solution(mesh):
    return jax.shard_map(
        body,
        mesh=mesh,
        in_specs=(
            P("rows", "tract"), P("rows", "tract"), P("rows", "tract"), P("rows", None),
            P("rows", None), P("rows"), P("rows"), P("rows", "tract", None),
        ),
        out_specs=(P("rows", "tract", None), P("rows", None), P("rows", None), P("rows"), P("rows")),
        check_vma=False,
    )
```

```python
import functools

import jax
import jax.numpy as jnp
from jax import lax
from jax.experimental import pallas as pl
from jax.experimental.pallas import tpu as pltpu
from jax.sharding import PartitionSpec as P

F32 = jnp.float32
BF16 = jnp.bfloat16
OFFSETS = 4
REACH = 5
SPAN = 8
EXTRA = 16
SMALL = 8
PIECES = 4
EDGE = 3
VMEM_LIMIT = 16 * 1024 * 1024
SENT = 48
LONG = 10**11
NT = (((1,), (1,)), ((), ()))
TN = (((0,), (0,)), ((), ()))
NN = (((1,), (0,)), ((), ()))


def dot(a, b, dims=NN, precision=None):
    return lax.dot_general(a, b, dims, precision=precision, preferred_element_type=F32)


def exact(a, b, dims=NN):
    return dot(a, b, dims, lax.Precision.HIGHEST)


def call(kernel, outs, *operands, scratch=(), cost=0, name=None, after=(), final=0, copied=False):
    vmem = pl.BlockSpec(memory_space=pltpu.VMEM)
    hbm = pl.BlockSpec(memory_space=pltpu.HBM)
    stored = [isinstance(operand, tuple) for operand in operands]
    held = [
        pltpu.with_memory_space_constraint(operand[0] if far else operand, pltpu.HBM if far else pltpu.VMEM)
        for operand, far in zip(operands, stored)
    ]
    count = len(operands)

    def run(*refs):
        kernel(*refs[:count], *refs[count + len(after) :])

    return pl.pallas_call(
        run if after else kernel,
        out_shape=[jax.ShapeDtypeStruct(*o) if at < final else pltpu.VMEM(*o) for at, o in enumerate(outs)],
        in_specs=[hbm if far else vmem for far in stored] + [pl.BlockSpec(memory_space=pl.ANY)] * len(after),
        out_specs=[hbm if at < final and copied else vmem for at in range(len(outs))],
        scratch_shapes=list(scratch),
        compiler_params=pltpu.CompilerParams(vmem_limit_bytes=VMEM_LIMIT),
        cost_estimate=pl.CostEstimate(flops=cost, bytes_accessed=0, transcendentals=0),
        name=name,
    )(*held, *after)


def swap(value, axis, bit):
    count = lax.axis_size(axis)
    return lax.ppermute(value, axis, [(i, i ^ bit) for i in range(count)])


def stack_kernel(*refs):
    out = refs[-1]
    rows = refs[0].shape[0]
    for at, value in enumerate(refs[:-1]):
        out[at * rows : (at + 1) * rows] = value[...].astype(out.dtype)


def stacked(*values, name, after=()):
    rows, width = values[0].shape
    return call(stack_kernel, [((len(values) * rows, width), values[0].dtype)], *values, name=name, after=after)[0]


def slots_of(bits):
    order = [0]
    for bit in bits:
        order = order + [m | bit for m in order]
    return order


def gathered(value, axis, bits, name, after=()):
    for bit in bits[:-1]:
        value = stacked(value, swap(value, axis, bit), name=name, after=after)
    return value, swap(value, axis, bits[-1])


def pieces_of(refs, count):
    each = count // len(refs)
    rows = refs[0].shape[0] // each
    return [ref.at[pl.ds(at * rows, rows), :] for ref in refs for at in range(each)]


def row_index():
    return lax.axis_index("rows")


def group_index():
    return lax.axis_index("rows") // (lax.axis_size("rows") // OFFSETS)


def piece_index():
    return lax.axis_index("tract") % PIECES


def load_kernel(rows, *refs):
    sources = refs[:6]
    table_low, score_here, bias_here, together, table_here, ids_here, sems = refs[6:]
    targets = [table_here, score_here, bias_here] + [ids_here.at[at] for at in range(3)]
    copies = [pltpu.make_async_copy(source, target, sems.at[at]) for at, (source, target) in enumerate(zip(sources, targets))]
    for copy in copies:
        copy.start()
    for copy in copies:
        copy.wait()
    table_low[...] = table_here[...].astype(BF16)
    for at in range(3):
        together[at * rows : (at + 1) * rows, :] = ids_here[at].astype(F32)


def weight_low_kernel(weight, out, here, sems):
    parts, size = here.shape[:2]
    copies = [
        pltpu.make_async_copy(weight.at[pl.ds(at * size, size), :], here.at[at], sems.at[at]) for at in range(parts)
    ]
    for copy in copies:
        copy.start()
    for at in range(parts):
        copies[at].wait()
        out[at * size : (at + 1) * size, :] = here[at].astype(BF16)


def pair_kernel(first, second, out):
    out[:8] = first[:8]
    out[8:] = second[:8]


def kept_kernel(*refs):
    half = len(refs) // 2
    for value, out in zip(refs[:half], refs[half:]):
        out[...] = value[...]


def placed(parts, width):
    total = None
    for part, at in parts:
        shard = part.shape[1]
        source = lax.broadcasted_iota(jnp.int32, (shard, width), 0) + at * shard
        column = lax.broadcasted_iota(jnp.int32, (shard, width), 1)
        row = jnp.broadcast_to(part[...], (8, shard)).astype(BF16)
        got = dot(row, (source == column).astype(BF16))
        total = got if total is None else total + got
    return total


def scorer_kernel(order, near_order, *refs):
    scores = pieces_of(refs[:2], len(order))
    biases = refs[2 : 2 + len(near_order)]
    weight_low, scorer, out = refs[2 + len(near_order) :]
    width = scorer.shape[1]
    full = placed([(part, row_index() ^ m) for part, m in zip(scores, order)], width)
    bias = placed([(part, row_index() ^ m) for part, m in zip(biases, near_order)], width)
    full = jnp.concatenate([full, full], 0).astype(BF16)
    scorer[...] = full
    at = lax.broadcasted_iota(jnp.int32, bias.shape, 0)
    out[...] = jnp.zeros(out.shape, F32)
    out[:8] = jnp.where(at == 0, dot(full, weight_low[...], NT)[:8], bias)


def table_kernel(order, first, second, table_low):
    slots = pieces_of((first, second), len(order))
    rows = slots[0].shape[0]
    for slot, m in zip(slots, order):
        at = pl.multiple_of((row_index() ^ m) * rows, rows)
        table_low[pl.ds(at, rows), :] = slot[...]


def products_kernel(table_low, weight_low, product, table_turned):
    product[...] = dot(table_low[...], weight_low[...]).astype(BF16)
    table_turned[...] = table_low[...].T


def planes_kernel(ids, out, hot):
    length = ids.shape[1]
    rows = ids.shape[0] // 3
    half = length // 2
    own = ids[...].astype(BF16)
    for m in range(SPAN):
        target = 2 * lax.broadcasted_iota(jnp.int32, (length, half), 1) + 1 - m
        source = lax.broadcasted_iota(jnp.int32, (length, half), 0)
        out[:, m * half : (m + 1) * half] = dot(own, (source == target).astype(BF16))
    name = names(hot.shape[0], half)
    for side in range(2):
        for row in range(rows):
            code = out[row : row + 1, side * half : (side + 1) * half]
            hot[:, (side * rows + row) * half : (side * rows + row + 1) * half] = one_hot(name, code)


def halo_kernel(planes, before, out):
    tail = 128
    earlier = before[:, before.shape[1] - tail :].astype(BF16)
    half = planes.shape[1] // SPAN
    for m in range(SPAN):
        part = planes[:, m * half : (m + 1) * half]
        if m > 1:
            target = 2 * lax.broadcasted_iota(jnp.int32, (tail, half), 1) + 1 - m + tail
            source = lax.broadcasted_iota(jnp.int32, (tail, half), 0)
            part = part + dot(earlier, (source == target).astype(BF16))
        out[:, m * half : (m + 1) * half] = part


def names(values, lanes):
    shape = (values // 16, 16, lanes)
    return (lax.broadcasted_iota(jnp.int32, shape, 0) * 16 + lax.broadcasted_iota(jnp.int32, shape, 1)).astype(F32).astype(BF16)


def one_hot(name, code):
    code = jnp.broadcast_to(code, name.shape[1:]).astype(BF16)
    return jnp.where(name == code[None], jnp.ones(name.shape, BF16), jnp.zeros(name.shape, BF16)).reshape(-1, name.shape[2])


def gathered_edges(planes):
    rows, lanes = planes[0].shape
    lane = lax.broadcasted_iota(jnp.int32, (rows, lanes), 1)
    row = lax.broadcasted_iota(jnp.int32, (rows, lanes), 0)
    total = jnp.zeros((rows, lanes), F32)
    for side, plane in enumerate(planes):
        for at in range(EDGE):
            place = (side * rows + row) * EDGE + at
            total = total + jnp.where(lane == place, plane[:, at : at + 1], 0.0)
    return jnp.sum(total, 0, keepdims=True)


class Window:
    def __init__(self, mask):
        self.mask = mask
        self.keep, self.divide = [], []
        for side in range(2):
            keep = [self.mask[k, side] for k in range(OFFSETS)]
            counts, total = [], 0.0
            for k in range(OFFSETS):
                total = total + keep[k]
                counts.append(1.0 / jnp.maximum(total, 1.0))
            self.keep.append(keep)
            self.divide.append(counts)

    def pooled(self, side, values):
        means, total = [], 0.0
        for k in range(OFFSETS):
            total = total + self.keep[side][k] * values[side + k]
            means.append(total * self.divide[side][k])
        return means

    def spread(self, sides):
        result = [0.0] * REACH
        for side in range(2):
            carried = 0.0
            for k in reversed(range(OFFSETS)):
                carried = carried + sides[side][k] * self.divide[side][k]
                result[side + k] = result[side + k] + self.keep[side][k] * carried
        return result


def window_of(planes, rows):
    segments = [plane[rows : 2 * rows] for plane in planes]
    valid = [plane[2 * rows :] for plane in planes]
    mask = {
        (k, j): (segments[j + k] == segments[j]).astype(F32) * valid[j + k]
        for k in range(OFFSETS)
        for j in range(REACH)
    }
    return [plane[:rows] for plane in planes], Window(mask)


CODES = 0
WEIGHTS = CODES + SPAN
MASKS = WEIGHTS + OFFSETS * REACH
PROBS = MASKS + OFFSETS * REACH
AVERAGE = PROBS + 2 * OFFSETS
PLANES = AVERAGE + 1


def lookup(row, codes):
    index = codes.astype(jnp.int32)
    lanes = 128
    low = jnp.bitwise_and(index, lanes - 1)
    parts = [
        jnp.take_along_axis(
            jnp.broadcast_to(row[:, at : at + lanes], codes.shape), low, axis=1
        )
        for at in range(0, row.shape[1], lanes)
    ]
    return jnp.where(index >= lanes, parts[1], parts[0])


def packed_row(ref, plane, row):
    return jnp.broadcast_to(ref[plane, pl.ds(row, 1), :], (16, ref.shape[2])).astype(BF16)


def spread_rows(plan, k, row, values):
    lanes = plan.shape[2]
    blocks = values // 16
    name = names(values, lanes)
    total = jnp.zeros((blocks, 16, lanes), BF16)
    for j in range(REACH):
        code = packed_row(plan, CODES + k + j, row)
        weight = packed_row(plan, WEIGHTS + k * REACH + j, row)
        total = jnp.where(name == code[None], total + weight[None], total)
    return total.reshape(values, lanes)


def accumulate(plan, total_ref, ks, cot, values, extra=None):
    rows, half = plan.shape[1:]
    for chunk in range(rows // 2):
        pieces = [
            jnp.concatenate(
                [
                    spread_rows(plan, k, 2 * chunk, values),
                    spread_rows(plan, k, 2 * chunk + 1, values),
                ],
                1,
            )
            for k in ks
        ]
        if extra is not None:
            pieces.append(extra(chunk))
        left = jnp.concatenate(pieces, 0)
        part = dot(left, cot[2 * chunk * half : 2 * (chunk + 1) * half, :])
        if chunk == 0:
            total_ref[...] = part
        else:
            total_ref[...] += part


def split(value):
    high = value.astype(BF16)
    return high, (value - high.astype(F32)).astype(BF16)


def thirds(value):
    high = value.astype(BF16)
    rest = value - high.astype(F32)
    middle = rest.astype(BF16)
    return high, middle, (rest - middle.astype(F32)).astype(BF16)


def far_kernel(order, slot, values, *refs):
    scorers = pieces_of(refs[:2], len(order))
    table_low, planes, scorer, cot = refs[2:6]
    sent_first, sent_second, plan, vectors, table, total = refs[6:]
    rows = plan.shape[1]
    every = jnp.concatenate([s[:8] for s in scorers], 0)
    parts = thirds(every)
    found = dot(jnp.concatenate(parts, 0), table_low[...], NT)
    count = every.shape[0]
    found = found[:count] + found[count : 2 * count] + found[2 * count :]
    for at, m in enumerate(order):
        table[group_index() ^ m] = found[at * 8 : (at + 1) * 8]
    half = planes.shape[1] // SPAN
    codes, window = window_of([planes[:, m * half : (m + 1) * half] for m in range(SPAN)], rows)
    bias = functools.reduce(jnp.add, [s[1:2] for s in scorers])
    both = [scorer[:8].astype(F32), jnp.broadcast_to(bias, (8, bias.shape[1]))]
    vectors[...] = jnp.concatenate(both, 0).astype(BF16)
    shared = jnp.sum(both[0] * both[1], 1, keepdims=True)[:1]
    conv_scores = [shared] * REACH
    for k in range(OFFSETS):
        row = table[k, :1, :]
        for m in range(k, k + REACH):
            conv_scores[m - k] = conv_scores[m - k] + window.mask[k, m - k] * lookup(row, codes[m])
    for m in range(SPAN):
        plan[CODES + m] = codes[m]
    shares = []
    for side in range(2):
        block = window.pooled(side, conv_scores)
        top = functools.reduce(jnp.maximum, block)
        exps = [jnp.exp(b - top) for b in block]
        inverse = 1.0 / functools.reduce(jnp.add, exps)
        shares.append([e * inverse for e in exps])
        for k in range(OFFSETS):
            plan[PROBS + side * OFFSETS + k] = shares[side][k]
    mixing = [0.5 * e for e in window.spread(shares)]
    plan[AVERAGE] = functools.reduce(jnp.add, mixing)
    for k in range(OFFSETS):
        for j in range(REACH):
            plan[MASKS + k * REACH + j] = window.mask[k, j]
            plan[WEIGHTS + k * REACH + j] = window.mask[k, j] * mixing[j]
    accumulate(plan, total, [group_index() ^ slot], cot, values)
    for at, sent in enumerate((sent_first, sent_second)):
        sent[...] = total[at * values // 2 : (at + 1) * values // 2].astype(BF16)


def block_kernel(slot, values, plan, cot, out):
    accumulate(plan, out, [group_index() ^ slot], cot, values)


def average_line(plan, chunk):
    return jnp.concatenate([plan[AVERAGE, row : row + 1, :] for row in (2 * chunk, 2 * chunk + 1)], 1)


def near_kernel(slots, values, plan, cot, own, sent, bias_out, total):
    half = plan.shape[2]

    def extra(chunk):
        line = jnp.broadcast_to(average_line(plan, chunk), (EXTRA, 2 * half))
        high, low = split(line)
        at = lax.broadcasted_iota(jnp.int32, line.shape, 0)
        return jnp.where(at == 0, high.astype(F32), jnp.where(at == 1, low.astype(F32), 0.0)).astype(BF16)

    accumulate(plan, total, [group_index() ^ m for m in slots], cot, values, extra)
    own[...] = total[:values]
    sent[...] = total[values : 2 * values].astype(BF16)
    end = total[len(slots) * values :]
    bias_out[...] = jnp.broadcast_to(end[:1] + end[1:2], (8, end.shape[1]))


def inner_kernel(order, values, products, plan, vectors, cot, *refs):
    before, out = (refs[0] if len(refs) > 1 else None), refs[-1]
    rows, half = plan.shape[1:]
    blocks = values // 16
    name = names(values, half)
    left = products[...]
    if before is None:
        left = jnp.concatenate([left, vectors[...]], 0)
    for chunk in range(rows // 2):
        here = cot[2 * chunk * half : 2 * (chunk + 1) * half, :]
        both = dot(left, here, NT)
        found = {}
        for place, m in enumerate(order):
            k = group_index() ^ m
            each = both[place * values : (place + 1) * values].astype(BF16)
            for side in range(2):
                row = 2 * chunk + side
                mine = each[:, side * half : (side + 1) * half].reshape(blocks, 16, half)
                for j in range(REACH):
                    code = packed_row(plan, CODES + k + j, row)
                    picked = jnp.zeros((16, half), BF16)
                    for at in range(blocks):
                        picked = jnp.where(name[at] == code, mine[at], picked)
                    mask = plan[MASKS + k * REACH + j, row : row + 1, :]
                    found[j, side] = found.get((j, side), 0.0) + picked.astype(F32) * mask
        for side in range(2):
            row = 2 * chunk + side
            for j in range(REACH):
                if before is None:
                    at = len(order) * values + 8
                    start = both[at : at + 1, side * half : (side + 1) * half]
                else:
                    start = before[j, row : row + 1, :]
                out[j, row : row + 1, :] = jnp.sum(found[j, side], 0, keepdims=True) + start


def score_kernel(values, inner_ref, plan, vectors, hot, out, flat):
    rows, half = plan.shape[1:]
    window = Window({(k, j): plan[MASKS + k * REACH + j] for k in range(OFFSETS) for j in range(REACH)})
    inner_rows = [0.5 * inner_ref[j] for j in range(REACH)]
    sides = []
    for side in range(2):
        inner = window.pooled(side, inner_rows)
        share = [plan[PROBS + side * OFFSETS + k] for k in range(OFFSETS)]
        mean = functools.reduce(jnp.add, [s * i for s, i in zip(share, inner)])
        sides.append([s * (i - mean) for s, i in zip(share, inner)])
    grads = window.spread(sides)
    overall = jnp.sum(jnp.sum(functools.reduce(jnp.add, grads), 1, keepdims=True), 0, keepdims=True)
    lane = lax.broadcasted_iota(jnp.int32, (rows, half), 1)
    flat[...] = jnp.zeros(flat.shape, F32)
    for k in range(OFFSETS):
        edges = []
        for side in range(2):
            inside = jnp.zeros((rows, half), F32)
            edge = jnp.zeros((rows, half), F32)
            for m in range(side, SPAN, 2):
                if not 0 <= m - k < REACH:
                    continue
                value = grads[m - k] * window.mask[k, m - k]
                steps = m // 2
                if steps:
                    inside = inside + jnp.where(lane < half - steps, pltpu.roll(value, half - steps, 1), 0.0)
                    moved = pltpu.roll(value, EDGE - steps, 1) if steps < EDGE else value
                    edge = edge + jnp.where((lane >= EDGE - steps) & (lane < EDGE), moved, 0.0)
                else:
                    inside = inside + value
            for row in range(rows):
                at = (side * rows + row) * half
                flat[k : k + 1, at : at + half] = inside[row : row + 1, :]
            edges.append(edge)
        flat[k : k + 1, 2 * rows * half :] = gathered_edges(edges)
    high, low = split(flat[...])
    both = jnp.concatenate([high.astype(F32), low.astype(F32)], 0).astype(BF16)
    edge = gathered_edges([plan[CODES + SPAN - 2 + side] for side in range(2)])
    lines = dot(both[:, : hot.shape[1]], hot[...], NT) + dot(both[:, hot.shape[1] :], one_hot(names(values, half), edge), NT)
    lines = lines[:8] + lines[8:]
    width = vectors.shape[1]
    out[...] = jnp.zeros(out.shape, F32)
    out[:1] = overall * vectors[:1].astype(F32)
    for k in range(OFFSETS + 1):
        row, lane = small_place(k, values, width)
        part = lines[k : k + 1] if k < OFFSETS else jnp.broadcast_to(overall, (1, values))
        out[row : row + 1, lane : lane + values] = part


def output_kernel(order, values, chunks_here, *refs):
    products = pieces_of(refs[:2], len(order))
    plan, vectors = refs[2:4]
    out, token, staged, sems = refs[-4:]
    token[...] = jnp.zeros(token.shape, F32)
    half = plan.shape[2]
    step = 2 * half
    biases = vectors[8:].astype(F32)
    at = lax.broadcasted_iota(jnp.int32, (8, step), 0)
    first = lax.broadcasted_iota(jnp.int32, biases.shape, 0)
    biases = jnp.where(first < 2, biases, 0.0)
    copies = []
    for place, chunk in enumerate(chunks_here):
        high, low = split(jnp.broadcast_to(average_line(plan, chunk), (8, step)))
        both = jnp.where(at == 0, high.astype(F32), jnp.where(at == 1, low.astype(F32), 0.0))
        total = dot(both, biases, TN)
        for slot, m in zip(products, order):
            k = group_index() ^ m
            left = jnp.concatenate([spread_rows(plan, k, row, values) for row in (2 * chunk, 2 * chunk + 1)], 1)
            total = total + dot(left, slot[...], TN)
        staged[place * step : (place + 1) * step, :] = total.astype(BF16)
        copies.append(
            pltpu.make_async_copy(
                staged.at[pl.ds(place * step, step), :], out.at[pl.ds(chunk * step, step), :], sems.at[place]
            )
        )
        copies[-1].start()
    for copy in copies:
        copy.wait()


def output_part(before, part, parts, order, values, products, plan, vectors, after):
    rows, half = plan.shape[1:]
    width = vectors.shape[1]
    each = rows // 2 // parts
    operands = [pltpu.with_memory_space_constraint(x, pltpu.VMEM) for x in (*products, plan, vectors)]
    operands += [] if before is None else [pltpu.with_memory_space_constraint(before, pltpu.HBM)]
    vmem = pl.BlockSpec(memory_space=pltpu.VMEM)
    elsewhere = pl.BlockSpec(memory_space=pl.ANY)
    count = len(products) + 2
    chunks_here = range(part * each, (part + 1) * each)

    def run(*refs):
        output_kernel(order, values, chunks_here, *refs[:count], *refs[-4:])

    return pl.pallas_call(
        run,
        out_shape=[jax.ShapeDtypeStruct((rows * half, width), BF16), pltpu.VMEM((8, 128), F32)],
        in_specs=[vmem] * count + [elsewhere] * (len(operands) - count + len(after)),
        out_specs=[elsewhere, vmem],
        input_output_aliases={} if before is None else {count: 0},
        scratch_shapes=[pltpu.VMEM((2 * half * each, width), BF16), pltpu.SemaphoreType.DMA((each,))],
        compiler_params=pltpu.CompilerParams(vmem_limit_bytes=VMEM_LIMIT),
        cost_estimate=pl.CostEstimate(flops=0, bytes_accessed=0, transcendentals=0),
        name="output",
    )(*operands, *after)


def chunks(values, piece, group):
    block = values // OFFSETS
    size = block // PIECES
    for actual in range(PIECES):
        for offset in range(OFFSETS):
            at = pl.multiple_of((piece ^ actual) * OFFSETS * size + (group ^ offset) * size, size)
            yield offset * block + actual * size, at, size


def pack(rows):
    high, low = split(rows)
    return jnp.concatenate([high.astype(F32), low.astype(F32)], 0).astype(BF16)


def small_place(at, values, width):
    per = width // values
    return 1 + at // per, at % per * values


def small_pack(rows):
    high, low = split(rows)
    return jnp.concatenate([high.astype(F32), low.astype(F32)], 0).astype(BF16)


def small_unpack(block):
    return block[: SMALL // 2].astype(F32) + block[SMALL // 2 :].astype(F32)


def small_sums(sums, bias):
    first = lax.broadcasted_iota(jnp.int32, sums.shape, 0) == 0
    return small_pack(sums[...] + jnp.where(first, bias[: sums.shape[0]], 0.0))


def sent_kernel(slots, near, far, sums, bias, *sends):
    size = near.shape[0] // PIECES
    for at, (slot, send) in enumerate(zip(slots, sends)):
        total = near[slot * size : (slot + 1) * size] + far[at * size : (at + 1) * size].astype(F32)
        send[:size] = total.astype(BF16)
        send[size:] = small_sums(sums, bias)


def rest_kernel(near, far, sums, bias, keep, send):
    size = keep.shape[0]
    keep[...] = near[:size] + far[:size].astype(F32)
    send[:size] = (near[2 * size : 3 * size] + far[size:].astype(F32)).astype(BF16)
    send[size:] = small_sums(sums, bias)


def slice_kernel(keep, own, *refs):
    others, send = refs[:-1], refs[-1]
    part = keep.shape[0]
    total = functools.reduce(jnp.add, [keep[...]] + [o[:part].astype(F32) for o in others])
    small = [small_unpack(x[part:]) for x in (own, *others)]
    while len(small) > 1:
        small = [small[at] + small[at + 1] for at in range(0, len(small), 2)]
    send[:part] = total.astype(BF16)
    send[part:] = small_pack(small[0])


def whole_kernel(mine, other, send):
    rows = mine.shape[0] - SMALL
    send[:rows] = (mine[:rows].astype(F32) + other[:rows].astype(F32)).astype(BF16)
    send[rows:] = small_pack(small_unpack(mine[rows:]) + small_unpack(other[rows:]))


def last_kernel(mine, other, block, sums):
    rows = block.shape[0]
    block[...] = (mine[:rows].astype(F32) + other[:rows].astype(F32)).astype(BF16)
    sums[...] = small_unpack(mine[rows:]) + small_unpack(other[rows:])


def turned_kernel(value, out):
    out[...] = value[...].T


def share_kernel(block, sums, weight_turned, keep, send):
    product = dot(block[...], weight_turned[...])
    rows = keep.shape[0]
    keep[...] = product[:rows]
    send[:rows] = product[rows:].astype(BF16)
    send[rows:] = small_pack(sums[...])


def half_kernel(keep, sums, other, rest, send, total):
    rows = rest.shape[0]
    both = keep[...] + other[: 2 * rows].astype(F32)
    total[...] = sums[...] + small_unpack(other[2 * rows :])
    rest[...] = both[:rows]
    send[:rows] = both[rows:].astype(BF16)
    send[rows:] = small_pack(total[...])


def combine_kernel(keep, sums, other, out, total):
    rows = keep.shape[0]
    out[...] = (keep[...] + other[:rows].astype(F32)).astype(BF16)
    total[...] = sums[...] + small_unpack(other[rows:])


def added_kernel(mine, other, out):
    out[...] = (mine[...].astype(F32) + other[...].astype(F32)).astype(out.dtype)


def arrange(source, target, group):
    values = source.shape[0]
    for at, place, size in chunks(values, piece_index(), group):
        target[pl.ds(place, size), :] = source[at : at + size]


def far_sum_kernel(mine, one, two, first, second, total):
    rows = one.shape[0]
    halves = [mine[:rows] + one[...].astype(F32), mine[rows:] + two[...].astype(F32)]
    arrange(jnp.concatenate(halves, 0), total, group_index() ^ 2)
    size = total.shape[0] // PIECES
    for out, slots in ((first, (1, 3)), (second, (0, 2))):
        for at, slot in enumerate(slots):
            out[at * size : (at + 1) * size] = total[slot * size : (slot + 1) * size].astype(BF16)


def near_sum_kernel(near, other, total):
    arrange(near[...] + other[...].astype(F32), total, group_index())


def weight_kernel(order, offsets, *refs):
    slots = refs[: len(order)]
    turned, vectors, sums = refs[len(order) : len(order) + 3]
    scorers = pieces_of(refs[len(order) + 3 : len(order) + 5], len(offsets))
    products = pieces_of(refs[len(order) + 5 : len(order) + 7], len(offsets))
    out, score_out, bias_out, ranks, full, staged, rows_ref, lines, ends, sems = refs[len(order) + 7 :]
    values, width = full.shape
    group, piece = group_index(), piece_index()
    block = values // OFFSETS
    size = block // PIECES
    copies = []

    def send(source, target):
        copies.append(pltpu.make_async_copy(source, target, sems.at[len(copies)]))
        copies[-1].start()

    for m, slot in zip(order, slots):
        for offset in range(OFFSETS):
            at = (group ^ offset) * block + (piece ^ m) * size
            full[pl.ds(pl.multiple_of(at, size), size), :] = slot[offset * size : (offset + 1) * size]
    for k in range(OFFSETS):
        row, lane = small_place(k, values, width)
        lines[k : k + 1] = sums[row : row + 1, lane : lane + values]
    line = lines[pl.ds(group, 1), :]
    scores = vectors[:1].astype(F32)
    first = lax.broadcasted_iota(jnp.int32, (8, values), 0) == 0
    both = pack(jnp.where(first, jnp.broadcast_to(line, first.shape), 0.0))
    parts, step = staged.shape[:2]
    for part in range(parts):
        here = turned[part * step : (part + 1) * step]
        through = dot(here, both, NT)
        staged[part] = dot(here, full[...]) + (through[:, :1] + through[:, 8:9]) * scores
        send(staged.at[part], out.at[pl.ds(part * step, step), :])
    shard = score_out.shape[1]
    source = lax.broadcasted_iota(jnp.int32, (width, shard), 0)
    column = lax.broadcasted_iota(jnp.int32, (width, shard), 1) + row_index() * shard
    here = (source == column).astype(BF16)
    row, lane = small_place(OFFSETS, values, width)
    score_grad = sums[row : row + 1, lane : lane + 1] * vectors[8:9].astype(F32)
    for product, m in zip(products, offsets):
        got = dot(pack(jnp.broadcast_to(lines[pl.ds(group ^ m, 1), :], (8, values))), product[...])
        score_grad = score_grad + got[:1] + got[8:9]
    at = lax.broadcasted_iota(jnp.int32, (8, width), 0)
    small = jnp.where(at == 0, score_grad, jnp.where(at == 1, sums[:1], 0.0))
    ends[...] = functools.reduce(jnp.add, [dot(part, here) for part in thirds(small)])
    send(ends.at[pl.ds(0, 1), :], score_out)
    send(ends.at[pl.ds(1, 1), :], bias_out)
    for scorer, m in zip(scorers, offsets):
        rows_ref[group ^ m] = scorer[...]
    high, low = split(lines[:OFFSETS])
    right_high, right_low = split(jnp.concatenate([rows_ref[k, :1] for k in range(OFFSETS)], 0))
    left = jnp.concatenate([x.astype(F32) for x in (high, low, high, low)], 0).astype(BF16)
    right = jnp.concatenate([x.astype(F32) for x in (right_high, right_high, right_low, right_low)], 0).astype(BF16)
    ranks[...] = dot(left, right, TN)
    for copy in copies:
        copy.wait()


def table_grad_kernel(order, *refs):
    slots, (ranks, out, table) = refs[: len(order)], refs[len(order) :]
    group, block = group_index(), table.shape[0]
    for slot, m in zip(slots, order):
        size = slot.shape[0]
        at = pl.multiple_of((piece_index() ^ m) * size, size)
        table[pl.ds(at, size), :] = slot[...].astype(F32) + ranks[pl.ds(pl.multiple_of(group * block, block) + at, size), :]
    rows = out.shape[0]
    inside = row_index() * rows - group * block
    out[...] = table[pl.ds(pl.multiple_of(inside, rows), rows), :]


def bits_of(count):
    return [1 << at for at in reversed(range(count.bit_length() - 1))]


def body(byte_values, segment_ids, valid, table, conv_weight, conv_bias, score_weight, cotangent):
    rows_count, tract_count = lax.axis_size("rows"), lax.axis_size("tract")
    rows_at = lax.axis_index("rows")
    values, width = table.shape[0] * rows_count, table.shape[1]
    rows, length = byte_values.shape
    half = length // 2
    copies = rows_count // OFFSETS
    order = [0, 2, 1, 3]
    group_bits = [2 * copies, copies]
    near_bits = [bit for bit in bits_of(rows_count) if bit < copies]

    row_bits = bits_of(rows_count)
    far_score = swap(score_weight[None], "rows", row_bits[0])
    near_order = slots_of(near_bits)
    biases = [conv_bias[None]]
    for bit in near_bits:
        biases = biases + [swap(value, "rows", bit) for value in biases]
    weight = conv_weight
    if copies > 1:
        near_by = [[g * copies + c for c in range(copies)] for g in range(OFFSETS)]
        weight = lax.all_gather(conv_weight, "rows", axis=0, tiled=True, axis_index_groups=near_by)
    shard = (1, conv_bias.shape[0])
    table_low, score, biases[0], ids = call(
        functools.partial(load_kernel, rows),
        [(table.shape, BF16), (shard, F32), (shard, F32), ((3 * rows, length), F32)],
        (table,), (score_weight[None],), (conv_bias[None],), (byte_values,), (segment_ids,), (valid,),
        scratch=[pltpu.VMEM(table.shape, F32), pltpu.VMEM((3, rows, length), jnp.int32), pltpu.SemaphoreType.DMA((6,))],
        name="load", cost=LONG,
    )
    parts = 4
    weight_low = call(
        weight_low_kernel, [(weight.shape, BF16)], (weight,),
        scratch=[pltpu.VMEM((parts, weight.shape[0] // parts, width), F32), pltpu.SemaphoreType.DMA((parts,))],
        name="weight_low", after=[table_low],
    )[0]
    scores = gathered(stacked(score, far_score, name="score"), "rows", row_bits[1:], "score")
    scorer, scored = call(
        functools.partial(scorer_kernel, slots_of(row_bits), near_order),
        [((EXTRA, width), BF16), ((SENT, width), F32)], *scores, *biases, weight_low, name="scorer",
    )
    far_scored = swap(scored, "rows", group_bits[0])
    far_table = swap(table, "rows", row_bits[0])
    table_low = call(
        stack_kernel, [((2 * table.shape[0], width), BF16)], table_low, far_table, name="table_pair", after=[scored],
    )[0]
    table_low = call(
        functools.partial(table_kernel, slots_of(row_bits)), [((values, width), BF16)],
        *gathered(table_low, "rows", row_bits[1:], "table_pair"), name="table",
    )[0]
    product, turned = call(
        products_kernel, [((values, width), BF16), ((width, values), BF16)], table_low, weight_low, name="products", after=[],
    )
    tail = stacked(ids, name="tail", after=[product])
    before = lax.ppermute(tail, "tract", [(i, i + 1) for i in range(tract_count - 1)])
    planes, hot = call(
        planes_kernel, [((3 * rows, SPAN * half), F32), ((values, 2 * rows * half), BF16)], ids, name="planes", after=[product],
    )
    planes = call(halo_kernel, [(planes.shape, F32)], planes, before, name="halo")[0]
    scorers = call(pair_kernel, [((16, width), F32)], scored, far_scored, name="scored")[0]
    scorers = scorers, swap(scorers, "rows", group_bits[1])

    cot = cotangent.reshape(rows * half, width)
    *far_sent, plan, vectors = call(
        functools.partial(far_kernel, order, 3, values),
        [((values // 2, width), BF16), ((values // 2, width), BF16), ((PLANES, rows, half), F32), ((EXTRA, width), BF16)],
        *scorers, table_low, planes, scorer, cot,
        scratch=[pltpu.VMEM((OFFSETS, 8, values), F32), pltpu.VMEM((values, width), F32)], name="far",
    )
    far = call(functools.partial(block_kernel, 2, values), [((values, width), F32)], plan, cot, name="far_own")[0]
    far_sent = [swap(half_sent, "rows", copies) for half_sent in far_sent]
    far = call(
        far_sum_kernel, [((values // 2, width), BF16)] * 2, far, *far_sent,
        scratch=[pltpu.VMEM((values, width), F32)], name="far_sum",
    )
    far_others = [swap(part, "rows", 2 * copies) for part in far]
    far_product = swap(product, "rows", 2 * copies)
    near, near_sent, bias_part = call(
        functools.partial(near_kernel, [0, 1], values),
        [((values, width), F32), ((values, width), BF16), ((8, width), F32)], plan, cot,
        scratch=[pltpu.VMEM((2 * values + EXTRA, width), F32)], name="near", after=[far_product, far[1]],
    )
    near_other = swap(near_sent, "rows", copies)

    product = stacked(product, far_product, name="passed")
    products = product, swap(product, "rows", copies)
    inner = call(
        functools.partial(inner_kernel, [0, 2], values), [((REACH, rows, half), F32)],
        products[0], plan, vectors, cot, name="inner_near", cost=LONG,
    )[0]
    inner = call(
        functools.partial(inner_kernel, [1, 3], values), [((REACH, rows, half), F32)],
        products[1], plan, vectors, cot, inner, name="inner_far",
    )[0]
    sums = call(
        functools.partial(score_kernel, values), [((SMALL // 2, width), F32)], inner, plan, vectors, hot,
        scratch=[pltpu.VMEM((8, hot.shape[1] + half), F32)], name="scores",
    )[0]

    rest = [("tract", 1 << at) for at in range(PIECES.bit_length() - 1, tract_count.bit_length() - 1)]
    rest += [("rows", 1 << at) for at in range(copies.bit_length() - 1)]
    size = values // PIECES
    near = call(near_sum_kernel, [((values, width), F32)], near, near_other, name="near_sum")[0]
    sent = ((size + SMALL, width), BF16)
    send_one, send_three = call(
        functools.partial(sent_kernel, (1, 3)), [sent, sent], near, far_others[0], sums, bias_part, name="merge",
    )
    keep, send_two = call(rest_kernel, [((size, width), F32), sent], near, far_others[1], sums, bias_part, name="rest")
    sends = [send_one, send_two, send_three]
    others = [swap(send, "tract", at + 1) for at, send in enumerate(sends)]
    parts = 2

    def fill(out, which, after):
        for part in which:
            out, token = output_part(out, part, parts, order, values, products, plan, vectors, [after])
        return out, token

    out, token = fill(None, [0], keep)
    send = call(slice_kernel, [((size + SMALL, width), BF16)], keep, sends[2], *others, name="slice", after=[token])[0]
    out, token = fill(out, [1], send)
    weight_turned = call(turned_kernel, [(weight_low.shape, BF16)], weight_low, name="turned", after=[token])[0]
    for axis, bit in rest[:-1]:
        other = swap(send, axis, bit)
        send = call(whole_kernel, [(send.shape, BF16)], send, other, name="whole")[0]
    other = swap(send, *rest[-1])
    block, sums = call(last_kernel, [((size, width), BF16), ((SMALL // 2, width), F32)], send, other, name="last", after=[token])

    part = size // OFFSETS
    keep, send = call(
        share_kernel, [((2 * part, width), F32), ((2 * part + SMALL, width), BF16)], block, sums, weight_turned, name="share",
    )
    other = swap(send, "rows", group_bits[0])
    blocks = {0: block} | {m: swap(block, "tract", m) for m in range(1, PIECES)}
    keep, send, sums = call(
        half_kernel, [((part, width), F32), ((part + SMALL, width), BF16), ((SMALL // 2, width), F32)], keep, sums, other, name="half",
    )
    other = swap(send, "rows", group_bits[1])
    table_piece, sums = call(combine_kernel, [((part, width), BF16), ((SMALL // 2, width), F32)], keep, sums, other, name="combine")
    table_pieces = {0: table_piece} | {m: swap(table_piece, "tract", m) for m in range(1, PIECES)}
    if copies > 1:
        turned = lax.dynamic_slice_in_dim(turned, rows_at % copies * (width // copies), width // copies, 0)
    weight_rows = conv_weight.shape[0]
    steps = 3
    weight_grad, score_grad, bias_grad, ranks = call(
        functools.partial(weight_kernel, list(blocks), order),
        [((weight_rows, width), F32), (shard, F32), (shard, F32), ((values, width), F32)],
        *blocks.values(), turned, vectors, sums, *scorers, *products,
        scratch=[pltpu.VMEM((values, width), BF16), pltpu.VMEM((steps, weight_rows // steps, width), F32),
                 pltpu.VMEM((OFFSETS, 8, width), F32), pltpu.VMEM((8, values), F32), pltpu.VMEM((8, shard[1]), F32),
                 pltpu.SemaphoreType.DMA((steps + 2,))],
        name="weights", final=3, copied=True,
    )
    table_grad = call(
        functools.partial(table_grad_kernel, list(table_pieces)), [(table.shape, F32)], *table_pieces.values(), ranks,
        scratch=[pltpu.VMEM((values // OFFSETS, width), F32)], name="table_grad", final=1,
    )[0]
    return out.reshape(cotangent.shape), table_grad, weight_grad, bias_grad[0], score_grad[0]


def solution(mesh):
    return jax.shard_map(
        body,
        mesh=mesh,
        in_specs=(
            P("rows", "tract"), P("rows", "tract"), P("rows", "tract"), P("rows", None),
            P("rows", None), P("rows"), P("rows"), P("rows", "tract", None),
        ),
        out_specs=(P("rows", "tract", None), P("rows", None), P("rows", None), P("rows"), P("rows")),
        check_vma=False,
    )
```

```python
import functools

import jax
import jax.numpy as jnp
from jax import lax
from jax.experimental import pallas as pl
from jax.experimental.pallas import tpu as pltpu
from jax.sharding import PartitionSpec as P

F32 = jnp.float32
BF16 = jnp.bfloat16
OFFSETS = 4
REACH = 5
SPAN = 8
EXTRA = 16
SMALL = 8
PIECES = 4
EDGE = 3
VMEM_LIMIT = 16 * 1024 * 1024
SENT = 48
LONG = 10**11
NT = (((1,), (1,)), ((), ()))
TN = (((0,), (0,)), ((), ()))
NN = (((1,), (0,)), ((), ()))


def dot(a, b, dims=NN, precision=None):
    return lax.dot_general(a, b, dims, precision=precision, preferred_element_type=F32)


def exact(a, b, dims=NN):
    return dot(a, b, dims, lax.Precision.HIGHEST)


def call(kernel, outs, *operands, scratch=(), cost=0, name=None, after=(), final=0, copied=False):
    vmem = pl.BlockSpec(memory_space=pltpu.VMEM)
    hbm = pl.BlockSpec(memory_space=pltpu.HBM)
    stored = [isinstance(operand, tuple) for operand in operands]
    held = [
        pltpu.with_memory_space_constraint(operand[0] if far else operand, pltpu.HBM if far else pltpu.VMEM)
        for operand, far in zip(operands, stored)
    ]
    count = len(operands)

    def run(*refs):
        kernel(*refs[:count], *refs[count + len(after) :])

    return pl.pallas_call(
        run if after else kernel,
        out_shape=[jax.ShapeDtypeStruct(*o) if at < final else pltpu.VMEM(*o) for at, o in enumerate(outs)],
        in_specs=[hbm if far else vmem for far in stored] + [pl.BlockSpec(memory_space=pl.ANY)] * len(after),
        out_specs=[hbm if at < final and copied else vmem for at in range(len(outs))],
        scratch_shapes=list(scratch),
        compiler_params=pltpu.CompilerParams(vmem_limit_bytes=VMEM_LIMIT),
        cost_estimate=pl.CostEstimate(flops=cost, bytes_accessed=0, transcendentals=0),
        name=name,
    )(*held, *after)


def swap(value, axis, bit):
    count = lax.axis_size(axis)
    return lax.ppermute(value, axis, [(i, i ^ bit) for i in range(count)])


def stack_kernel(*refs):
    out = refs[-1]
    rows = refs[0].shape[0]
    for at, value in enumerate(refs[:-1]):
        out[at * rows : (at + 1) * rows] = value[...].astype(out.dtype)


def stacked(*values, name, after=()):
    rows, width = values[0].shape
    return call(stack_kernel, [((len(values) * rows, width), values[0].dtype)], *values, name=name, after=after)[0]


def slots_of(bits):
    order = [0]
    for bit in bits:
        order = order + [m | bit for m in order]
    return order


def gathered(value, axis, bits, name, after=()):
    for bit in bits[:-1]:
        value = stacked(value, swap(value, axis, bit), name=name, after=after)
    return value, swap(value, axis, bits[-1])


def pieces_of(refs, count):
    each = count // len(refs)
    rows = refs[0].shape[0] // each
    return [ref.at[pl.ds(at * rows, rows), :] for ref in refs for at in range(each)]


def row_index():
    return lax.axis_index("rows")


def group_index():
    return lax.axis_index("rows") // (lax.axis_size("rows") // OFFSETS)


def piece_index():
    return lax.axis_index("tract") % PIECES


def load_kernel(rows, *refs):
    sources = refs[:6]
    table_low, score_here, bias_here, together, table_here, ids_here, sems = refs[6:]
    targets = [table_here, score_here, bias_here] + [ids_here.at[at] for at in range(3)]
    copies = [pltpu.make_async_copy(source, target, sems.at[at]) for at, (source, target) in enumerate(zip(sources, targets))]
    for copy in copies:
        copy.start()
    for copy in copies:
        copy.wait()
    table_low[...] = table_here[...].astype(BF16)
    for at in range(3):
        together[at * rows : (at + 1) * rows, :] = ids_here[at].astype(F32)


def weight_low_kernel(weight, out, here, sems):
    parts, size = here.shape[:2]
    copies = [
        pltpu.make_async_copy(weight.at[pl.ds(at * size, size), :], here.at[at], sems.at[at]) for at in range(parts)
    ]
    for copy in copies:
        copy.start()
    for at in range(parts):
        copies[at].wait()
        out[at * size : (at + 1) * size, :] = here[at].astype(BF16)


def pair_kernel(first, second, out):
    out[:8] = first[:8]
    out[8:] = second[:8]


def kept_kernel(*refs):
    half = len(refs) // 2
    for value, out in zip(refs[:half], refs[half:]):
        out[...] = value[...]


def placed(parts, width):
    total = None
    for part, at in parts:
        shard = part.shape[1]
        source = lax.broadcasted_iota(jnp.int32, (shard, width), 0) + at * shard
        column = lax.broadcasted_iota(jnp.int32, (shard, width), 1)
        row = jnp.broadcast_to(part[...], (8, shard)).astype(BF16)
        got = dot(row, (source == column).astype(BF16))
        total = got if total is None else total + got
    return total


def scorer_kernel(order, near_order, *refs):
    scores = pieces_of(refs[:2], len(order))
    biases = refs[2 : 2 + len(near_order)]
    weight_low, scorer, out = refs[2 + len(near_order) :]
    width = scorer.shape[1]
    full = placed([(part, row_index() ^ m) for part, m in zip(scores, order)], width)
    bias = placed([(part, row_index() ^ m) for part, m in zip(biases, near_order)], width)
    full = jnp.concatenate([full, full], 0).astype(BF16)
    scorer[...] = full
    at = lax.broadcasted_iota(jnp.int32, bias.shape, 0)
    out[...] = jnp.zeros(out.shape, F32)
    out[:8] = jnp.where(at == 0, dot(full, weight_low[...], NT)[:8], bias)


def table_kernel(order, first, second, table_low):
    slots = pieces_of((first, second), len(order))
    rows = slots[0].shape[0]
    for slot, m in zip(slots, order):
        at = pl.multiple_of((row_index() ^ m) * rows, rows)
        table_low[pl.ds(at, rows), :] = slot[...]


def products_kernel(table_low, weight_low, product, table_turned):
    product[...] = dot(table_low[...], weight_low[...]).astype(BF16)
    table_turned[...] = table_low[...].T


def planes_kernel(ids, out, hot):
    length = ids.shape[1]
    rows = ids.shape[0] // 3
    half = length // 2
    own = ids[...].astype(BF16)
    for m in range(SPAN):
        target = 2 * lax.broadcasted_iota(jnp.int32, (length, half), 1) + 1 - m
        source = lax.broadcasted_iota(jnp.int32, (length, half), 0)
        out[:, m * half : (m + 1) * half] = dot(own, (source == target).astype(BF16))
    name = names(hot.shape[0], half)
    for side in range(2):
        for row in range(rows):
            code = out[row : row + 1, side * half : (side + 1) * half]
            hot[:, (side * rows + row) * half : (side * rows + row + 1) * half] = one_hot(name, code)


def halo_kernel(planes, before, out):
    tail = 128
    earlier = before[:, before.shape[1] - tail :].astype(BF16)
    half = planes.shape[1] // SPAN
    for m in range(SPAN):
        part = planes[:, m * half : (m + 1) * half]
        if m > 1:
            target = 2 * lax.broadcasted_iota(jnp.int32, (tail, half), 1) + 1 - m + tail
            source = lax.broadcasted_iota(jnp.int32, (tail, half), 0)
            part = part + dot(earlier, (source == target).astype(BF16))
        out[:, m * half : (m + 1) * half] = part


def names(values, lanes):
    shape = (values // 16, 16, lanes)
    return (lax.broadcasted_iota(jnp.int32, shape, 0) * 16 + lax.broadcasted_iota(jnp.int32, shape, 1)).astype(F32).astype(BF16)


def one_hot(name, code):
    code = jnp.broadcast_to(code, name.shape[1:]).astype(BF16)
    return jnp.where(name == code[None], jnp.ones(name.shape, BF16), jnp.zeros(name.shape, BF16)).reshape(-1, name.shape[2])


def gathered_edges(planes):
    rows, lanes = planes[0].shape
    lane = lax.broadcasted_iota(jnp.int32, (rows, lanes), 1)
    row = lax.broadcasted_iota(jnp.int32, (rows, lanes), 0)
    total = jnp.zeros((rows, lanes), F32)
    for side, plane in enumerate(planes):
        for at in range(EDGE):
            place = (side * rows + row) * EDGE + at
            total = total + jnp.where(lane == place, plane[:, at : at + 1], 0.0)
    return jnp.sum(total, 0, keepdims=True)


class Window:
    def __init__(self, mask):
        self.mask = mask
        self.keep, self.divide = [], []
        for side in range(2):
            keep = [self.mask[k, side] for k in range(OFFSETS)]
            counts, total = [], 0.0
            for k in range(OFFSETS):
                total = total + keep[k]
                counts.append(1.0 / jnp.maximum(total, 1.0))
            self.keep.append(keep)
            self.divide.append(counts)

    def pooled(self, side, values):
        means, total = [], 0.0
        for k in range(OFFSETS):
            total = total + self.keep[side][k] * values[side + k]
            means.append(total * self.divide[side][k])
        return means

    def spread(self, sides):
        result = [0.0] * REACH
        for side in range(2):
            carried = 0.0
            for k in reversed(range(OFFSETS)):
                carried = carried + sides[side][k] * self.divide[side][k]
                result[side + k] = result[side + k] + self.keep[side][k] * carried
        return result


def window_of(planes, rows):
    segments = [plane[rows : 2 * rows] for plane in planes]
    valid = [plane[2 * rows :] for plane in planes]
    mask = {
        (k, j): (segments[j + k] == segments[j]).astype(F32) * valid[j + k]
        for k in range(OFFSETS)
        for j in range(REACH)
    }
    return [plane[:rows] for plane in planes], Window(mask)


CODES = 0
WEIGHTS = CODES + SPAN
MASKS = WEIGHTS + OFFSETS * REACH
PROBS = MASKS + OFFSETS * REACH
AVERAGE = PROBS + 2 * OFFSETS
PLANES = AVERAGE + 1


def lookup(row, codes):
    index = codes.astype(jnp.int32)
    lanes = 128
    low = jnp.bitwise_and(index, lanes - 1)
    parts = [
        jnp.take_along_axis(
            jnp.broadcast_to(row[:, at : at + lanes], codes.shape), low, axis=1
        )
        for at in range(0, row.shape[1], lanes)
    ]
    return jnp.where(index >= lanes, parts[1], parts[0])


def packed_row(ref, plane, row):
    return jnp.broadcast_to(ref[plane, pl.ds(row, 1), :], (16, ref.shape[2])).astype(BF16)


def spread_rows(plan, k, row, values):
    lanes = plan.shape[2]
    blocks = values // 16
    name = names(values, lanes)
    total = jnp.zeros((blocks, 16, lanes), BF16)
    for j in range(REACH):
        code = packed_row(plan, CODES + k + j, row)
        weight = packed_row(plan, WEIGHTS + k * REACH + j, row)
        total = jnp.where(name == code[None], total + weight[None], total)
    return total.reshape(values, lanes)


def accumulate(plan, total_ref, ks, cot, values, extra=None):
    rows, half = plan.shape[1:]
    for chunk in range(rows // 2):
        pieces = [
            jnp.concatenate(
                [
                    spread_rows(plan, k, 2 * chunk, values),
                    spread_rows(plan, k, 2 * chunk + 1, values),
                ],
                1,
            )
            for k in ks
        ]
        if extra is not None:
            pieces.append(extra(chunk))
        left = jnp.concatenate(pieces, 0)
        part = dot(left, cot[2 * chunk * half : 2 * (chunk + 1) * half, :])
        if chunk == 0:
            total_ref[...] = part
        else:
            total_ref[...] += part


def split(value):
    high = value.astype(BF16)
    return high, (value - high.astype(F32)).astype(BF16)


def thirds(value):
    high = value.astype(BF16)
    rest = value - high.astype(F32)
    middle = rest.astype(BF16)
    return high, middle, (rest - middle.astype(F32)).astype(BF16)


def far_kernel(order, slot, values, *refs):
    scorers = pieces_of(refs[:2], len(order))
    table_low, planes, scorer, cot = refs[2:6]
    sent_first, sent_second, plan, vectors, table, total = refs[6:]
    rows = plan.shape[1]
    every = jnp.concatenate([s[:8] for s in scorers], 0)
    parts = thirds(every)
    found = dot(jnp.concatenate(parts, 0), table_low[...], NT)
    count = every.shape[0]
    found = found[:count] + found[count : 2 * count] + found[2 * count :]
    for at, m in enumerate(order):
        table[group_index() ^ m] = found[at * 8 : (at + 1) * 8]
    half = planes.shape[1] // SPAN
    codes, window = window_of([planes[:, m * half : (m + 1) * half] for m in range(SPAN)], rows)
    bias = functools.reduce(jnp.add, [s[1:2] for s in scorers])
    both = [scorer[:8].astype(F32), jnp.broadcast_to(bias, (8, bias.shape[1]))]
    vectors[...] = jnp.concatenate(both, 0).astype(BF16)
    shared = jnp.sum(both[0] * both[1], 1, keepdims=True)[:1]
    conv_scores = [shared] * REACH
    for k in range(OFFSETS):
        row = table[k, :1, :]
        for m in range(k, k + REACH):
            conv_scores[m - k] = conv_scores[m - k] + window.mask[k, m - k] * lookup(row, codes[m])
    for m in range(SPAN):
        plan[CODES + m] = codes[m]
    shares = []
    for side in range(2):
        block = window.pooled(side, conv_scores)
        top = functools.reduce(jnp.maximum, block)
        exps = [jnp.exp(b - top) for b in block]
        inverse = 1.0 / functools.reduce(jnp.add, exps)
        shares.append([e * inverse for e in exps])
        for k in range(OFFSETS):
            plan[PROBS + side * OFFSETS + k] = shares[side][k]
    mixing = [0.5 * e for e in window.spread(shares)]
    plan[AVERAGE] = functools.reduce(jnp.add, mixing)
    for k in range(OFFSETS):
        for j in range(REACH):
            plan[MASKS + k * REACH + j] = window.mask[k, j]
            plan[WEIGHTS + k * REACH + j] = window.mask[k, j] * mixing[j]
    accumulate(plan, total, [group_index() ^ slot], cot, values)
    for at, sent in enumerate((sent_first, sent_second)):
        sent[...] = total[at * values // 2 : (at + 1) * values // 2].astype(BF16)


def block_kernel(slot, values, plan, cot, out):
    accumulate(plan, out, [group_index() ^ slot], cot, values)


def average_line(plan, chunk):
    return jnp.concatenate([plan[AVERAGE, row : row + 1, :] for row in (2 * chunk, 2 * chunk + 1)], 1)


def near_kernel(slots, values, plan, cot, own, sent, bias_out, total):
    half = plan.shape[2]

    def extra(chunk):
        line = jnp.broadcast_to(average_line(plan, chunk), (EXTRA, 2 * half))
        high, low = split(line)
        at = lax.broadcasted_iota(jnp.int32, line.shape, 0)
        return jnp.where(at == 0, high.astype(F32), jnp.where(at == 1, low.astype(F32), 0.0)).astype(BF16)

    accumulate(plan, total, [group_index() ^ m for m in slots], cot, values, extra)
    own[...] = total[:values]
    sent[...] = total[values : 2 * values].astype(BF16)
    end = total[len(slots) * values :]
    bias_out[...] = jnp.broadcast_to(end[:1] + end[1:2], (8, end.shape[1]))


def inner_kernel(order, values, products, plan, vectors, cot, *refs):
    before, out = (refs[0] if len(refs) > 1 else None), refs[-1]
    rows, half = plan.shape[1:]
    blocks = values // 16
    name = names(values, half)
    left = products[...]
    if before is None:
        left = jnp.concatenate([left, vectors[...]], 0)
    for chunk in range(rows // 2):
        here = cot[2 * chunk * half : 2 * (chunk + 1) * half, :]
        both = dot(left, here, NT)
        found = {}
        for place, m in enumerate(order):
            k = group_index() ^ m
            each = both[place * values : (place + 1) * values].astype(BF16)
            for side in range(2):
                row = 2 * chunk + side
                mine = each[:, side * half : (side + 1) * half].reshape(blocks, 16, half)
                for j in range(REACH):
                    code = packed_row(plan, CODES + k + j, row)
                    picked = jnp.zeros((16, half), BF16)
                    for at in range(blocks):
                        picked = jnp.where(name[at] == code, mine[at], picked)
                    mask = plan[MASKS + k * REACH + j, row : row + 1, :]
                    found[j, side] = found.get((j, side), 0.0) + picked.astype(F32) * mask
        for side in range(2):
            row = 2 * chunk + side
            for j in range(REACH):
                if before is None:
                    at = len(order) * values + 8
                    start = both[at : at + 1, side * half : (side + 1) * half]
                else:
                    start = before[j, row : row + 1, :]
                out[j, row : row + 1, :] = jnp.sum(found[j, side], 0, keepdims=True) + start


def score_kernel(values, inner_ref, plan, vectors, hot, out, flat):
    rows, half = plan.shape[1:]
    window = Window({(k, j): plan[MASKS + k * REACH + j] for k in range(OFFSETS) for j in range(REACH)})
    inner_rows = [0.5 * inner_ref[j] for j in range(REACH)]
    sides = []
    for side in range(2):
        inner = window.pooled(side, inner_rows)
        share = [plan[PROBS + side * OFFSETS + k] for k in range(OFFSETS)]
        mean = functools.reduce(jnp.add, [s * i for s, i in zip(share, inner)])
        sides.append([s * (i - mean) for s, i in zip(share, inner)])
    grads = window.spread(sides)
    overall = jnp.sum(jnp.sum(functools.reduce(jnp.add, grads), 1, keepdims=True), 0, keepdims=True)
    lane = lax.broadcasted_iota(jnp.int32, (rows, half), 1)
    flat[...] = jnp.zeros(flat.shape, F32)
    for k in range(OFFSETS):
        edges = []
        for side in range(2):
            inside = jnp.zeros((rows, half), F32)
            edge = jnp.zeros((rows, half), F32)
            for m in range(side, SPAN, 2):
                if not 0 <= m - k < REACH:
                    continue
                value = grads[m - k] * window.mask[k, m - k]
                steps = m // 2
                if steps:
                    inside = inside + jnp.where(lane < half - steps, pltpu.roll(value, half - steps, 1), 0.0)
                    moved = pltpu.roll(value, EDGE - steps, 1) if steps < EDGE else value
                    edge = edge + jnp.where((lane >= EDGE - steps) & (lane < EDGE), moved, 0.0)
                else:
                    inside = inside + value
            for row in range(rows):
                at = (side * rows + row) * half
                flat[k : k + 1, at : at + half] = inside[row : row + 1, :]
            edges.append(edge)
        flat[k : k + 1, 2 * rows * half :] = gathered_edges(edges)
    high, low = split(flat[...])
    both = jnp.concatenate([high.astype(F32), low.astype(F32)], 0).astype(BF16)
    edge = gathered_edges([plan[CODES + SPAN - 2 + side] for side in range(2)])
    lines = dot(both[:, : hot.shape[1]], hot[...], NT) + dot(both[:, hot.shape[1] :], one_hot(names(values, half), edge), NT)
    lines = lines[:8] + lines[8:]
    width = vectors.shape[1]
    out[...] = jnp.zeros(out.shape, F32)
    out[:1] = overall * vectors[:1].astype(F32)
    for k in range(OFFSETS + 1):
        row, lane = small_place(k, values, width)
        part = lines[k : k + 1] if k < OFFSETS else jnp.broadcast_to(overall, (1, values))
        out[row : row + 1, lane : lane + values] = part


def output_kernel(order, values, chunks_here, *refs):
    products = pieces_of(refs[:2], len(order))
    plan, vectors = refs[2:4]
    out, token, staged, sems = refs[-4:]
    token[...] = jnp.zeros(token.shape, F32)
    half = plan.shape[2]
    step = 2 * half
    biases = vectors[8:].astype(F32)
    at = lax.broadcasted_iota(jnp.int32, (8, step), 0)
    first = lax.broadcasted_iota(jnp.int32, biases.shape, 0)
    biases = jnp.where(first < 2, biases, 0.0)
    copies = []
    for place, chunk in enumerate(chunks_here):
        high, low = split(jnp.broadcast_to(average_line(plan, chunk), (8, step)))
        both = jnp.where(at == 0, high.astype(F32), jnp.where(at == 1, low.astype(F32), 0.0))
        total = dot(both, biases, TN)
        for slot, m in zip(products, order):
            k = group_index() ^ m
            left = jnp.concatenate([spread_rows(plan, k, row, values) for row in (2 * chunk, 2 * chunk + 1)], 1)
            total = total + dot(left, slot[...], TN)
        staged[place * step : (place + 1) * step, :] = total.astype(BF16)
        copies.append(
            pltpu.make_async_copy(
                staged.at[pl.ds(place * step, step), :], out.at[pl.ds(chunk * step, step), :], sems.at[place]
            )
        )
        copies[-1].start()
    for copy in copies:
        copy.wait()


def output_part(before, part, parts, order, values, products, plan, vectors, after):
    rows, half = plan.shape[1:]
    width = vectors.shape[1]
    each = rows // 2 // parts
    operands = [pltpu.with_memory_space_constraint(x, pltpu.VMEM) for x in (*products, plan, vectors)]
    operands += [] if before is None else [pltpu.with_memory_space_constraint(before, pltpu.HBM)]
    vmem = pl.BlockSpec(memory_space=pltpu.VMEM)
    elsewhere = pl.BlockSpec(memory_space=pl.ANY)
    count = len(products) + 2
    chunks_here = range(part * each, (part + 1) * each)

    def run(*refs):
        output_kernel(order, values, chunks_here, *refs[:count], *refs[-4:])

    return pl.pallas_call(
        run,
        out_shape=[jax.ShapeDtypeStruct((rows * half, width), BF16), pltpu.VMEM((8, 128), F32)],
        in_specs=[vmem] * count + [elsewhere] * (len(operands) - count + len(after)),
        out_specs=[elsewhere, vmem],
        input_output_aliases={} if before is None else {count: 0},
        scratch_shapes=[pltpu.VMEM((2 * half * each, width), BF16), pltpu.SemaphoreType.DMA((each,))],
        compiler_params=pltpu.CompilerParams(vmem_limit_bytes=VMEM_LIMIT),
        cost_estimate=pl.CostEstimate(flops=0, bytes_accessed=0, transcendentals=0),
        name="output",
    )(*operands, *after)


def chunks(values, piece, group):
    block = values // OFFSETS
    size = block // PIECES
    for actual in range(PIECES):
        for offset in range(OFFSETS):
            at = pl.multiple_of((piece ^ actual) * OFFSETS * size + (group ^ offset) * size, size)
            yield offset * block + actual * size, at, size


def pack(rows):
    high, low = split(rows)
    return jnp.concatenate([high.astype(F32), low.astype(F32)], 0).astype(BF16)


def small_place(at, values, width):
    per = width // values
    return 1 + at // per, at % per * values


def small_pack(rows):
    high, low = split(rows)
    return jnp.concatenate([high.astype(F32), low.astype(F32)], 0).astype(BF16)


def small_unpack(block):
    return block[: SMALL // 2].astype(F32) + block[SMALL // 2 :].astype(F32)


def small_sums(sums, bias):
    first = lax.broadcasted_iota(jnp.int32, sums.shape, 0) == 0
    return small_pack(sums[...] + jnp.where(first, bias[: sums.shape[0]], 0.0))


def sent_kernel(slots, near, far, sums, bias, *sends):
    size = near.shape[0] // PIECES
    for at, (slot, send) in enumerate(zip(slots, sends)):
        total = near[slot * size : (slot + 1) * size] + far[at * size : (at + 1) * size].astype(F32)
        send[:size] = total.astype(BF16)
        send[size:] = small_sums(sums, bias)


def rest_kernel(near, far, sums, bias, keep, send):
    size = keep.shape[0]
    keep[...] = near[:size] + far[:size].astype(F32)
    send[:size] = (near[2 * size : 3 * size] + far[size:].astype(F32)).astype(BF16)
    send[size:] = small_sums(sums, bias)


def slice_kernel(keep, own, *refs):
    others, send = refs[:-1], refs[-1]
    part = keep.shape[0]
    total = functools.reduce(jnp.add, [keep[...]] + [o[:part].astype(F32) for o in others])
    small = [small_unpack(x[part:]) for x in (own, *others)]
    while len(small) > 1:
        small = [small[at] + small[at + 1] for at in range(0, len(small), 2)]
    send[:part] = total.astype(BF16)
    send[part:] = small_pack(small[0])


def whole_kernel(mine, other, send):
    rows = mine.shape[0] - SMALL
    send[:rows] = (mine[:rows].astype(F32) + other[:rows].astype(F32)).astype(BF16)
    send[rows:] = small_pack(small_unpack(mine[rows:]) + small_unpack(other[rows:]))


def last_kernel(mine, other, block, sums):
    rows = block.shape[0]
    block[...] = (mine[:rows].astype(F32) + other[:rows].astype(F32)).astype(BF16)
    sums[...] = small_unpack(mine[rows:]) + small_unpack(other[rows:])


def turned_kernel(value, out):
    out[...] = value[...].T


def share_kernel(block, sums, weight_turned, keep, send):
    product = dot(block[...], weight_turned[...])
    rows = keep.shape[0]
    keep[...] = product[:rows]
    send[:rows] = product[rows:].astype(BF16)
    send[rows:] = small_pack(sums[...])


def half_kernel(keep, sums, other, rest, send, total):
    rows = rest.shape[0]
    both = keep[...] + other[: 2 * rows].astype(F32)
    total[...] = sums[...] + small_unpack(other[2 * rows :])
    rest[...] = both[:rows]
    send[:rows] = both[rows:].astype(BF16)
    send[rows:] = small_pack(total[...])


def combine_kernel(keep, sums, other, out, total):
    rows = keep.shape[0]
    out[...] = (keep[...] + other[:rows].astype(F32)).astype(BF16)
    total[...] = sums[...] + small_unpack(other[rows:])


def added_kernel(mine, other, out):
    out[...] = (mine[...].astype(F32) + other[...].astype(F32)).astype(out.dtype)


def arrange(source, target, group):
    values = source.shape[0]
    for at, place, size in chunks(values, piece_index(), group):
        target[pl.ds(place, size), :] = source[at : at + size]


def far_sum_kernel(mine, one, two, first, second, total):
    rows = one.shape[0]
    halves = [mine[:rows] + one[...].astype(F32), mine[rows:] + two[...].astype(F32)]
    arrange(jnp.concatenate(halves, 0), total, group_index() ^ 2)
    size = total.shape[0] // PIECES
    for out, slots in ((first, (1, 3)), (second, (0, 2))):
        for at, slot in enumerate(slots):
            out[at * size : (at + 1) * size] = total[slot * size : (slot + 1) * size].astype(BF16)


def near_sum_kernel(near, other, total):
    arrange(near[...] + other[...].astype(F32), total, group_index())


def weight_kernel(order, offsets, *refs):
    slots = refs[: len(order)]
    turned, vectors, sums = refs[len(order) : len(order) + 3]
    scorers = pieces_of(refs[len(order) + 3 : len(order) + 5], len(offsets))
    products = pieces_of(refs[len(order) + 5 : len(order) + 7], len(offsets))
    out, score_out, bias_out, ranks, full, staged, rows_ref, lines, ends, sems = refs[len(order) + 7 :]
    values, width = full.shape
    group, piece = group_index(), piece_index()
    block = values // OFFSETS
    size = block // PIECES
    copies = []

    def send(source, target):
        copies.append(pltpu.make_async_copy(source, target, sems.at[len(copies)]))
        copies[-1].start()

    for m, slot in zip(order, slots):
        for offset in range(OFFSETS):
            at = (group ^ offset) * block + (piece ^ m) * size
            full[pl.ds(pl.multiple_of(at, size), size), :] = slot[offset * size : (offset + 1) * size]
    for k in range(OFFSETS):
        row, lane = small_place(k, values, width)
        lines[k : k + 1] = sums[row : row + 1, lane : lane + values]
    line = lines[pl.ds(group, 1), :]
    scores = vectors[:1].astype(F32)
    first = lax.broadcasted_iota(jnp.int32, (8, values), 0) == 0
    both = pack(jnp.where(first, jnp.broadcast_to(line, first.shape), 0.0))
    parts, step = staged.shape[:2]
    for part in range(parts):
        here = turned[part * step : (part + 1) * step]
        through = dot(here, both, NT)
        staged[part] = dot(here, full[...]) + (through[:, :1] + through[:, 8:9]) * scores
        send(staged.at[part], out.at[pl.ds(part * step, step), :])
    shard = score_out.shape[1]
    source = lax.broadcasted_iota(jnp.int32, (width, shard), 0)
    column = lax.broadcasted_iota(jnp.int32, (width, shard), 1) + row_index() * shard
    here = (source == column).astype(BF16)
    row, lane = small_place(OFFSETS, values, width)
    score_grad = sums[row : row + 1, lane : lane + 1] * vectors[8:9].astype(F32)
    for product, m in zip(products, offsets):
        got = dot(pack(jnp.broadcast_to(lines[pl.ds(group ^ m, 1), :], (8, values))), product[...])
        score_grad = score_grad + got[:1] + got[8:9]
    at = lax.broadcasted_iota(jnp.int32, (8, width), 0)
    small = jnp.where(at == 0, score_grad, jnp.where(at == 1, sums[:1], 0.0))
    ends[...] = functools.reduce(jnp.add, [dot(part, here) for part in thirds(small)])
    send(ends.at[pl.ds(0, 1), :], score_out)
    send(ends.at[pl.ds(1, 1), :], bias_out)
    for scorer, m in zip(scorers, offsets):
        rows_ref[group ^ m] = scorer[...]
    high, low = split(lines[:OFFSETS])
    right_high, right_low = split(jnp.concatenate([rows_ref[k, :1] for k in range(OFFSETS)], 0))
    left = jnp.concatenate([x.astype(F32) for x in (high, low, high, low)], 0).astype(BF16)
    right = jnp.concatenate([x.astype(F32) for x in (right_high, right_high, right_low, right_low)], 0).astype(BF16)
    ranks[...] = dot(left, right, TN)
    for copy in copies:
        copy.wait()


def table_grad_kernel(order, *refs):
    slots, (ranks, out, table) = refs[: len(order)], refs[len(order) :]
    group, block = group_index(), table.shape[0]
    for slot, m in zip(slots, order):
        size = slot.shape[0]
        at = pl.multiple_of((piece_index() ^ m) * size, size)
        table[pl.ds(at, size), :] = slot[...].astype(F32) + ranks[pl.ds(pl.multiple_of(group * block, block) + at, size), :]
    rows = out.shape[0]
    inside = row_index() * rows - group * block
    out[...] = table[pl.ds(pl.multiple_of(inside, rows), rows), :]


def bits_of(count):
    return [1 << at for at in reversed(range(count.bit_length() - 1))]


def body(byte_values, segment_ids, valid, table, conv_weight, conv_bias, score_weight, cotangent):
    rows_count, tract_count = lax.axis_size("rows"), lax.axis_size("tract")
    rows_at = lax.axis_index("rows")
    values, width = table.shape[0] * rows_count, table.shape[1]
    rows, length = byte_values.shape
    half = length // 2
    copies = rows_count // OFFSETS
    order = [0, 2, 1, 3]
    group_bits = [2 * copies, copies]
    near_bits = [bit for bit in bits_of(rows_count) if bit < copies]

    row_bits = bits_of(rows_count)
    far_score = swap(score_weight[None], "rows", row_bits[0])
    near_order = slots_of(near_bits)
    biases = [conv_bias[None]]
    for bit in near_bits:
        biases = biases + [swap(value, "rows", bit) for value in biases]
    weight = conv_weight
    if copies > 1:
        near_by = [[g * copies + c for c in range(copies)] for g in range(OFFSETS)]
        weight = lax.all_gather(conv_weight, "rows", axis=0, tiled=True, axis_index_groups=near_by)
    shard = (1, conv_bias.shape[0])
    table_low, score, biases[0], ids = call(
        functools.partial(load_kernel, rows),
        [(table.shape, BF16), (shard, F32), (shard, F32), ((3 * rows, length), F32)],
        (table,), (score_weight[None],), (conv_bias[None],), (byte_values,), (segment_ids,), (valid,),
        scratch=[pltpu.VMEM(table.shape, F32), pltpu.VMEM((3, rows, length), jnp.int32), pltpu.SemaphoreType.DMA((6,))],
        name="load",
    )
    parts = 4
    weight_low = call(
        weight_low_kernel, [(weight.shape, BF16)], (weight,),
        scratch=[pltpu.VMEM((parts, weight.shape[0] // parts, width), F32), pltpu.SemaphoreType.DMA((parts,))],
        name="weight_low", after=[table_low], cost=LONG,
    )[0]
    scores = gathered(stacked(score, far_score, name="score"), "rows", row_bits[1:], "score")
    scorer, scored = call(
        functools.partial(scorer_kernel, slots_of(row_bits), near_order),
        [((EXTRA, width), BF16), ((SENT, width), F32)], *scores, *biases, weight_low, name="scorer",
    )
    far_scored = swap(scored, "rows", group_bits[0])
    far_table = swap(table_low, "rows", row_bits[0])
    table_low = stacked(table_low, far_table, name="table_pair", after=[scored])
    table_low = call(
        functools.partial(table_kernel, slots_of(row_bits)), [((values, width), BF16)],
        *gathered(table_low, "rows", row_bits[1:], "table_pair"), name="table",
    )[0]
    product, turned = call(
        products_kernel, [((values, width), BF16), ((width, values), BF16)], table_low, weight_low, name="products", after=[],
    )
    tail = stacked(ids, name="tail", after=[product])
    before = lax.ppermute(tail, "tract", [(i, i + 1) for i in range(tract_count - 1)])
    planes, hot = call(
        planes_kernel, [((3 * rows, SPAN * half), F32), ((values, 2 * rows * half), BF16)], ids, name="planes", after=[product],
    )
    planes = call(halo_kernel, [(planes.shape, F32)], planes, before, name="halo")[0]
    scorers = call(pair_kernel, [((16, width), F32)], scored, far_scored, name="scored")[0]
    scorers = scorers, swap(scorers, "rows", group_bits[1])

    cot = cotangent.reshape(rows * half, width)
    *far_sent, plan, vectors = call(
        functools.partial(far_kernel, order, 3, values),
        [((values // 2, width), BF16), ((values // 2, width), BF16), ((PLANES, rows, half), F32), ((EXTRA, width), BF16)],
        *scorers, table_low, planes, scorer, cot,
        scratch=[pltpu.VMEM((OFFSETS, 8, values), F32), pltpu.VMEM((values, width), F32)], name="far",
    )
    far = call(functools.partial(block_kernel, 2, values), [((values, width), F32)], plan, cot, name="far_own")[0]
    far_sent = [swap(half_sent, "rows", copies) for half_sent in far_sent]
    far = call(
        far_sum_kernel, [((values // 2, width), BF16)] * 2, far, *far_sent,
        scratch=[pltpu.VMEM((values, width), F32)], name="far_sum",
    )
    far_others = [swap(part, "rows", 2 * copies) for part in far]
    far_product = swap(product, "rows", 2 * copies)
    near, near_sent, bias_part = call(
        functools.partial(near_kernel, [0, 1], values),
        [((values, width), F32), ((values, width), BF16), ((8, width), F32)], plan, cot,
        scratch=[pltpu.VMEM((2 * values + EXTRA, width), F32)], name="near", after=[far_product, far[1]],
    )
    near_other = swap(near_sent, "rows", copies)

    product = stacked(product, far_product, name="passed")
    products = product, swap(product, "rows", copies)
    inner = call(
        functools.partial(inner_kernel, [0, 2], values), [((REACH, rows, half), F32)],
        products[0], plan, vectors, cot, name="inner_near", cost=LONG,
    )[0]
    inner = call(
        functools.partial(inner_kernel, [1, 3], values), [((REACH, rows, half), F32)],
        products[1], plan, vectors, cot, inner, name="inner_far",
    )[0]
    sums = call(
        functools.partial(score_kernel, values), [((SMALL // 2, width), F32)], inner, plan, vectors, hot,
        scratch=[pltpu.VMEM((8, hot.shape[1] + half), F32)], name="scores",
    )[0]

    rest = [("tract", 1 << at) for at in range(PIECES.bit_length() - 1, tract_count.bit_length() - 1)]
    rest += [("rows", 1 << at) for at in range(copies.bit_length() - 1)]
    size = values // PIECES
    near = call(near_sum_kernel, [((values, width), F32)], near, near_other, name="near_sum")[0]
    sent = ((size + SMALL, width), BF16)
    send_one, send_three = call(
        functools.partial(sent_kernel, (1, 3)), [sent, sent], near, far_others[0], sums, bias_part, name="merge",
    )
    keep, send_two = call(rest_kernel, [((size, width), F32), sent], near, far_others[1], sums, bias_part, name="rest")
    sends = [send_one, send_two, send_three]
    others = [swap(send, "tract", at + 1) for at, send in enumerate(sends)]
    parts = 2

    def fill(out, which, after):
        for part in which:
            out, token = output_part(out, part, parts, order, values, products, plan, vectors, [after])
        return out, token

    out, token = fill(None, [0], keep)
    send = call(slice_kernel, [((size + SMALL, width), BF16)], keep, sends[2], *others, name="slice", after=[token])[0]
    out, token = fill(out, [1], send)
    weight_turned = call(turned_kernel, [(weight_low.shape, BF16)], weight_low, name="turned", after=[token])[0]
    for axis, bit in rest[:-1]:
        other = swap(send, axis, bit)
        send = call(whole_kernel, [(send.shape, BF16)], send, other, name="whole")[0]
    other = swap(send, *rest[-1])
    block, sums = call(last_kernel, [((size, width), BF16), ((SMALL // 2, width), F32)], send, other, name="last", after=[token])

    part = size // OFFSETS
    keep, send = call(
        share_kernel, [((2 * part, width), F32), ((2 * part + SMALL, width), BF16)], block, sums, weight_turned, name="share",
    )
    other = swap(send, "rows", group_bits[0])
    blocks = {0: block} | {m: swap(block, "tract", m) for m in range(1, PIECES)}
    keep, send, sums = call(
        half_kernel, [((part, width), F32), ((part + SMALL, width), BF16), ((SMALL // 2, width), F32)], keep, sums, other, name="half",
    )
    other = swap(send, "rows", group_bits[1])
    table_piece, sums = call(combine_kernel, [((part, width), BF16), ((SMALL // 2, width), F32)], keep, sums, other, name="combine")
    table_pieces = {0: table_piece} | {m: swap(table_piece, "tract", m) for m in range(1, PIECES)}
    if copies > 1:
        turned = lax.dynamic_slice_in_dim(turned, rows_at % copies * (width // copies), width // copies, 0)
    weight_rows = conv_weight.shape[0]
    steps = 3
    weight_grad, score_grad, bias_grad, ranks = call(
        functools.partial(weight_kernel, list(blocks), order),
        [((weight_rows, width), F32), (shard, F32), (shard, F32), ((values, width), F32)],
        *blocks.values(), turned, vectors, sums, *scorers, *products,
        scratch=[pltpu.VMEM((values, width), BF16), pltpu.VMEM((steps, weight_rows // steps, width), F32),
                 pltpu.VMEM((OFFSETS, 8, width), F32), pltpu.VMEM((8, values), F32), pltpu.VMEM((8, shard[1]), F32),
                 pltpu.SemaphoreType.DMA((steps + 2,))],
        name="weights", final=3, copied=True,
    )
    table_grad = call(
        functools.partial(table_grad_kernel, list(table_pieces)), [(table.shape, F32)], *table_pieces.values(), ranks,
        scratch=[pltpu.VMEM((values // OFFSETS, width), F32)], name="table_grad", final=1,
    )[0]
    return out.reshape(cotangent.shape), table_grad, weight_grad, bias_grad[0], score_grad[0]


def solution(mesh):
    return jax.shard_map(
        body,
        mesh=mesh,
        in_specs=(
            P("rows", "tract"), P("rows", "tract"), P("rows", "tract"), P("rows", None),
            P("rows", None), P("rows"), P("rows"), P("rows", "tract", None),
        ),
        out_specs=(P("rows", "tract", None), P("rows", None), P("rows", None), P("rows"), P("rows")),
        check_vma=False,
    )
```
